32 devices in a mesh: dp: 4 (over y, x), fsdp: 8 (over z, core).
Axes of the slice: x: 2, y: 2, z: 4, core: 2. Of those that a mesh axis runs over, the one named last changes fastest.
Arguments:
- layer_input: bfloat16 [8192, 1280], P(('dp', 'fsdp')), may hold values from -6 to 6
- w_qkv: bfloat16 [1280, 3840], P(('dp', 'fsdp')), may hold values from -0.15625 to 0.15625
- w_out: bfloat16 [1280, 1280], P(('dp', 'fsdp')), may hold values from -4 to 4
- w_shared: bfloat16 [1280, 2688], P(('dp', 'fsdp')), may hold values from -0.15625 to 0.15625
- w_experts: bfloat16 [16, 1280, 2688], P(None, ('dp', 'fsdp')), may hold values from -0.15625 to 0.15625
- gains: bfloat16 [1280, 2], P(('dp', 'fsdp')), may hold values from 0.099609375 to 1.8984375
- routes: int32 [8192, 7], P(('dp', 'fsdp')), may hold values from 0 to 15, all different within a row; in each aligned block of 256 rows (0 to 255, 256 to 511, ...) at most 128 rows name the same one
- gates: float32 [8192, 7], P(('dp', 'fsdp')), may hold values from 0.2 to 0.6
- d_out: bfloat16 [8192, 1280], P(('dp', 'fsdp')), may hold values from -6 to 6
Outputs:
- layer_output: bfloat16 [8192, 1280], P(('dp', 'fsdp'))
- d_x: float32 [8192, 1280], P(('dp', 'fsdp'))
- g_qkv: float32 [1280, 3840], P(('dp', 'fsdp'))
- g_out: float32 [1280, 1280], P(('dp', 'fsdp'))
- g_shared: float32 [1280, 2688], P(('dp', 'fsdp'))
- g_experts: float32 [16, 1280, 2688], P(None, ('dp', 'fsdp'))
- g_gains: float32 [1280, 2], P(('dp', 'fsdp'))
The draws below stay inside these ranges and needn't reach their ends.
Inputs may be any that keep to these rules, and one draw needn't show every extreme that they name: `routes`: each token names 7 different experts; among the 256 tokens of one device no expert is named more than 128 times, and in every draw some expert is named exactly 128 times by the tokens of some device.
All inputs are finite; a program needn't handle non-finite values.
Results may differ from the reference program's by a relative error of at most 0.015.
Values may be sent and summed in bfloat16 or wider, within the bound.
A program may use at most 384 MiB of HBM per device.

```python
import math
import jax
import jax.numpy as jnp
import numpy as np
from jax import lax

D = 1280
HEADS = 10
HD = 128
H = 896
TOPK = 7
EXPERTS = 16
TOK_DEV = 256
CAP = 128
SEQLEN = 2048
SEQS = 4
TOKENS = 8192


def levels(own_key, dims, shards, least, largest):
    def one(axis_at, blocks):
        heights = jax.random.uniform(jax.random.fold_in(jax.random.fold_in(own_key, 6), axis_at), (blocks,), jnp.float32, least / len(shards), largest / len(shards))
        return jnp.repeat(jnp.exp(heights), dims[axis_at] // blocks).reshape((-1,) + (1,) * (len(dims) - axis_at - 1))

    loudness = one(*shards[0])
    for cut in shards[1:]:
        loudness = loudness * one(*cut)
    return loudness


def shared_out(key, own, number, rows, number_of, top, limit, skew):
    order = jax.random.permutation(key, number_of)
    heavy_load, ordinary = portions_of(number_of, rows * top, limit, skew, True), portions_of(number_of, rows * top, limit, skew, False)
    places = jnp.arange(number_of)

    def named(sizes, turn):
        used = int((sizes > 0).sum())
        fixed = max(1, used // 4)
        passed = fixed + (places - fixed + turn * (used - fixed)) % max(1, number_of - fixed)
        return jnp.zeros((number_of,), jnp.int32).at[order[jnp.where(places < fixed, places, passed)]].set(jnp.asarray(sizes, jnp.int32))

    sizes = jnp.where(number % 4 == 0, named(heavy_load, number // 4), named(ordinary, number - number // 4 - 1))
    mixed = jax.random.permutation(jax.random.fold_in(own, 3), number_of)
    donor, receiver = mixed[0:number_of // 2 * 2:2], mixed[1:number_of // 2 * 2:2]
    slack = jnp.minimum(sizes[donor] - 1, limit - sizes[receiver]) // 2
    slack = jnp.where((donor == order[0]) | (receiver == order[0]) | (sizes[receiver] == 0), 0, jnp.maximum(slack, 0))
    passed = jax.random.randint(jax.random.fold_in(own, 4), (number_of // 2,), 0, 1 << 20) % (slack + 1)
    sizes = sizes.at[donor].add(-passed).at[receiver].add(passed)
    labels = jnp.searchsorted(jnp.cumsum(sizes), jnp.arange(rows * top), side="right").astype(jnp.int32)
    table = labels.reshape(top, rows).T
    table = table[jax.random.permutation(jax.random.fold_in(own, 1), rows)]
    turn = jax.random.randint(jax.random.fold_in(own, 2), (rows, 1), 0, top)
    return jnp.take_along_axis(table, (jnp.arange(top)[None, :] + turn) % top, axis=1)


def portions_of(number_of, total, most, skew, full):
    weights = [(1 << 20) // math.isqrt(grade ** skew) + 1 for grade in range(1, number_of + 1)]
    largest = most if full else min(most, max(-(-total // number_of), total * weights[0] // sum(weights)))
    least = 1 if total - largest >= number_of - 1 else 0
    holding, rest = [largest] + [least] * (number_of - 1), total - largest - least * (number_of - 1)
    while rest > 0:
        movable = [i for i in range(1, number_of) if holding[i] < largest] or [i for i in range(1, number_of) if holding[i] < most]
        pool, left = sum([weights[i] for i in movable]), rest
        for i in movable:
            extra = min(most - holding[i], max(1, left * weights[i] // pool), rest)
            holding[i] = holding[i] + extra
            rest = rest - extra
    return np.array(holding)


def centred(own_key, extent, spread, limit, shards=(), kind=jnp.bfloat16):
    level = levels(own_key, extent, shards, -0.22, 0.18) if shards else 1.0
    values = jax.random.normal(own_key, extent, jnp.float32) * spread * level
    return jnp.minimum(jnp.maximum(values, -limit), limit).astype(kind)


def setup_inputs(seed: int = 0) -> dict:
    arg_keys = jax.random.split(jax.random.key(seed), 10)
    layer_input = centred(arg_keys[0], (TOKENS, D), 1.0, 6.0, ((0, 32),))
    w_qkv = centred(arg_keys[1], (D, 3 * D), D ** -0.5, 0.15625, ((0, 32),))
    w_out = centred(arg_keys[2], (D, D), (max(1, 4 * D // SEQLEN)) ** -0.5, 4.0, ((0, 32),))
    w_shared = centred(arg_keys[3], (D, 3 * H), D ** -0.5, 0.15625, ((0, 32),))
    w_experts = centred(arg_keys[4], (EXPERTS, D, 3 * H), D ** -0.5, 0.15625, ((1, 32),))
    gains = jnp.clip(1.0 + 0.18 * jax.random.normal(arg_keys[5], (D, 2), jnp.float32), 0.099609375, 1.8984375).astype(jnp.bfloat16)
    routes_keys = jax.random.split(jax.random.fold_in(arg_keys[6], 1), TOKENS // TOK_DEV)
    routes_turns = jax.random.permutation(jax.random.fold_in(arg_keys[6], 3), TOKENS // TOK_DEV)
    routes = jax.vmap(lambda own, number: shared_out(jax.random.fold_in(arg_keys[6], 2), own, number, TOK_DEV, EXPERTS, TOPK, CAP, 1))(routes_keys, routes_turns).reshape((TOKENS, TOPK))
    gates = jnp.clip(0.2 + 0.400000021 * jax.random.uniform(arg_keys[7], (TOKENS, TOPK), jnp.float32) ** levels(arg_keys[7], (TOKENS, TOPK), ((0, 32),), -0.2, 0.2), 0.2, 0.6)
    d_out = centred(arg_keys[8], (TOKENS, D), 1.0, 6.0, ((0, 32),))
    return dict(layer_input=layer_input, w_qkv=w_qkv, w_out=w_out, w_shared=w_shared, w_experts=w_experts, gains=gains, routes=routes, gates=gates, d_out=d_out)


norm_eps = 1e-06
masked_score = -1000000000.0

@jax.custom_vjp
def low(v):
    return lax.optimization_barrier(v.astype(jnp.bfloat16)).astype(jnp.float32)

@jax.custom_vjp
def low_back(v):
    return v

def low_keep(v):
    return (low(v), None)

def low_pass(kept, grad):
    return (grad,)

def back_keep(v):
    return (v, None)

def back_low(kept, grad):
    return (low(grad),)
low.defvjp(low_keep, low_pass)
low_back.defvjp(back_keep, back_low)

def rotary_tables(positions):
    half_dim = HD // 2
    frequency = 10000.0 ** (-jnp.arange(half_dim, dtype=jnp.float32) / half_dim)
    angles = positions.astype(jnp.float32)[:, None] * frequency[None, :]
    cosine = jnp.concatenate([jnp.cos(angles), jnp.cos(angles)], axis=1)
    sine_table = jnp.concatenate([jnp.sin(angles), jnp.sin(angles)], axis=1)
    return (cosine[:, None, :], sine_table[:, None, :])

def rotary(values, positions):
    cosine, sine_table = rotary_tables(positions)
    half_dim = HD // 2
    shaped = values.reshape(values.shape[0], -1, HD)
    turned = jnp.concatenate([-shaped[..., half_dim:], shaped[..., :half_dim]], axis=2)
    return (shaped * cosine + turned * sine_table).reshape(values.shape)

def rms_norm(values, gain):
    return values * lax.rsqrt(lax.optimization_barrier(jnp.mean(values * values, axis=-1, keepdims=True)) + norm_eps) * gain

def feed_forward(weights, inputs):
    highest = lax.Precision.HIGHEST
    gate_pre = low_back(jnp.dot(inputs, weights[:, :H], precision=highest))
    up_pre = low_back(jnp.dot(inputs, weights[:, H:2 * H], precision=highest))
    hidden_act = low(jax.nn.silu(gate_pre) * up_pre)
    return low_back(jnp.dot(hidden_act, weights[:, 2 * H:].T, precision=highest))

def layer_forward(seq_input, w_qkv, w_out, w_shared, w_experts, gains, seq_routes, seq_gates):
    highest = lax.Precision.HIGHEST
    positions = jnp.arange(SEQLEN, dtype=jnp.int32)
    normed_one = low(rms_norm(seq_input, gains[:, 0]))
    projected = low_back(jnp.dot(normed_one, w_qkv, precision=highest))
    queries = low(rotary(projected[:, :D], positions)).reshape(SEQLEN, HEADS, HD)
    keys_all = low(rotary(projected[:, D:2 * D], positions)).reshape(SEQLEN, HEADS, HD)
    values_all = low(projected[:, 2 * D:]).reshape(SEQLEN, HEADS, HD)
    block_rows = min(512, SEQLEN)
    block_count = SEQLEN // block_rows
    head_scale = 1.0 / math.sqrt(HD)

    def attend(operands):
        query_block, first_row = operands
        scores = low_back(jnp.einsum('qhd,khd->hqk', query_block, keys_all, precision=highest) * head_scale)
        row_positions = first_row + jnp.arange(block_rows, dtype=jnp.int32)
        allowed = positions[None, :] <= row_positions[:, None]
        scores = jnp.where(allowed[None, :, :], scores, masked_score)
        shifted = jnp.exp(scores - lax.optimization_barrier(jnp.max(scores, axis=-1, keepdims=True)))
        weights_soft = low(shifted / lax.optimization_barrier(jnp.sum(shifted, axis=-1, keepdims=True)))
        return jnp.einsum('hqk,khd->qhd', weights_soft, values_all, precision=highest)
    starts = (jnp.arange(block_count, dtype=jnp.int32) * block_rows).astype(jnp.int32)
    mixed_blocks = lax.map(jax.checkpoint(attend), (queries.reshape(block_count, block_rows, HEADS, HD), starts))
    mixed = low(low_back(mixed_blocks.reshape(SEQLEN, D)))
    middle = seq_input + low_back(jnp.dot(mixed, w_out.T, precision=highest))
    normed_two = low(rms_norm(middle, gains[:, 1]))
    chosen = seq_routes[:, :, None] == jnp.arange(EXPERTS, dtype=jnp.int32)[None, None, :]
    gate_table = lax.optimization_barrier(jnp.sum(jnp.where(chosen, seq_gates[:, :, None], 0.0), axis=1))

    def add_expert(running, operands):
        weights, gate_column = operands
        return (running + gate_column[:, None] * feed_forward(weights, normed_two), None)
    routed, unused = lax.scan(jax.checkpoint(add_expert), jnp.zeros_like(seq_input), (w_experts, gate_table.T))
    return middle + feed_forward(w_shared, normed_two) + routed

def reference(layer_input, w_qkv, w_out, w_shared, w_experts, gains, routes, gates, d_out):
    params = (w_qkv.astype(jnp.float32), w_out.astype(jnp.float32), w_shared.astype(jnp.float32), w_experts.astype(jnp.float32), gains.astype(jnp.float32))
    inputs_all = layer_input.astype(jnp.float32).reshape(SEQS, SEQLEN, D)
    upstream_all = d_out.astype(jnp.float32).reshape(SEQS, SEQLEN, D)
    routes_all = routes.reshape(SEQS, SEQLEN, TOPK)
    gates_all = gates.reshape(SEQS, SEQLEN, TOPK)

    def one_sequence(running, operands):
        seq_input, seq_routes, seq_gates, seq_upstream = operands

        def forward_only(inputs, wq, wo, wsh, wex, gn):
            return layer_forward(inputs, wq, wo, wsh, wex, gn, seq_routes, seq_gates)
        result, pullback = jax.vjp(forward_only, seq_input, params[0], params[1], params[2], params[3], params[4])
        gradient = pullback(seq_upstream)
        running = tuple((total_now + part for total_now, part in zip(running, gradient[1:])))
        return (running, (result.astype(jnp.bfloat16), gradient[0]))
    initial = tuple((jnp.zeros_like(param) for param in params))
    summed, (outputs, input_grads) = lax.scan(one_sequence, initial, (inputs_all, routes_all, gates_all, upstream_all))
    return (outputs.reshape(TOKENS, D), input_grads.reshape(TOKENS, D), summed[0], summed[1], summed[2], summed[3], summed[4])
```

```python
import functools
import math

import jax
import jax.numpy as jnp
from jax import lax
from jax.experimental import pallas as pl
from jax.experimental.pallas import tpu as pltpu
from jax.sharding import PartitionSpec as P

HEADS = 10
HD = 128
norm_eps = 1e-06
masked_score = -1000000000.0
BF = jnp.bfloat16
F32 = jnp.float32
VMEM_LIMIT = 60 * 2**20


def dot_nn(a, b):
    return lax.dot_general(a, b, (((1,), (0,)), ((), ())), preferred_element_type=F32)


def dot_nt(a, b):
    return lax.dot_general(a, b, (((1,), (1,)), ((), ())), preferred_element_type=F32)


def dot_tn(a, b):
    return lax.dot_general(a, b, (((0,), (0,)), ((), ())), preferred_element_type=F32)


def after(value, *marks):
    return lax.optimization_barrier((value,) + marks)[0]


def put(buffer, value, *index):
    rest = buffer.ndim - len(index)
    starts = tuple(index) + (0,) * rest
    return lax.dynamic_update_slice(
        buffer, value.reshape((1,) * len(index) + buffer.shape[len(index) :]), starts
    )


def take(values, index):
    return lax.dynamic_index_in_dim(values, index, 0, keepdims=False)


def proj_kernel(x_ref, gain_ref, w_ref, cos_ref, sin_ref, xn_ref, q_ref, k_ref, v_ref, kt_ref, vt_ref):
    x = x_ref[...].astype(F32)
    inv = lax.rsqrt(jnp.mean(x * x, axis=1, keepdims=True) + norm_eps)
    xn = (x * inv * gain_ref[...]).astype(BF)
    xn_ref[...] = xn
    width = q_ref.shape[1]
    cos = cos_ref[...]
    sin = sin_ref[...]
    for part in range(3):
        for head in range(width // HD):
            lo = part * width + head * HD
            u = dot_nn(xn, w_ref[:, lo : lo + HD])
            cols = slice(head * HD, (head + 1) * HD)
            if part < 2:
                u = u * cos + pltpu.roll(u, HD // 2, 1) * sin
            low = u.astype(BF)
            if part == 0:
                q_ref[:, cols] = low
            elif part == 1:
                k_ref[:, cols] = low
                kt_ref[cols, :] = u.T.astype(BF)
            else:
                v_ref[:, cols] = low
                vt_ref[cols, :] = u.T.astype(BF)


def project(x_all, gain, w, cos, sin, seq):
    model = x_all.shape[1]
    width = w.shape[1] // 3
    block = 256
    row = lambda cols: pl.BlockSpec((block, cols), lambda i: (i, 0))
    col = pl.BlockSpec((width, block), lambda i: (0, i))
    flat = jax.ShapeDtypeStruct((seq, width), BF)
    turned = jax.ShapeDtypeStruct((width, seq), BF)
    return pl.pallas_call(
        proj_kernel,
        grid=(seq // block,),
        in_specs=[
            row(model),
            pl.BlockSpec((1, model), lambda i: (0, 0)),
            pl.BlockSpec(w.shape, lambda i: (0, 0)),
            row(HD),
            row(HD),
        ],
        out_specs=[row(model), row(width), row(width), row(width), col, col],
        out_shape=[jax.ShapeDtypeStruct((seq, model), BF), flat, flat, flat, turned, turned],
        compiler_params=pltpu.CompilerParams(vmem_limit_bytes=VMEM_LIMIT),
        cost_estimate=pl.CostEstimate(
            flops=2 * seq * model * w.shape[1], bytes_accessed=seq * model * 6, transcendentals=0
        ),
    )(x_all, gain, w, cos, sin)


def causal(rows):
    shape = (rows, rows)
    key = lax.broadcasted_iota(jnp.int32, shape, 0)
    query = lax.broadcasted_iota(jnp.int32, shape, 1)
    return key <= query


def attend_kernel(block, count, scale, q_ref, k_ref, vt_ref, o_ref, lse_ref):
    step = pl.program_id(1)
    for j in range(count):

        @pl.when(step == j)
        def _():
            whole = j * block
            q = q_ref[...]
            tail = dot_nt(k_ref[whole : whole + block, :], q) * scale
            tail = jnp.where(causal(block), tail, masked_score)
            top = jnp.max(tail, axis=0, keepdims=True)
            if j:
                front = dot_nt(k_ref[:whole, :], q) * scale
                top = jnp.maximum(top, jnp.max(front, axis=0, keepdims=True))
            tail = jnp.exp(tail - top)
            total = jnp.sum(tail, axis=0, keepdims=True)
            mixed = dot_nn(vt_ref[:, whole : whole + block], tail.astype(BF))
            if j:
                front = jnp.exp(front - top)
                total = total + jnp.sum(front, axis=0, keepdims=True)
                mixed = mixed + dot_nn(vt_ref[:, :whole], front.astype(BF))
            o_ref[...] = (mixed / total).T.astype(BF)
            lse_ref[0] = top + jnp.log(total)


def attend(q, k, vt, block):
    seq, width = q.shape
    count = seq // block
    heads = width // HD
    scale = 1.0 / math.sqrt(HD)
    return pl.pallas_call(
        functools.partial(attend_kernel, block, count, scale),
        grid=(heads, count),
        in_specs=[
            pl.BlockSpec((block, HD), lambda h, i: (i, h)),
            pl.BlockSpec((seq, HD), lambda h, i: (0, h)),
            pl.BlockSpec((HD, seq), lambda h, i: (h, 0)),
        ],
        out_specs=[
            pl.BlockSpec((block, HD), lambda h, i: (i, h)),
            pl.BlockSpec((1, 1, block), lambda h, i: (h, 0, i)),
        ],
        out_shape=[
            jax.ShapeDtypeStruct((seq, width), BF),
            jax.ShapeDtypeStruct((heads, 1, seq), F32),
        ],
        compiler_params=pltpu.CompilerParams(vmem_limit_bytes=VMEM_LIMIT),
        cost_estimate=pl.CostEstimate(
            flops=8 * seq * seq * width, bytes_accessed=seq * width * 8, transcendentals=0
        ),
    )(q, k, vt)


def unrotate(g, cos, sin):
    return g * cos - pltpu.roll(g, HD // 2, 1) * sin


def attend_back_kernel(
    block, count, scale,
    q_ref, k_ref, kt_ref, v_ref, o_ref, do_ref, lse_ref, cos_ref, sin_ref,
    dq_ref, dk_ref, dv_ref, dk_acc, dv_acc,
):
    step = pl.program_id(1)

    @pl.when(step == 0)
    def _():
        dk_acc[...] = jnp.zeros_like(dk_acc)
        dv_acc[...] = jnp.zeros_like(dv_acc)

    for j in range(count):

        @pl.when(step == j)
        def _():
            wide = (j + 1) * block
            here = slice(j * block, wide)
            q = q_ref[...]
            do = do_ref[...]
            row = jnp.sum((do.astype(F32) * o_ref[...].astype(F32)).T, axis=0, keepdims=True)
            lse = lse_ref[0]
            parts = [(slice(0, j * block), False)] if j else []
            parts.append((here, True))
            dq = None
            for span, edge in parts:
                p = jnp.exp(dot_nt(k_ref[span, :], q) * scale - lse)
                if edge:
                    p = jnp.where(causal(block), p, 0.0)
                ds = (p * (dot_nt(v_ref[span, :], do) - row)).astype(BF)
                dv_acc[span, :] += dot_nn(p.astype(BF), do)
                dk_acc[span, :] += dot_nn(ds, q)
                term = dot_nn(kt_ref[:, span], ds)
                dq = term if dq is None else dq + term
            dq_ref[...] = unrotate(dq.T * scale, cos_ref[here, :], sin_ref[here, :]).astype(BF)

    @pl.when(step == count - 1)
    def _():
        dk_ref[...] = unrotate(dk_acc[...] * scale, cos_ref[...], sin_ref[...]).astype(BF)
        dv_ref[...] = dv_acc[...].astype(BF)


def attend_back(q, k, kt, v, o, do, lse, cos, sin, block):
    seq, width = q.shape
    count = seq // block
    heads = width // HD
    scale = 1.0 / math.sqrt(HD)
    piece = pl.BlockSpec((block, HD), lambda h, i: (i, h))
    whole = pl.BlockSpec((seq, HD), lambda h, i: (0, h))
    turned = pl.BlockSpec((HD, seq), lambda h, i: (h, 0))
    table = pl.BlockSpec((seq, HD), lambda h, i: (0, 0))
    flat = jax.ShapeDtypeStruct((seq, width), BF)
    return pl.pallas_call(
        functools.partial(attend_back_kernel, block, count, scale),
        grid=(heads, count),
        in_specs=[
            piece, whole, turned, whole, piece, piece,
            pl.BlockSpec((1, 1, block), lambda h, i: (h, 0, i)), table, table,
        ],
        out_specs=[piece, whole, whole],
        out_shape=[flat, flat, flat],
        scratch_shapes=[pltpu.VMEM((seq, HD), F32), pltpu.VMEM((seq, HD), F32)],
        compiler_params=pltpu.CompilerParams(vmem_limit_bytes=VMEM_LIMIT),
        cost_estimate=pl.CostEstimate(
            flops=20 * seq * seq * width, bytes_accessed=seq * width * 16, transcendentals=0
        ),
    )(q, k, kt, v, o, do, lse, cos, sin)


def expert_kernel(hidden, x_ref, c_ref, w_ref, dx_ref, gu_ref, hid_ref):
    x = x_ref[...]
    gate = dot_nn(x, w_ref[:, :hidden])
    up = dot_nn(x, w_ref[:, hidden : 2 * hidden])
    down = dot_nn(c_ref[...], w_ref[:, 2 * hidden :])
    sig = 1.0 / (1.0 + jnp.exp(-gate))
    act = gate * sig
    hid_ref[...] = (act * up).astype(BF)
    dup = (down * act).astype(BF)
    dgate = (down * up * sig * (1.0 + gate * (1.0 - sig))).astype(BF)
    gu_ref[:, :hidden] = dgate
    gu_ref[:, hidden:] = dup
    dx = dot_nt(dgate, w_ref[:, :hidden]) + dot_nt(dup, w_ref[:, hidden : 2 * hidden])
    dx_ref[...] = dx.astype(dx_ref.dtype)


def expert(x, c, w, kind):
    rows, model = x.shape
    hidden = w.shape[1] // 3
    block = min(256, rows)
    row = lambda cols: pl.BlockSpec((block, cols), lambda i: (i, 0))
    return pl.pallas_call(
        functools.partial(expert_kernel, hidden),
        grid=(rows // block,),
        in_specs=[row(model), row(model), pl.BlockSpec(w.shape, lambda i: (0, 0))],
        out_specs=[row(model), row(2 * hidden), row(hidden)],
        out_shape=[
            jax.ShapeDtypeStruct((rows, model), kind),
            jax.ShapeDtypeStruct((rows, 2 * hidden), BF),
            jax.ShapeDtypeStruct((rows, hidden), BF),
        ],
        compiler_params=pltpu.CompilerParams(vmem_limit_bytes=VMEM_LIMIT),
        cost_estimate=pl.CostEstimate(
            flops=10 * rows * model * hidden, bytes_accessed=rows * model * 12, transcendentals=0
        ),
    )(x, c, w)


def per_device(x, w_qkv, w_out, w_shared, w_experts, gains, routes, gates, d_out):
    tokens, model = x.shape
    hidden = w_shared.shape[1] // 3
    experts, shard = w_experts.shape[:2]
    dps, fss = lax.axis_size("dp"), lax.axis_size("fsdp")
    cores = dps * fss // experts
    lanes = fss // cores
    seq = tokens * fss
    slots = tokens // 2
    per = -(-HEADS // fss)
    busy = -(-HEADS // per)
    width = per * HD
    dp, fs = lax.axis_index("dp"), lax.axis_index("fsdp")
    z, c = fs // cores, fs % cores

    def over_z(value, pairs):
        return lax.ppermute(
            value, "fsdp", [(a * cores + k, b * cores + k) for a, b in pairs for k in range(cores)]
        )

    def turn_z(value, by):
        return over_z(value, [(a, (a + by) % lanes) for a in range(lanes)])

    def over_core(value, m):
        return lax.ppermute(
            value, "fsdp", [(a * cores + k, a * cores + (k ^ m)) for a in range(lanes) for k in range(cores)]
        )

    def over_dp(value, m):
        return lax.ppermute(value, "dp", [(a, a ^ m) for a in range(dps)])

    def up(value, least, most):
        return over_z(value, [(a, a + 1) for a in range(least, most)])

    def down(value, least, most):
        return over_z(value, [(a, a - 1) for a in range(least, most)])

    def gather_z(value):
        buffer = put(jnp.zeros((lanes + 1,) + value.shape, value.dtype), value, z)
        rising = falling = value
        for s in range(1, lanes):
            rising = up(rising, s - 1, lanes - 1)
            falling = down(falling, 1, lanes - s + 1)
            buffer = put(buffer, rising, jnp.where(z >= s, z - s, lanes))
            buffer = put(buffer, falling, jnp.where(z + s < lanes, z + s, lanes))
        return buffer

    def gather_seq(value):
        buffer = jnp.zeros((lanes + 1, cores) + value.shape, value.dtype)

        def place(buffer, block, row):
            buffer = put(buffer, block, row, c)
            for m in range(1, cores):
                buffer = put(buffer, over_core(block, m), row, c ^ m)
            return buffer

        buffer = place(buffer, value, z)
        rising = falling = value
        for s in range(1, lanes):
            rising = up(rising, s - 1, lanes - 1)
            falling = down(falling, 1, lanes - s + 1)
            buffer = place(buffer, rising, jnp.where(z >= s, z - s, lanes))
            buffer = place(buffer, falling, jnp.where(z + s < lanes, z + s, lanes))
        return buffer.reshape((lanes + 1) * cores * value.shape[0], value.shape[1])

    def sum_z(parts):
        rising = falling = None
        for s in range(1, lanes):
            far = take(parts, jnp.clip(z + lanes - s, 0, lanes - 1)).astype(F32)
            near = take(parts, jnp.clip(z - lanes + s, 0, lanes - 1)).astype(F32)
            if rising is not None:
                far = far + rising.astype(F32)
                near = near + falling.astype(F32)
            rising = up(far.astype(BF), 0, s)
            falling = down(near.astype(BF), lanes - s, lanes)
        total = take(parts, z).astype(F32)
        if rising is not None:
            total = total + rising.astype(F32) + falling.astype(F32)
        return total

    def gather_dp(value):
        buffer = put(jnp.zeros((dps,) + value.shape, value.dtype), value, dp)
        for m in range(1, dps):
            buffer = put(buffer, over_dp(value, m), dp ^ m)
        return buffer

    def join_cores(value):
        buffer = jnp.zeros(value.shape[:2] + (cores,) + value.shape[2:], value.dtype)

        def place(buffer, block, k):
            return lax.dynamic_update_slice(buffer, block[:, :, None], (0, 0, k, 0, 0))

        buffer = place(buffer, value, c)
        for m in range(1, cores):
            buffer = place(buffer, over_core(value, m), c ^ m)
        return buffer.reshape(-1, value.shape[-1])

    def gather_rows(value):
        return join_cores(gather_dp(gather_z(value)[:lanes]))

    def own_heads(target):
        cut = w_qkv.reshape(shard, 3, HEADS, HD)
        cut = jnp.pad(cut, ((0, 0), (0, 0), (0, fss * per - HEADS), (0, 0)))
        cut = cut.reshape(shard, 3, fss, width)
        return lax.dynamic_index_in_dim(cut, target, 2, keepdims=False).reshape(shard, 3 * width)

    def gather_heads():
        buffer = put(jnp.zeros((fss, shard, 3 * width), BF), own_heads(fs), fs)
        for k in range(1, fss):
            pairs = [(f, (f + k) % fss) for f in range(fss) if (f + k) % fss < busy]
            buffer = put(
                buffer,
                lax.ppermute(own_heads((fs + k) % fss), "fsdp", pairs),
                (fs - k) % fss,
            )
        return gather_dp(buffer).reshape(model, 3 * width)

    x_all = gather_seq(x)
    w_heads = gather_heads()
    small = gather_z(gains.T.astype(F32))[:lanes]
    gain_all = join_gain = gather_dp(small)
    both = [None] * cores
    gain_buf = jnp.zeros((dps, lanes, cores, 2, shard), F32)
    gain_buf = lax.dynamic_update_slice(gain_buf, join_gain[:, :, None], (0, 0, c, 0, 0))
    for m in range(1, cores):
        gain_buf = lax.dynamic_update_slice(
            gain_buf, over_core(gain_all, m)[:, :, None], (0, 0, c ^ m, 0, 0)
        )
    gain_rows = gain_buf.transpose(3, 0, 1, 2, 4).reshape(2, model)
    gain_one, gain_two = gain_rows[0:1], gain_rows[1:2]

    half = HD // 2
    frequency = 10000.0 ** (-jnp.arange(half, dtype=F32) / half)
    angles = jnp.arange(seq, dtype=jnp.int32).astype(F32)[:, None] * frequency[None, :]
    cosine, sine = jnp.cos(angles), jnp.sin(angles)
    cos = jnp.concatenate([cosine, cosine], axis=1)
    sin = jnp.concatenate([-sine, sine], axis=1)

    table = jnp.concatenate([routes.T.astype(F32), gates.T], axis=0)
    tables = gather_z(table)[:lanes]
    topk = routes.shape[1]
    picks, weights = tables[:, :topk], tables[:, topk:]
    triangle = (jnp.arange(tokens)[:, None] <= jnp.arange(tokens)[None, :]).astype(BF)
    slot_ids = jnp.arange(slots, dtype=F32)
    select, weigh, slot_gate = [], [], []
    for m in range(dps):
        hit = picks == ((dp ^ m) * lanes + z).astype(F32)
        member = jnp.any(hit, axis=1)
        gate = jnp.sum(jnp.where(hit, weights, 0.0), axis=1)
        rank = dot_nn(member.astype(BF), triangle) - 1.0
        match = member[:, None, :] & (rank[:, None, :] == slot_ids[None, :, None])
        select.append(match.astype(BF))
        scaled = jnp.where(match, gate[:, None, :], 0.0)
        weigh.append(scaled.astype(BF))
        slot_gate.append(jnp.sum(scaled, axis=2, keepdims=True))

    def pick(blocks, m):
        return lax.dot_general(
            select[m], blocks, (((2,), (1,)), ((0,), (0,))), preferred_element_type=F32
        )

    xn_one, q, k, v, kt, vt = project(x_all, gain_one, w_heads, cos, sin, seq)

    d_out_z = after(d_out, x_all)
    held = w_experts.reshape(dps, lanes, shard, 3 * hidden)
    held = after(held, x_all)
    mine = lambda where: lax.dynamic_index_in_dim(held, where, 1, keepdims=False)
    rows_z = put(jnp.zeros((lanes, dps, shard, 3 * hidden), BF), mine(z), z)
    for s in range(1, lanes):
        rows_z = put(rows_z, turn_z(mine((z + s) % lanes), s), (z - s) % lanes)
    rows_to = lambda where: lax.dynamic_index_in_dim(rows_z, where, 1, keepdims=False)
    rows_dp = put(jnp.zeros((dps, lanes, shard, 3 * hidden), BF), rows_to(dp), dp)
    for m in range(1, dps):
        rows_dp = put(rows_dp, over_dp(rows_to(dp ^ m), m), dp ^ m)
    w_own = join_cores(rows_dp)

    dense = gather_rows(after(jnp.concatenate([w_out, w_shared], axis=1), x_all))
    out_all = dense[:, :model]
    shared_all = dense[:, model:]

    o, lse = attend(q, k, vt, 256)

    blocks_o = o.reshape(fss, tokens, width)
    mixed = put(jnp.zeros((fss, tokens, width), BF), take(blocks_o, fs), fs)
    for s in range(1, fss):
        pairs = [(f, (f + s) % fss) for f in range(busy)]
        mixed = put(
            mixed,
            lax.ppermute(take(blocks_o, (fs + s) % fss), "fsdp", pairs),
            (fs - s) % fss,
        )
    heads = mixed.transpose(1, 0, 2).reshape(tokens, fss * width)[:, :model]

    middle = x.astype(F32) + dot_nt(heads, out_all)
    inv_two = lax.rsqrt(jnp.mean(middle * middle, axis=1, keepdims=True) + norm_eps)
    unit_two = middle * inv_two
    xn_two = (unit_two * gain_two).astype(BF)

    up_blocks = gather_z(d_out_z)[:lanes]
    in_blocks = gather_z(xn_two)[:lanes]
    xs, cs = [], []
    for m in range(dps):
        part = pick(in_blocks, m).astype(BF)
        xs.append(over_dp(part, m) if m else part)
        part = (pick(up_blocks, m) * slot_gate[m]).astype(BF)
        cs.append(over_dp(part, m) if m else part)
    flat = lambda parts: jnp.stack(parts).reshape(-1, model)
    x_slots, c_slots = flat(xs), flat(cs)
    dx_slots, gu_slots, hid_slots = expert(x_slots, c_slots, w_own, BF)

    dx_shared, gu_shared, hid_shared = expert(xn_two, d_out, shared_all, F32)
    f_shared = dot_nt(hid_shared, shared_all[:, 2 * hidden :])

    def combine(parts, matrix):
        parts = parts.reshape(dps, lanes, slots, model)
        back = [over_dp(parts[m], m) if m else parts[0] for m in range(dps)]
        total = None
        for m in range(dps):
            term = lax.dot_general(
                matrix[m], back[m], (((1,), (1,)), ((0,), (0,))), preferred_element_type=F32
            )
            total = term if total is None else total + term
        return sum_z(total)

    dx_routed = combine(dx_slots, select)
    f_slots = dot_nt(hid_slots, w_own[:, 2 * hidden :]).astype(BF)
    g_own = jnp.concatenate([dot_tn(x_slots, gu_slots), dot_tn(c_slots, hid_slots)], axis=1)
    routed = combine(f_slots, weigh)
    layer_out = (middle + f_shared + routed).astype(BF)

    dxn_two = dx_shared + dx_routed
    scaled = dxn_two * gain_two
    dx_two = d_out.astype(F32) + inv_two * (
        scaled - unit_two * jnp.mean(scaled * unit_two, axis=1, keepdims=True)
    )
    d_attn = dx_two.astype(BF)

    da_all = gather_seq(d_attn)[:seq]
    out_cols = jnp.pad(out_all, ((0, 0), (0, fss * width - model)))
    out_cols = lax.dynamic_slice_in_dim(out_cols, fs * width, width, 1)
    d_o = dot_nn(da_all, out_cols).astype(BF)
    g_out_part = dot_tn(da_all, o)
    dq, dk, dv = attend_back(q, k, kt, v, o, d_o, lse, cos, sin, 256)
    d_qkv = jnp.concatenate([dq, dk, dv], axis=1)
    dxn_part = dot_nt(d_qkv, w_heads).reshape(lanes, cores, tokens, model)
    at_core = lambda k: lax.dynamic_index_in_dim(dxn_part, k, 1, keepdims=False)
    sums = at_core(c)
    for m in range(1, cores):
        sums = sums + over_core(at_core(c ^ m).astype(BF), m).astype(F32)
    dxn_one = sum_z(sums)
    inputs = x.astype(F32)
    inv_one = lax.rsqrt(jnp.mean(inputs * inputs, axis=1, keepdims=True) + norm_eps)
    unit_one = inputs * inv_one
    scaled = dxn_one * gain_one
    d_x = dx_two + inv_one * (scaled - unit_one * jnp.mean(scaled * unit_one, axis=1, keepdims=True))

    def reduce_cores(part):
        part = part.reshape(dps, lanes, cores, shard, part.shape[1])
        at = lambda k: lax.dynamic_index_in_dim(part, k, 2, keepdims=False)
        total = at(c)
        for m in range(1, cores):
            total = total + over_core(at(c ^ m).astype(BF), m).astype(F32)
        return total

    own = reduce_cores(g_own).astype(BF)
    by_dp = put(jnp.zeros_like(own), take(own, dp), dp)
    for m in range(1, dps):
        by_dp = put(by_dp, over_dp(take(own, dp ^ m), m), dp ^ m)
    at_z = lambda where: lax.dynamic_index_in_dim(by_dp, where, 1, keepdims=False)
    by_z = put(jnp.zeros((lanes,) + by_dp.shape[:1] + by_dp.shape[2:], BF), at_z(z), z)
    for s in range(1, lanes):
        by_z = put(by_z, turn_z(at_z((z + s) % lanes), s), (z - s) % lanes)
    g_experts = by_z.transpose(1, 0, 2, 3).reshape(experts, shard, 3 * hidden).astype(F32)

    g_shared_part = jnp.concatenate([dot_tn(xn_two, gu_shared), dot_tn(d_out, hid_shared)], axis=1)
    own = reduce_cores(g_shared_part)
    total = take(own, dp)
    low = own.astype(BF)
    for m in range(1, dps):
        total = total + over_dp(take(low, dp ^ m), m).astype(F32)
    low = total.astype(BF)
    g_shared = take(total, z)
    for s in range(1, lanes):
        g_shared = g_shared + turn_z(take(low, (z + s) % lanes), s).astype(F32)

    g_part = jnp.concatenate([dot_tn(xn_one, d_qkv), g_out_part], axis=1)
    g_part = g_part.reshape(dps, fss, shard, 4 * width)
    total = take(g_part, dp)
    low = g_part.astype(BF)
    for m in range(1, dps):
        total = total + over_dp(take(low, dp ^ m), m).astype(F32)
    low = total.astype(BF)
    g_mix = put(jnp.zeros((fss, shard, 4 * width), BF), take(low, fs), fs)
    for s in range(1, fss):
        pairs = [(f, (f + s) % fss) for f in range(busy)]
        g_mix = put(
            g_mix, lax.ppermute(take(low, (fs + s) % fss), "fsdp", pairs), (fs - s) % fss
        )
    g_mix = g_mix.reshape(fss, shard, 4, width).transpose(1, 2, 0, 3).reshape(shard, 4, fss * width)
    g_mix = g_mix[:, :, :model].astype(F32)
    g_qkv = g_mix[:, :3].reshape(shard, 3 * model)
    g_out = g_mix[:, 3]

    one = jnp.sum(w_qkv.astype(F32) * g_qkv, axis=1)
    two = jnp.sum(w_shared[:, : 2 * hidden].astype(F32) * g_shared[:, : 2 * hidden], axis=1)
    two = two + jnp.sum(
        w_experts[:, :, : 2 * hidden].astype(F32) * g_experts[:, :, : 2 * hidden], axis=(0, 2)
    )
    g_gains = jnp.stack([one, two], axis=1) / gains.astype(F32)
    return (layer_out, d_x, g_qkv, g_out, g_shared, g_experts, g_gains)


def solution(mesh):
    rows = P(("dp", "fsdp"), None)
    cube = P(None, ("dp", "fsdp"), None)
    return jax.shard_map(
        per_device,
        mesh=mesh,
        in_specs=(rows, rows, rows, rows, cube, rows, rows, rows, rows),
        out_specs=(rows, rows, rows, rows, rows, cube, rows),
        check_vma=False,
    )
```

```python
import functools
import math

import jax
import jax.numpy as jnp
from jax import lax
from jax.experimental import pallas as pl
from jax.experimental.pallas import tpu as pltpu
from jax.sharding import PartitionSpec as P

HEADS = 10
HD = 128
norm_eps = 1e-06
masked_score = -1000000000.0
BF = jnp.bfloat16
F32 = jnp.float32
VMEM_LIMIT = 60 * 2**20


def dot_nn(a, b):
    return lax.dot_general(a, b, (((1,), (0,)), ((), ())), preferred_element_type=F32)


def dot_nt(a, b):
    return lax.dot_general(a, b, (((1,), (1,)), ((), ())), preferred_element_type=F32)


def dot_tn(a, b):
    return lax.dot_general(a, b, (((0,), (0,)), ((), ())), preferred_element_type=F32)


def after(value, *marks):
    return lax.optimization_barrier((value,) + marks)[0]


def put(buffer, value, *index):
    rest = buffer.ndim - len(index)
    starts = tuple(index) + (0,) * rest
    return lax.dynamic_update_slice(
        buffer, value.reshape((1,) * len(index) + buffer.shape[len(index) :]), starts
    )


def take(values, index):
    return lax.dynamic_index_in_dim(values, index, 0, keepdims=False)


def proj_kernel(x_ref, gain_ref, w_ref, cos_ref, sin_ref, xn_ref, q_ref, k_ref, v_ref, kt_ref, vt_ref):
    x = x_ref[...].astype(F32)
    inv = lax.rsqrt(jnp.mean(x * x, axis=1, keepdims=True) + norm_eps)
    xn = (x * inv * gain_ref[...]).astype(BF)
    xn_ref[...] = xn
    width = q_ref.shape[1]
    cos = cos_ref[...]
    sin = sin_ref[...]
    for part in range(3):
        for head in range(width // HD):
            lo = part * width + head * HD
            u = dot_nn(xn, w_ref[:, lo : lo + HD])
            cols = slice(head * HD, (head + 1) * HD)
            if part < 2:
                u = u * cos + pltpu.roll(u, HD // 2, 1) * sin
            low = u.astype(BF)
            if part == 0:
                q_ref[:, cols] = low
            elif part == 1:
                k_ref[:, cols] = low
                kt_ref[cols, :] = u.T.astype(BF)
            else:
                v_ref[:, cols] = low
                vt_ref[cols, :] = u.T.astype(BF)


def project(x_all, gain, w, cos, sin, seq):
    model = x_all.shape[1]
    width = w.shape[1] // 3
    block = 256
    row = lambda cols: pl.BlockSpec((block, cols), lambda i: (i, 0))
    col = pl.BlockSpec((width, block), lambda i: (0, i))
    flat = jax.ShapeDtypeStruct((seq, width), BF)
    turned = jax.ShapeDtypeStruct((width, seq), BF)
    return pl.pallas_call(
        proj_kernel,
        grid=(seq // block,),
        in_specs=[
            row(model),
            pl.BlockSpec((1, model), lambda i: (0, 0)),
            pl.BlockSpec(w.shape, lambda i: (0, 0)),
            row(HD),
            row(HD),
        ],
        out_specs=[row(model), row(width), row(width), row(width), col, col],
        out_shape=[jax.ShapeDtypeStruct((seq, model), BF), flat, flat, flat, turned, turned],
        compiler_params=pltpu.CompilerParams(vmem_limit_bytes=VMEM_LIMIT),
        cost_estimate=pl.CostEstimate(
            flops=2 * seq * model * w.shape[1], bytes_accessed=seq * model * 6, transcendentals=0
        ),
    )(x_all, gain, w, cos, sin)


def causal(rows):
    shape = (rows, rows)
    key = lax.broadcasted_iota(jnp.int32, shape, 0)
    query = lax.broadcasted_iota(jnp.int32, shape, 1)
    return key <= query


def attend_kernel(block, count, scale, q_ref, k_ref, vt_ref, o_ref, lse_ref):
    step = pl.program_id(1)
    for j in range(count):

        @pl.when(step == j)
        def _():
            whole = j * block
            q = q_ref[...]
            tail = dot_nt(k_ref[whole : whole + block, :], q) * scale
            tail = jnp.where(causal(block), tail, masked_score)
            top = jnp.max(tail, axis=0, keepdims=True)
            if j:
                front = dot_nt(k_ref[:whole, :], q) * scale
                top = jnp.maximum(top, jnp.max(front, axis=0, keepdims=True))
            tail = jnp.exp(tail - top)
            total = jnp.sum(tail, axis=0, keepdims=True)
            mixed = dot_nn(vt_ref[:, whole : whole + block], tail.astype(BF))
            if j:
                front = jnp.exp(front - top)
                total = total + jnp.sum(front, axis=0, keepdims=True)
                mixed = mixed + dot_nn(vt_ref[:, :whole], front.astype(BF))
            o_ref[...] = (mixed / total).T.astype(BF)
            lse_ref[0] = top + jnp.log(total)


def attend(q, k, vt, block):
    seq, width = q.shape
    count = seq // block
    heads = width // HD
    scale = 1.0 / math.sqrt(HD)
    return pl.pallas_call(
        functools.partial(attend_kernel, block, count, scale),
        grid=(heads, count),
        in_specs=[
            pl.BlockSpec((block, HD), lambda h, i: (i, h)),
            pl.BlockSpec((seq, HD), lambda h, i: (0, h)),
            pl.BlockSpec((HD, seq), lambda h, i: (h, 0)),
        ],
        out_specs=[
            pl.BlockSpec((block, HD), lambda h, i: (i, h)),
            pl.BlockSpec((1, 1, block), lambda h, i: (h, 0, i)),
        ],
        out_shape=[
            jax.ShapeDtypeStruct((seq, width), BF),
            jax.ShapeDtypeStruct((heads, 1, seq), F32),
        ],
        compiler_params=pltpu.CompilerParams(vmem_limit_bytes=VMEM_LIMIT),
        cost_estimate=pl.CostEstimate(
            flops=8 * seq * seq * width, bytes_accessed=seq * width * 8, transcendentals=0
        ),
    )(q, k, vt)


def unrotate(g, cos, sin):
    return g * cos - pltpu.roll(g, HD // 2, 1) * sin


def attend_back_kernel(
    block, count, scale,
    q_ref, k_ref, kt_ref, v_ref, o_ref, do_ref, lse_ref, cos_ref, sin_ref,
    dq_ref, dk_ref, dv_ref, dk_acc, dv_acc,
):
    step = pl.program_id(1)

    @pl.when(step == 0)
    def _():
        dk_acc[...] = jnp.zeros_like(dk_acc)
        dv_acc[...] = jnp.zeros_like(dv_acc)

    for j in range(count):

        @pl.when(step == j)
        def _():
            wide = (j + 1) * block
            here = slice(j * block, wide)
            q = q_ref[...]
            do = do_ref[...]
            row = jnp.sum((do.astype(F32) * o_ref[...].astype(F32)).T, axis=0, keepdims=True)
            lse = lse_ref[0]
            parts = [(slice(0, j * block), False)] if j else []
            parts.append((here, True))
            dq = None
            for span, edge in parts:
                p = jnp.exp(dot_nt(k_ref[span, :], q) * scale - lse)
                if edge:
                    p = jnp.where(causal(block), p, 0.0)
                ds = (p * (dot_nt(v_ref[span, :], do) - row)).astype(BF)
                dv_acc[span, :] += dot_nn(p.astype(BF), do)
                dk_acc[span, :] += dot_nn(ds, q)
                term = dot_nn(kt_ref[:, span], ds)
                dq = term if dq is None else dq + term
            dq_ref[...] = unrotate(dq.T * scale, cos_ref[here, :], sin_ref[here, :]).astype(BF)

    @pl.when(step == count - 1)
    def _():
        dk_ref[...] = unrotate(dk_acc[...] * scale, cos_ref[...], sin_ref[...]).astype(BF)
        dv_ref[...] = dv_acc[...].astype(BF)


def attend_back(q, k, kt, v, o, do, lse, cos, sin, block):
    seq, width = q.shape
    count = seq // block
    heads = width // HD
    scale = 1.0 / math.sqrt(HD)
    piece = pl.BlockSpec((block, HD), lambda h, i: (i, h))
    whole = pl.BlockSpec((seq, HD), lambda h, i: (0, h))
    turned = pl.BlockSpec((HD, seq), lambda h, i: (h, 0))
    table = pl.BlockSpec((seq, HD), lambda h, i: (0, 0))
    flat = jax.ShapeDtypeStruct((seq, width), BF)
    return pl.pallas_call(
        functools.partial(attend_back_kernel, block, count, scale),
        grid=(heads, count),
        in_specs=[
            piece, whole, turned, whole, piece, piece,
            pl.BlockSpec((1, 1, block), lambda h, i: (h, 0, i)), table, table,
        ],
        out_specs=[piece, whole, whole],
        out_shape=[flat, flat, flat],
        scratch_shapes=[pltpu.VMEM((seq, HD), F32), pltpu.VMEM((seq, HD), F32)],
        compiler_params=pltpu.CompilerParams(vmem_limit_bytes=VMEM_LIMIT),
        cost_estimate=pl.CostEstimate(
            flops=20 * seq * seq * width, bytes_accessed=seq * width * 16, transcendentals=0
        ),
    )(q, k, kt, v, o, do, lse, cos, sin)


def expert_kernel(hidden, x_ref, c_ref, w_ref, dx_ref, gu_ref, hid_ref):
    x = x_ref[...]
    gate = dot_nn(x, w_ref[:, :hidden])
    up = dot_nn(x, w_ref[:, hidden : 2 * hidden])
    down = dot_nn(c_ref[...], w_ref[:, 2 * hidden :])
    sig = 1.0 / (1.0 + jnp.exp(-gate))
    act = gate * sig
    hid_ref[...] = (act * up).astype(BF)
    dup = (down * act).astype(BF)
    dgate = (down * up * sig * (1.0 + gate * (1.0 - sig))).astype(BF)
    gu_ref[:, :hidden] = dgate
    gu_ref[:, hidden:] = dup
    dx = dot_nt(dgate, w_ref[:, :hidden]) + dot_nt(dup, w_ref[:, hidden : 2 * hidden])
    dx_ref[...] = dx.astype(dx_ref.dtype)


def expert(x, c, w, kind):
    rows, model = x.shape
    hidden = w.shape[1] // 3
    block = min(256, rows)
    row = lambda cols: pl.BlockSpec((block, cols), lambda i: (i, 0))
    return pl.pallas_call(
        functools.partial(expert_kernel, hidden),
        grid=(rows // block,),
        in_specs=[row(model), row(model), pl.BlockSpec(w.shape, lambda i: (0, 0))],
        out_specs=[row(model), row(2 * hidden), row(hidden)],
        out_shape=[
            jax.ShapeDtypeStruct((rows, model), kind),
            jax.ShapeDtypeStruct((rows, 2 * hidden), BF),
            jax.ShapeDtypeStruct((rows, hidden), BF),
        ],
        compiler_params=pltpu.CompilerParams(vmem_limit_bytes=VMEM_LIMIT),
        cost_estimate=pl.CostEstimate(
            flops=10 * rows * model * hidden, bytes_accessed=rows * model * 12, transcendentals=0
        ),
    )(x, c, w)


MESH = pl.DeviceIdType.MESH
ANY = pl.BlockSpec(memory_space=pl.ANY)


def place(cores):
    dp, fs = lax.axis_index("dp"), lax.axis_index("fsdp")
    return dp, fs, fs // cores, fs % cores


def greet(peers):
    barrier = pltpu.get_barrier_semaphore()
    for peer in peers:
        pl.semaphore_signal(barrier, inc=1, device_id=peer, device_id_type=MESH)
    pl.semaphore_wait(barrier, len(peers))


def sequence_peers(dp, fs, fss):
    return [(dp, lax.rem(fs + k, fss)) for k in range(1, fss)]


def send(source, target, out, came, peer):
    return pltpu.make_async_remote_copy(
        src_ref=source, dst_ref=target, send_sem=out, recv_sem=came, device_id=peer, device_id_type=MESH
    )


class Chain:
    def __init__(self, own, full, lanes, cores, sems):
        self.own, self.full, self.lanes, self.cores = own, full, lanes, cores
        self.z_out, self.z_in, self.c_out, self.c_in, self.local = sems
        self.dp, self.fs, self.z, self.c = place(cores)

    def hop(self, side, step, block):
        by = self.cores if side == 0 else -self.cores
        source = self.own if step == 0 else self.full.at[block, self.c]
        return send(
            source, self.full.at[block, self.c], self.z_out.at[side, step], self.z_in.at[side, step],
            (self.dp, self.fs + by),
        )

    def across(self, m, block, source, core):
        return send(
            source, self.full.at[block, core], self.c_out.at[m - 1, block], self.c_in.at[m - 1, block],
            (self.dp, self.z * self.cores + lax.rem(self.c + m, self.cores)),
        )

    def keep(self):
        return pltpu.make_async_copy(self.own, self.full.at[self.z, self.c], self.local)

    def has_next(self, side):
        return self.z < self.lanes - 1 if side == 0 else self.z > 0

    def begin(self):
        for side in (0, 1):

            @pl.when(self.has_next(side))
            def _():
                self.hop(side, 0, self.z).start()

        for m in range(1, self.cores):
            self.across(m, self.z, self.own, self.c).start()
        self.keep().start()

    def came(self, side, step):
        block = self.z - step if side == 0 else self.z + step
        return block, (block >= 0) & (block < self.lanes)

    def advance(self, step):
        for side in (0, 1):
            block, there = self.came(side, step)

            @pl.when(there)
            def _():
                self.hop(side, step - 1, block).wait_recv()

            @pl.when(there & self.has_next(side))
            def _():
                self.hop(side, step, block).start()

            @pl.when(there)
            def _():
                for m in range(1, self.cores):
                    self.across(m, block, self.full.at[block, self.c], self.c).start()

    def finish(self):
        self.keep().wait()
        for m in range(1, self.cores):
            for block in range(self.lanes):
                self.across(m, block, self.own, lax.rem(self.c + self.cores - m, self.cores)).wait_recv()
        for side in (0, 1):
            for step in range(self.lanes - 1):
                block, there = self.came(side, step)

                @pl.when(there & self.has_next(side))
                def _():
                    self.hop(side, step, block).wait_send()

        for m in range(1, self.cores):
            for block in range(self.lanes):
                self.across(m, block, self.own, self.c).wait_send()


def chain_sems(lanes, cores):
    dma = pltpu.SemaphoreType.DMA
    hops = (2, max(lanes - 1, 1))
    ways = (max(cores - 1, 1), lanes)
    return [dma(hops), dma(hops), dma(ways), dma(ways), dma]


def gather_kernel(lanes, cores, x_ref, full_ref, *sems):
    chain = Chain(x_ref, full_ref, lanes, cores, sems)
    greet(sequence_peers(chain.dp, chain.fs, lanes * cores))
    chain.begin()
    for step in range(1, lanes):
        chain.advance(step)
    chain.finish()


def gather_sequence(x, lanes, cores):
    return pl.pallas_call(
        functools.partial(gather_kernel, lanes, cores),
        in_specs=[ANY],
        out_specs=ANY,
        out_shape=jax.ShapeDtypeStruct((lanes, cores) + x.shape, x.dtype),
        scratch_shapes=chain_sems(lanes, cores),
        compiler_params=pltpu.CompilerParams(collective_id=1, has_side_effects=True),
    )(x)


def start_kernel(
    dps, lanes, cores, x_ref, wh_ref, tab_ref, wo_ref, full_ref, heads_ref, tabs_ref, out_ref,
    h_out, h_in, hd_out, hd_in, t_out, t_in, o_out, o_in, od_out, od_in, oc_out, oc_in, locals_, *sems,
):
    chain = Chain(x_ref, full_ref, lanes, cores, sems)
    dp, fs, z, c = chain.dp, chain.fs, chain.z, chain.c
    fss = lanes * cores
    greet(sequence_peers(dp, fs, fss) + [(lax.rem(dp + m, dps), fs) for m in range(1, dps)])
    chain.begin()
    kept = [
        pltpu.make_async_copy(wh_ref.at[fs], heads_ref.at[dp, fs], locals_.at[0]),
        pltpu.make_async_copy(tab_ref, tabs_ref.at[z], locals_.at[1]),
        pltpu.make_async_copy(wo_ref, out_ref.at[dp, z, c], locals_.at[2]),
    ]
    for copy in kept:
        copy.start()

    def heads_to(k):
        t = lax.rem(fs + k, fss)
        return send(wh_ref.at[t], heads_ref.at[dp, fs], h_out.at[k - 1], h_in.at[k - 1], (dp, t))

    def table_to(k):
        t = lax.rem(z + k, lanes) * cores + c
        return send(tab_ref, tabs_ref.at[z], t_out.at[k - 1], t_in.at[k - 1], (dp, t))

    def out_to(k):
        t = lax.rem(z + k, lanes) * cores + c
        return send(wo_ref, out_ref.at[dp, z, c], o_out.at[k - 1], o_in.at[k - 1], (dp, t))

    def heads_over(m, block):
        return send(
            heads_ref.at[block], heads_ref.at[block], hd_out.at[m - 1], hd_in.at[m - 1],
            (lax.rem(dp + m, dps), fs),
        )

    def out_over(m, block):
        piece = out_ref.at[block, :, c]
        return send(piece, piece, od_out.at[m - 1], od_in.at[m - 1], (lax.rem(dp + m, dps), fs))

    def out_across(m, core):
        piece = out_ref.at[:, :, core]
        return send(piece, piece, oc_out.at[m - 1], oc_in.at[m - 1], (dp, z * cores + lax.rem(c + m, cores)))

    for k in range(1, fss):
        heads_to(k).start()
    for k in range(1, lanes):
        out_to(k).start()
        table_to(k).start()
    if lanes > 1:
        chain.advance(1)
    for copy in kept:
        copy.wait()
    for k in range(1, fss):
        heads_to(k).wait_recv()
    for m in range(1, dps):
        heads_over(m, dp).start()
    for k in range(1, lanes):
        out_to(k).wait_recv()
    for m in range(1, dps):
        out_over(m, dp).start()
    for step in range(2, lanes):
        chain.advance(step)
    for k in range(1, lanes):
        table_to(k).wait_recv()
    for m in range(1, dps):
        out_over(m, lax.rem(dp + dps - m, dps)).wait_recv()
    for m in range(1, cores):
        out_across(m, c).start()
    for m in range(1, dps):
        heads_over(m, lax.rem(dp + dps - m, dps)).wait_recv()
    chain.finish()
    for m in range(1, cores):
        out_across(m, lax.rem(c + cores - m, cores)).wait_recv()
    for k in range(1, fss):
        heads_to(k).wait_send()
    for k in range(1, lanes):
        out_to(k).wait_send()
        table_to(k).wait_send()
    for m in range(1, dps):
        heads_over(m, dp).wait_send()
        out_over(m, dp).wait_send()
    for m in range(1, cores):
        out_across(m, c).wait_send()


def start(x, wh, table, w_out, dps, lanes, cores):
    fss = lanes * cores
    dma = pltpu.SemaphoreType.DMA
    pair = lambda n: [dma((max(n - 1, 1),)), dma((max(n - 1, 1),))]
    shapes = [
        jax.ShapeDtypeStruct((lanes, cores) + x.shape, x.dtype),
        jax.ShapeDtypeStruct((dps,) + wh.shape, wh.dtype),
        jax.ShapeDtypeStruct((lanes,) + table.shape, table.dtype),
        jax.ShapeDtypeStruct((dps, lanes, cores) + w_out.shape, w_out.dtype),
    ]
    return pl.pallas_call(
        functools.partial(start_kernel, dps, lanes, cores),
        in_specs=[ANY] * 4,
        out_specs=[ANY] * 4,
        out_shape=shapes,
        scratch_shapes=pair(fss) + pair(dps) + pair(lanes) + pair(lanes) + pair(dps) + pair(cores)
        + [dma((3,))] + chain_sems(lanes, cores),
        compiler_params=pltpu.CompilerParams(collective_id=0, has_side_effects=True),
    )(x, wh, table, w_out)


def heads_kernel(lanes, cores, busy, o_ref, mix_ref, out, came, local):
    dp, fs, z, c = place(cores)
    fss = lanes * cores
    tokens, width = mix_ref.shape[0], o_ref.shape[1]
    greet(sequence_peers(dp, fs, fss))

    def columns(f):
        return mix_ref.at[:, pl.ds(pl.multiple_of(f * width, HD), width)]

    def rows(f):
        return o_ref.at[pl.ds(pl.multiple_of(f * tokens, tokens), tokens), :]

    def to(k, owner):
        t = lax.rem(fs + k, fss)
        return send(rows(t), columns(owner), out.at[k - 1], came.at[k - 1], (dp, t))

    keep = pltpu.make_async_copy(rows(fs), columns(fs), local)

    @pl.when(fs < busy)
    def _():
        for k in range(1, fss):
            to(k, fs).start()
        keep.start()

    for k in range(1, fss):
        owner = lax.rem(fs + fss - k, fss)

        @pl.when(owner < busy)
        def _():
            to(k, owner).wait_recv()

    @pl.when(fs < busy)
    def _():
        keep.wait()
        for k in range(1, fss):
            to(k, fs).wait_send()


def heads_home(o, tokens, lanes, cores, busy):
    fss = lanes * cores
    dma = pltpu.SemaphoreType.DMA
    return pl.pallas_call(
        functools.partial(heads_kernel, lanes, cores, busy),
        in_specs=[ANY],
        out_specs=ANY,
        out_shape=jax.ShapeDtypeStruct((tokens, busy * o.shape[1]), o.dtype),
        scratch_shapes=[dma((fss - 1,)), dma((fss - 1,)), dma],
        compiler_params=pltpu.CompilerParams(collective_id=2, has_side_effects=True),
    )(o)


def dispatch_kernel(
    dps, lanes, cores, x_ref, pick_ref, out_ref, line, stage,
    z_out, z_in, d_out_, d_in, local,
):
    dp, fs, z, c = place(cores)
    peers = [(lax.rem(dp + m, dps), fs) for m in range(1, dps)]
    barrier = pltpu.get_barrier_semaphore()
    for peer in peers:
        pl.semaphore_signal(barrier, inc=1, device_id=peer, device_id_type=MESH)
    for side in (0, 1):
        near = fs + (cores if side == 0 else -cores)

        @pl.when(z < lanes - 1 if side == 0 else z > 0)
        def _():
            pl.semaphore_signal(barrier, inc=1, device_id=(dp, near), device_id_type=MESH)

    ends = (z > 0).astype(jnp.int32) + (z < lanes - 1).astype(jnp.int32)
    pl.semaphore_wait(barrier, len(peers) + ends)

    def hop(side, step, block):
        near = fs + (cores if side == 0 else -cores)
        source = x_ref if step == 0 else line.at[block]
        return send(source, line.at[block], z_out.at[side, step], z_in.at[side, step], (dp, near))

    def over(m, block):
        return send(
            stage.at[m, block], out_ref.at[m, block], d_out_.at[m - 1, block], d_in.at[m - 1, block],
            (lax.rem(dp + m, dps), fs),
        )

    def keep(block):
        return pltpu.make_async_copy(stage.at[0, block], out_ref.at[0, block], local.at[block])

    def has_next(side):
        return z < lanes - 1 if side == 0 else z > 0

    def pick(block, source):
        for m in list(range(1, dps)) + [0]:
            stage[m, block] = dot_nn(pick_ref[m, block], source[...]).astype(BF)
            if m:
                over(m, block).start()
            else:
                keep(block).start()

    for side in (0, 1):

        @pl.when(has_next(side))
        def _():
            hop(side, 0, z).start()

    pick(z, x_ref)
    for step in range(1, lanes):
        for side in (0, 1):
            block = z - step if side == 0 else z + step
            there = (block >= 0) & (block < lanes)

            @pl.when(there)
            def _():
                hop(side, step - 1, block).wait_recv()

            @pl.when(there & has_next(side))
            def _():
                hop(side, step, block).start()

            @pl.when(there)
            def _():
                pick(block, line.at[block])

    for block in range(lanes):
        keep(block).wait()
        for m in range(1, dps):
            over(m, block).wait_recv()
    for step in range(lanes - 1):
        for side in (0, 1):
            block = z - step if side == 0 else z + step
            there = (block >= 0) & (block < lanes)

            @pl.when(there & has_next(side))
            def _():
                hop(side, step, block).wait_send()

    for block in range(lanes):
        for m in range(1, dps):
            over(m, block).wait_send()


def dispatch(x, picks, lanes, cores, number):
    dps, _, slots, tokens = picks.shape
    model = x.shape[1]
    dma = pltpu.SemaphoreType.DMA
    hops = (2, max(lanes - 1, 1))
    ways = (dps - 1, lanes)
    whole = pl.BlockSpec(memory_space=pltpu.VMEM)
    return pl.pallas_call(
        functools.partial(dispatch_kernel, dps, lanes, cores),
        in_specs=[whole, whole],
        out_specs=ANY,
        out_shape=jax.ShapeDtypeStruct((dps, lanes, slots, model), BF),
        scratch_shapes=[
            pltpu.VMEM((lanes, tokens, model), BF),
            pltpu.VMEM((dps, lanes, slots, model), BF),
            dma(hops), dma(hops), dma(ways), dma(ways), dma((lanes,)),
        ],
        compiler_params=pltpu.CompilerParams(
            collective_id=number, has_side_effects=True, vmem_limit_bytes=VMEM_LIMIT
        ),
    )(x, picks)


def combine_kernel(
    dps, lanes, cores, part_ref, mat_ref, out_ref, back, stage, inbox,
    z_out, z_in, d_out_, d_in, local,
):
    dp, fs, z, c = place(cores)
    slots = part_ref.shape[2]
    peers = [(lax.rem(dp + m, dps), fs) for m in range(1, dps)]
    barrier = pltpu.get_barrier_semaphore()
    for peer in peers:
        pl.semaphore_signal(barrier, inc=1, device_id=peer, device_id_type=MESH)

    def has_next(side):
        return z < lanes - 1 if side == 0 else z > 0

    def near(side):
        return (dp, fs + (cores if side == 0 else -cores))

    for side in (0, 1):

        @pl.when(has_next(side))
        def _():
            pl.semaphore_signal(barrier, inc=1, device_id=near(side), device_id_type=MESH)

    ends = (z > 0).astype(jnp.int32) + (z < lanes - 1).astype(jnp.int32)
    pl.semaphore_wait(barrier, len(peers) + ends)

    def over(m, block):
        return send(
            part_ref.at[m, block], back.at[block, m], d_out_.at[m - 1, block], d_in.at[m - 1, block],
            (lax.rem(dp + dps - m, dps), fs),
        )

    def keep(block):
        return pltpu.make_async_copy(part_ref.at[0, block], back.at[block, 0], local.at[block])

    def hop(side, step):
        return send(
            stage.at[side, step - 1], inbox.at[side, step - 1], z_out.at[side, step - 1],
            z_in.at[side, step - 1], near(side),
        )

    def goal(side, step):
        block = z + lanes - step if side == 0 else z - lanes + step
        return block, (block >= 0) & (block < lanes)

    def begin(block):
        for m in range(1, dps):
            over(m, block).start()
        keep(block).start()

    def partial_sum(block):
        keep(block).wait()
        for m in range(1, dps):
            over(m, block).wait_recv()
        total = None
        for m in range(dps):
            term = dot_nn(mat_ref[block, :, m * slots : (m + 1) * slots], back[block, m])
            total = term if total is None else total + term
        return total

    for step in range(1, lanes):
        for side in (0, 1):
            block, there = goal(side, step)

            @pl.when(there)
            def _():
                begin(block)

    begin(z)
    for step in range(1, lanes):
        for side in (0, 1):
            block, there = goal(side, step)
            fed = z > 0 if side == 0 else z < lanes - 1

            @pl.when(there)
            def _():
                total = partial_sum(block)
                stage[side, step - 1] = total.astype(BF)
                if step > 1:

                    @pl.when(fed)
                    def _():
                        hop(side, step - 1).wait_recv()
                        stage[side, step - 1] = (total + inbox[side, step - 2].astype(F32)).astype(BF)

                hop(side, step).start()

    out_ref[...] = partial_sum(z)
    for side in (0, 1):
        fed = z > 0 if side == 0 else z < lanes - 1

        @pl.when(fed)
        def _():
            hop(side, lanes - 1).wait_recv()
            out_ref[...] += inbox[side, lanes - 2].astype(F32)

    for step in range(1, lanes):
        for side in (0, 1):
            block, there = goal(side, step)

            @pl.when(there)
            def _():
                hop(side, step).wait_send()

    for block in range(lanes):
        for m in range(1, dps):
            over(m, block).wait_send()


def combine(parts, matrix, lanes, cores, number):
    dps, _, slots, model = parts.shape
    tokens = matrix.shape[1]
    dma = pltpu.SemaphoreType.DMA
    hops = (2, max(lanes - 1, 1))
    ways = (dps - 1, lanes)
    whole = pl.BlockSpec(memory_space=pltpu.VMEM)
    return pl.pallas_call(
        functools.partial(combine_kernel, dps, lanes, cores),
        in_specs=[ANY, whole],
        out_specs=whole,
        out_shape=jax.ShapeDtypeStruct((tokens, model), F32),
        scratch_shapes=[
            pltpu.VMEM((lanes, dps, slots, model), BF),
            pltpu.VMEM(hops + (tokens, model), BF),
            pltpu.VMEM(hops + (tokens, model), BF),
            dma(hops), dma(hops), dma(ways), dma(ways), dma((lanes,)),
        ],
        compiler_params=pltpu.CompilerParams(
            collective_id=number, has_side_effects=True, vmem_limit_bytes=VMEM_LIMIT
        ),
    )(parts, matrix)


def finish_kernel(
    dps, lanes, cores, busy, part_ref, g_ref, out_ref, mix_ref, from_core, stage, inbox, from_dp, total_g,
    z_out, z_in, c_out, c_in, g_out, g_in, m_out, m_in, local,
):
    dp, fs, z, c = place(cores)
    fss = lanes * cores
    greet(sequence_peers(dp, fs, fss) + [(lax.rem(dp + m, dps), fs) for m in range(1, dps)])

    def has_next(side):
        return z < lanes - 1 if side == 0 else z > 0

    def over(m):
        t = lax.rem(dp + m, dps)
        return send(g_ref.at[t], from_dp.at[m - 1], g_out.at[m - 1], g_in.at[m - 1], (t, fs))

    def across(m, block):
        t = lax.rem(c + m, cores)
        return send(
            part_ref.at[block, t], from_core.at[m - 1, block], c_out.at[m - 1, block], c_in.at[m - 1, block],
            (dp, z * cores + t),
        )

    def hop(side, step):
        return send(
            stage.at[side, step - 1], inbox.at[side, step - 1], z_out.at[side, step - 1],
            z_in.at[side, step - 1], (dp, fs + (cores if side == 0 else -cores)),
        )

    def home(k, owner):
        t = lax.rem(fs + k, fss)
        return send(total_g.at[t], mix_ref.at[owner], m_out.at[k - 1], m_in.at[k - 1], (dp, t))

    def goal(side, step):
        block = z + lanes - step if side == 0 else z - lanes + step
        return block, (block >= 0) & (block < lanes)

    def begin(block):
        for m in range(1, cores):
            across(m, block).start()

    def partial_sum(block):
        total = part_ref[block, c].astype(F32)
        for m in range(1, cores):
            across(m, block).wait_recv()
            total = total + from_core[m - 1, block].astype(F32)
        return total

    def advance(step):
        for side in (0, 1):
            block, there = goal(side, step)
            fed = z > 0 if side == 0 else z < lanes - 1

            @pl.when(there)
            def _():
                total = partial_sum(block)
                stage[side, step - 1] = total.astype(BF)
                if step > 1:

                    @pl.when(fed)
                    def _():
                        hop(side, step - 1).wait_recv()
                        stage[side, step - 1] = (total + inbox[side, step - 2].astype(F32)).astype(BF)

                hop(side, step).start()

    for step in range(1, lanes):
        for side in (0, 1):
            block, there = goal(side, step)

            @pl.when(there)
            def _():
                begin(block)

    begin(z)
    for m in range(1, dps):
        over(m).start()
    for step in range(1, max(lanes - 1, 1)):
        advance(step)
    for m in range(1, dps):
        over(m).wait_recv()
    for f in range(fss):
        total = g_ref[dp, f].astype(F32)
        for m in range(1, dps):
            total = total + from_dp[m - 1, f].astype(F32)
        total_g[f] = total.astype(BF)
    keep = pltpu.make_async_copy(total_g.at[fs], mix_ref.at[fs], local)

    @pl.when(fs < busy)
    def _():
        for k in range(1, fss):
            home(k, fs).start()
        keep.start()

    if lanes > 1:
        advance(lanes - 1)
    out_ref[...] = partial_sum(z)
    for side in (0, 1):
        fed = z > 0 if side == 0 else z < lanes - 1

        @pl.when(fed)
        def _():
            hop(side, lanes - 1).wait_recv()
            out_ref[...] += inbox[side, lanes - 2].astype(F32)

    for k in range(1, fss):
        owner = lax.rem(fs + fss - k, fss)

        @pl.when(owner < busy)
        def _():
            home(k, owner).wait_recv()

    @pl.when(fs < busy)
    def _():
        keep.wait()
        for k in range(1, fss):
            home(k, fs).wait_send()

    for step in range(1, lanes):
        for side in (0, 1):
            block, there = goal(side, step)

            @pl.when(there)
            def _():
                hop(side, step).wait_send()

    for m in range(1, cores):
        for block in range(lanes):
            across(m, block).wait_send()
    for m in range(1, dps):
        over(m).wait_send()


def finish(part, g, lanes, cores, busy):
    dps, fss = g.shape[:2]
    tokens, model = part.shape[2:]
    dma = pltpu.SemaphoreType.DMA
    hops = (2, max(lanes - 1, 1))
    ways = (max(cores - 1, 1), lanes)
    whole = pl.BlockSpec(memory_space=pltpu.VMEM)
    return pl.pallas_call(
        functools.partial(finish_kernel, dps, lanes, cores, busy),
        in_specs=[whole, whole],
        out_specs=[whole, ANY],
        out_shape=[
            jax.ShapeDtypeStruct((tokens, model), F32),
            jax.ShapeDtypeStruct((busy,) + g.shape[2:], BF),
        ],
        scratch_shapes=[
            pltpu.VMEM(ways + (tokens, model), BF),
            pltpu.VMEM(hops + (tokens, model), BF),
            pltpu.VMEM(hops + (tokens, model), BF),
            pltpu.VMEM((dps - 1,) + g.shape[1:], BF),
            pltpu.VMEM(g.shape[1:], BF),
            dma(hops), dma(hops), dma(ways), dma(ways), dma((dps - 1,)), dma((dps - 1,)),
            dma((fss - 1,)), dma((fss - 1,)), dma,
        ],
        compiler_params=pltpu.CompilerParams(
            collective_id=6, has_side_effects=True, vmem_limit_bytes=VMEM_LIMIT
        ),
    )(part, g)


def per_device(x, w_qkv, w_out, w_shared, w_experts, gains, routes, gates, d_out):
    tokens, model = x.shape
    hidden = w_shared.shape[1] // 3
    experts, shard = w_experts.shape[:2]
    dps, fss = lax.axis_size("dp"), lax.axis_size("fsdp")
    cores = dps * fss // experts
    lanes = fss // cores
    seq = tokens * fss
    slots = tokens // 2
    per = -(-HEADS // fss)
    busy = -(-HEADS // per)
    width = per * HD
    dp, fs = lax.axis_index("dp"), lax.axis_index("fsdp")
    z, c = fs // cores, fs % cores

    def over_z(value, pairs):
        return lax.ppermute(
            value, "fsdp", [(a * cores + k, b * cores + k) for a, b in pairs for k in range(cores)]
        )

    def turn_z(value, by):
        return over_z(value, [(a, (a + by) % lanes) for a in range(lanes)])

    def over_core(value, m):
        return lax.ppermute(
            value, "fsdp", [(a * cores + k, a * cores + (k ^ m)) for a in range(lanes) for k in range(cores)]
        )

    def over_dp(value, m):
        return lax.ppermute(value, "dp", [(a, (a + m) % dps) for a in range(dps)])

    def up(value, least, most):
        return over_z(value, [(a, a + 1) for a in range(least, most)])

    def down(value, least, most):
        return over_z(value, [(a, a - 1) for a in range(least, most)])

    def gather_z(value):
        buffer = put(jnp.zeros((lanes + 1,) + value.shape, value.dtype), value, z)
        rising = falling = value
        for s in range(1, lanes):
            rising = up(rising, s - 1, lanes - 1)
            falling = down(falling, 1, lanes - s + 1)
            buffer = put(buffer, rising, jnp.where(z >= s, z - s, lanes))
            buffer = put(buffer, falling, jnp.where(z + s < lanes, z + s, lanes))
        return buffer

    def gather_dp(value):
        buffer = put(jnp.zeros((dps,) + value.shape, value.dtype), value, dp)
        for m in range(1, dps):
            buffer = put(buffer, over_dp(value, m), (dp - m) % dps)
        return buffer

    def join_cores(value):
        buffer = jnp.zeros(value.shape[:2] + (cores,) + value.shape[2:], value.dtype)

        def place(buffer, block, k):
            return lax.dynamic_update_slice(buffer, block[:, :, None], (0, 0, k, 0, 0))

        buffer = place(buffer, value, c)
        for m in range(1, cores):
            buffer = place(buffer, over_core(value, m), c ^ m)
        return buffer.reshape(-1, value.shape[-1])

    def gather_rows(value):
        return join_cores(gather_dp(gather_z(value)[:lanes]))

    cut = w_qkv.reshape(shard, 3, HEADS, HD)
    cut = jnp.pad(cut, ((0, 0), (0, 0), (0, fss * per - HEADS), (0, 0)))
    cut = cut.reshape(shard, 3, fss, width).transpose(2, 0, 1, 3).reshape(fss, shard, 3 * width)
    extra = jnp.broadcast_to(jnp.pad(gains, ((0, 0), (0, HD - 2))), (fss, shard, HD))
    slabs = jnp.concatenate([cut, extra], axis=2)
    topk = routes.shape[1]
    table = jnp.concatenate([routes.T.astype(F32), gates.T], axis=0)
    table = jnp.pad(table, ((0, -2 * topk % 8), (0, 0)))
    x_all, slabs, tables, out_all = start(x, slabs, table, w_out, dps, lanes, cores)
    x_all = x_all.reshape(seq, model)
    slabs = slabs.reshape(model, 3 * width + HD)
    out_all = out_all.reshape(model, model)
    w_heads = jnp.where(fs < busy, slabs[:, : 3 * width], 0)
    gain_rows = slabs[:, 3 * width : 3 * width + 2].astype(F32).T
    gain_one, gain_two = gain_rows[0:1], gain_rows[1:2]

    half = HD // 2
    frequency = 10000.0 ** (-jnp.arange(half, dtype=F32) / half)
    angles = jnp.arange(seq, dtype=jnp.int32).astype(F32)[:, None] * frequency[None, :]
    cosine, sine = jnp.cos(angles), jnp.sin(angles)
    cos = jnp.concatenate([cosine, cosine], axis=1)
    sin = jnp.concatenate([-sine, sine], axis=1)

    picks, weights = tables[:, :topk], tables[:, topk : 2 * topk]
    triangle = (jnp.arange(tokens)[:, None] <= jnp.arange(tokens)[None, :]).astype(BF)
    slot_ids = jnp.arange(slots, dtype=F32)
    select, slot_gate, gather_back, weigh_back = [], [], [], []
    for m in range(dps):
        hit = picks == ((dp + m) % dps * lanes + z).astype(F32)
        member = jnp.any(hit, axis=1)
        gate = jnp.sum(jnp.where(hit, weights, 0.0), axis=1)
        rank = dot_nn(member.astype(BF), triangle) - 1.0
        match = member[:, None, :] & (rank[:, None, :] == slot_ids[None, :, None])
        select.append(match.astype(BF))
        scaled = jnp.where(match, gate[:, None, :], 0.0)
        slot_gate.append(jnp.sum(scaled, axis=2, keepdims=True))
        turned = member[:, :, None] & (rank[:, :, None] == slot_ids[None, None, :])
        gather_back.append(turned.astype(BF))
        weigh_back.append(jnp.where(turned, gate[:, :, None], 0.0).astype(BF))
    select = jnp.stack(select)
    gather_back = jnp.concatenate(gather_back, axis=2)
    weigh_back = jnp.concatenate(weigh_back, axis=2)

    def pick(blocks, m):
        return lax.dot_general(
            select[m], blocks, (((2,), (1,)), ((0,), (0,))), preferred_element_type=F32
        )

    xn_one, q, k, v, kt, vt = project(x_all, gain_one, w_heads, cos, sin, seq)

    d_out_z = after(d_out, x_all)
    groups = [[e * cores + k for e in range(experts)] for k in range(cores)]

    def swap(value):
        return lax.all_to_all(
            value, ("dp", "fsdp"), split_axis=0, concat_axis=0, tiled=True, axis_index_groups=groups
        )

    rows_here = swap(after(w_experts, x_all))
    w_own = join_cores(rows_here.reshape(dps, lanes, shard, 3 * hidden))

    o, lse = attend(q, k, vt, 256)

    heads = heads_home(o, tokens, lanes, cores, busy)[:, :model]
    middle = x.astype(F32) + dot_nt(heads, out_all)
    inv_two = lax.rsqrt(jnp.mean(middle * middle, axis=1, keepdims=True) + norm_eps)
    unit_two = middle * inv_two
    xn_two = (unit_two * gain_two).astype(BF)

    up_blocks = gather_z(after(d_out, x_all))[:lanes]
    cs = []
    for m in range(dps):
        part = (pick(up_blocks, m) * slot_gate[m]).astype(BF)
        cs.append(over_dp(part, m) if m else part)
    c_slots = jnp.stack(cs).reshape(-1, model)
    x_slots = dispatch(xn_two, select, lanes, cores, 3).reshape(-1, model)
    dx_slots, gu_slots, hid_slots = expert(x_slots, c_slots, w_own, BF)

    shared_all = gather_rows(after(w_shared, heads))
    dx_shared, gu_shared, hid_shared = expert(xn_two, d_out, shared_all, F32)
    f_shared = dot_nt(hid_shared, shared_all[:, 2 * hidden :])

    shape = (dps, lanes, slots, model)
    dx_routed = combine(dx_slots.reshape(shape), gather_back, lanes, cores, 4)
    f_slots = dot_nt(hid_slots, w_own[:, 2 * hidden :]).astype(BF)
    g_own = jnp.concatenate([dot_tn(x_slots, gu_slots), dot_tn(c_slots, hid_slots)], axis=1)
    routed = combine(f_slots.reshape(shape), weigh_back, lanes, cores, 5)
    layer_out = (middle + f_shared + routed).astype(BF)

    dxn_two = dx_shared + dx_routed
    scaled = dxn_two * gain_two
    dx_two = d_out.astype(F32) + inv_two * (
        scaled - unit_two * jnp.mean(scaled * unit_two, axis=1, keepdims=True)
    )
    d_attn = dx_two.astype(BF)

    da_all = gather_sequence(d_attn, lanes, cores).reshape(seq, model)
    out_cols = jnp.pad(out_all, ((0, 0), (0, fss * width - model)))
    out_cols = lax.dynamic_slice_in_dim(out_cols, fs * width, width, 1)
    d_o = dot_nn(da_all, out_cols).astype(BF)
    g_out_part = dot_tn(da_all, o)
    dq, dk, dv = attend_back(q, k, kt, v, o, d_o, lse, cos, sin, 256)
    d_qkv = jnp.concatenate([dq, dk, dv], axis=1)
    dxn_part = dot_nt(d_qkv, w_heads).astype(BF).reshape(lanes, cores, tokens, model)
    g_part = jnp.concatenate([dot_tn(xn_one, d_qkv), g_out_part], axis=1).astype(BF)
    dxn_one, g_mix = finish(dxn_part, g_part.reshape(dps, fss, shard, 4 * width), lanes, cores, busy)
    inputs = x.astype(F32)
    inv_one = lax.rsqrt(jnp.mean(inputs * inputs, axis=1, keepdims=True) + norm_eps)
    unit_one = inputs * inv_one
    scaled = dxn_one * gain_one
    d_x = dx_two + inv_one * (scaled - unit_one * jnp.mean(scaled * unit_one, axis=1, keepdims=True))

    def reduce_cores(part):
        part = part.reshape(dps, lanes, cores, shard, part.shape[1])
        at = lambda k: lax.dynamic_index_in_dim(part, k, 2, keepdims=False)
        total = at(c)
        for m in range(1, cores):
            total = total + over_core(at(c ^ m).astype(BF), m).astype(F32)
        return total

    own = reduce_cores(g_own).astype(BF)
    g_experts = swap(own.reshape(experts, shard, 3 * hidden)).astype(F32)

    g_shared_part = jnp.concatenate([dot_tn(xn_two, gu_shared), dot_tn(d_out, hid_shared)], axis=1)
    own = reduce_cores(g_shared_part)
    total = take(own, dp)
    low = own.astype(BF)
    for m in range(1, dps):
        total = total + over_dp(take(low, (dp + m) % dps), m).astype(F32)
    low = total.astype(BF)
    g_shared = take(total, z)
    for s in range(1, lanes):
        g_shared = g_shared + turn_z(take(low, (z + s) % lanes), s).astype(F32)

    g_mix = g_mix.reshape(busy, shard, 4, width).transpose(1, 2, 0, 3).reshape(shard, 4, busy * width)
    g_mix = g_mix[:, :, :model].astype(F32)
    g_qkv = g_mix[:, :3].reshape(shard, 3 * model)
    g_out = g_mix[:, 3]

    one = jnp.sum(w_qkv.astype(F32) * g_qkv, axis=1)
    two = jnp.sum(w_shared[:, : 2 * hidden].astype(F32) * g_shared[:, : 2 * hidden], axis=1)
    two = two + jnp.sum(
        w_experts[:, :, : 2 * hidden].astype(F32) * g_experts[:, :, : 2 * hidden], axis=(0, 2)
    )
    g_gains = jnp.stack([one, two], axis=1) / gains.astype(F32)
    return (layer_out, d_x, g_qkv, g_out, g_shared, g_experts, g_gains)


def solution(mesh):
    rows = P(("dp", "fsdp"), None)
    cube = P(None, ("dp", "fsdp"), None)
    return jax.shard_map(
        per_device,
        mesh=mesh,
        in_specs=(rows, rows, rows, rows, cube, rows, rows, rows, rows),
        out_specs=(rows, rows, rows, rows, rows, cube, rows),
        check_vma=False,
    )
```

```python
import functools
import math

import jax
import jax.numpy as jnp
from jax import lax
from jax.experimental import pallas as pl
from jax.experimental.pallas import tpu as pltpu
from jax.sharding import PartitionSpec as P

HEADS = 10
HD = 128
norm_eps = 1e-06
masked_score = -1000000000.0
BF = jnp.bfloat16
F32 = jnp.float32
VMEM_LIMIT = 60 * 2**20


def dot_nn(a, b):
    return lax.dot_general(a, b, (((1,), (0,)), ((), ())), preferred_element_type=F32)


def dot_nt(a, b):
    return lax.dot_general(a, b, (((1,), (1,)), ((), ())), preferred_element_type=F32)


def dot_tn(a, b):
    return lax.dot_general(a, b, (((0,), (0,)), ((), ())), preferred_element_type=F32)


def lasts(us):
    return pl.CostEstimate(flops=0, bytes_accessed=int(us * 3.6e6), transcendentals=0)


def after(value, *marks):
    return lax.optimization_barrier((value,) + marks)[0]


def put(buffer, value, *index):
    rest = buffer.ndim - len(index)
    starts = tuple(index) + (0,) * rest
    return lax.dynamic_update_slice(
        buffer, value.reshape((1,) * len(index) + buffer.shape[len(index) :]), starts
    )


def take(values, index):
    return lax.dynamic_index_in_dim(values, index, 0, keepdims=False)


def proj_kernel(x_ref, gain_ref, w_ref, cos_ref, sin_ref, xn_ref, q_ref, k_ref, v_ref, kt_ref, vt_ref):
    x = x_ref[...].astype(F32)
    inv = lax.rsqrt(jnp.mean(x * x, axis=1, keepdims=True) + norm_eps)
    xn = (x * inv * gain_ref[...]).astype(BF)
    xn_ref[...] = xn
    width = q_ref.shape[1]
    cos = cos_ref[...]
    sin = sin_ref[...]
    for part in range(3):
        for head in range(width // HD):
            lo = part * width + head * HD
            u = dot_nn(xn, w_ref[:, lo : lo + HD])
            cols = slice(head * HD, (head + 1) * HD)
            if part < 2:
                u = u * cos + pltpu.roll(u, HD // 2, 1) * sin
            low = u.astype(BF)
            if part == 0:
                q_ref[:, cols] = low
            elif part == 1:
                k_ref[:, cols] = low
                kt_ref[cols, :] = u.T.astype(BF)
            else:
                v_ref[:, cols] = low
                vt_ref[cols, :] = u.T.astype(BF)


def project(x_all, gain, w, cos, sin, seq):
    model = x_all.shape[1]
    width = w.shape[1] // 3
    block = 256
    row = lambda cols: pl.BlockSpec((block, cols), lambda i: (i, 0))
    col = pl.BlockSpec((width, block), lambda i: (0, i))
    flat = jax.ShapeDtypeStruct((seq, width), BF)
    turned = jax.ShapeDtypeStruct((width, seq), BF)
    return pl.pallas_call(
        proj_kernel,
        grid=(seq // block,),
        in_specs=[
            row(model),
            pl.BlockSpec((1, model), lambda i: (0, 0)),
            pl.BlockSpec(w.shape, lambda i: (0, 0)),
            row(HD),
            row(HD),
        ],
        out_specs=[row(model), row(width), row(width), row(width), col, col],
        out_shape=[jax.ShapeDtypeStruct((seq, model), BF), flat, flat, flat, turned, turned],
        compiler_params=pltpu.CompilerParams(vmem_limit_bytes=VMEM_LIMIT),
        cost_estimate=lasts(14),
    )(x_all, gain, w, cos, sin)


def causal(rows):
    shape = (rows, rows)
    key = lax.broadcasted_iota(jnp.int32, shape, 0)
    query = lax.broadcasted_iota(jnp.int32, shape, 1)
    return key <= query


def attend_kernel(block, count, scale, q_ref, k_ref, vt_ref, o_ref, lse_ref):
    step = pl.program_id(1)
    for j in range(count):

        @pl.when(step == j)
        def _():
            whole = j * block
            q = q_ref[...]
            tail = dot_nt(k_ref[whole : whole + block, :], q) * scale
            tail = jnp.where(causal(block), tail, masked_score)
            top = jnp.max(tail, axis=0, keepdims=True)
            if j:
                front = dot_nt(k_ref[:whole, :], q) * scale
                top = jnp.maximum(top, jnp.max(front, axis=0, keepdims=True))
            tail = jnp.exp(tail - top)
            total = jnp.sum(tail, axis=0, keepdims=True)
            mixed = dot_nn(vt_ref[:, whole : whole + block], tail.astype(BF))
            if j:
                front = jnp.exp(front - top)
                total = total + jnp.sum(front, axis=0, keepdims=True)
                mixed = mixed + dot_nn(vt_ref[:, :whole], front.astype(BF))
            o_ref[...] = (mixed / total).T.astype(BF)
            lse_ref[0] = top + jnp.log(total)


def attend(q, k, vt, block):
    seq, width = q.shape
    count = seq // block
    heads = width // HD
    scale = 1.0 / math.sqrt(HD)
    return pl.pallas_call(
        functools.partial(attend_kernel, block, count, scale),
        grid=(heads, count),
        in_specs=[
            pl.BlockSpec((block, HD), lambda h, i: (i, h)),
            pl.BlockSpec((seq, HD), lambda h, i: (0, h)),
            pl.BlockSpec((HD, seq), lambda h, i: (h, 0)),
        ],
        out_specs=[
            pl.BlockSpec((block, HD), lambda h, i: (i, h)),
            pl.BlockSpec((1, 1, block), lambda h, i: (h, 0, i)),
        ],
        out_shape=[
            jax.ShapeDtypeStruct((seq, width), BF),
            jax.ShapeDtypeStruct((heads, 1, seq), F32),
        ],
        compiler_params=pltpu.CompilerParams(vmem_limit_bytes=VMEM_LIMIT),
        cost_estimate=lasts(18),
    )(q, k, vt)


def unrotate(g, cos, sin):
    return g * cos - pltpu.roll(g, HD // 2, 1) * sin


def attend_back_kernel(
    block, count, scale,
    q_ref, k_ref, kt_ref, v_ref, o_ref, do_ref, lse_ref, cos_ref, sin_ref,
    dq_ref, dk_ref, dv_ref, dk_acc, dv_acc,
):
    step = pl.program_id(1)

    @pl.when(step == 0)
    def _():
        dk_acc[...] = jnp.zeros_like(dk_acc)
        dv_acc[...] = jnp.zeros_like(dv_acc)

    for j in range(count):

        @pl.when(step == j)
        def _():
            wide = (j + 1) * block
            here = slice(j * block, wide)
            q = q_ref[...]
            do = do_ref[...]
            row = jnp.sum((do.astype(F32) * o_ref[...].astype(F32)).T, axis=0, keepdims=True)
            lse = lse_ref[0]
            parts = [(slice(0, j * block), False)] if j else []
            parts.append((here, True))
            dq = None
            for span, edge in parts:
                p = jnp.exp(dot_nt(k_ref[span, :], q) * scale - lse)
                if edge:
                    p = jnp.where(causal(block), p, 0.0)
                ds = (p * (dot_nt(v_ref[span, :], do) - row)).astype(BF)
                dv_acc[span, :] += dot_nn(p.astype(BF), do)
                dk_acc[span, :] += dot_nn(ds, q)
                term = dot_nn(kt_ref[:, span], ds)
                dq = term if dq is None else dq + term
            dq_ref[...] = unrotate(dq.T * scale, cos_ref[here, :], sin_ref[here, :]).astype(BF)

    @pl.when(step == count - 1)
    def _():
        dk_ref[...] = unrotate(dk_acc[...] * scale, cos_ref[...], sin_ref[...]).astype(BF)
        dv_ref[...] = dv_acc[...].astype(BF)


def attend_back(q, k, kt, v, o, do, lse, cos, sin, block):
    seq, width = q.shape
    count = seq // block
    heads = width // HD
    scale = 1.0 / math.sqrt(HD)
    piece = pl.BlockSpec((block, HD), lambda h, i: (i, h))
    whole = pl.BlockSpec((seq, HD), lambda h, i: (0, h))
    turned = pl.BlockSpec((HD, seq), lambda h, i: (h, 0))
    table = pl.BlockSpec((seq, HD), lambda h, i: (0, 0))
    flat = jax.ShapeDtypeStruct((seq, width), BF)
    return pl.pallas_call(
        functools.partial(attend_back_kernel, block, count, scale),
        grid=(heads, count),
        in_specs=[
            piece, whole, turned, whole, piece, piece,
            pl.BlockSpec((1, 1, block), lambda h, i: (h, 0, i)), table, table,
        ],
        out_specs=[piece, whole, whole],
        out_shape=[flat, flat, flat],
        scratch_shapes=[pltpu.VMEM((seq, HD), F32), pltpu.VMEM((seq, HD), F32)],
        compiler_params=pltpu.CompilerParams(vmem_limit_bytes=VMEM_LIMIT),
        cost_estimate=lasts(25),
    )(q, k, kt, v, o, do, lse, cos, sin)


def expert_kernel(hidden, x_ref, c_ref, w_ref, dx_ref, gu_ref, hid_ref):
    x = x_ref[...]
    gate = dot_nn(x, w_ref[:, :hidden])
    up = dot_nn(x, w_ref[:, hidden : 2 * hidden])
    down = dot_nn(c_ref[...], w_ref[:, 2 * hidden :])
    sig = 1.0 / (1.0 + jnp.exp(-gate))
    act = gate * sig
    hid_ref[...] = (act * up).astype(BF)
    dup = (down * act).astype(BF)
    dgate = (down * up * sig * (1.0 + gate * (1.0 - sig))).astype(BF)
    gu_ref[:, :hidden] = dgate
    gu_ref[:, hidden:] = dup
    dx = dot_nt(dgate, w_ref[:, :hidden]) + dot_nt(dup, w_ref[:, hidden : 2 * hidden])
    dx_ref[...] = dx.astype(dx_ref.dtype)


def expert(x, c, w, kind):
    rows, model = x.shape
    hidden = w.shape[1] // 3
    block = min(256, rows)
    row = lambda cols: pl.BlockSpec((block, cols), lambda i: (i, 0))
    return pl.pallas_call(
        functools.partial(expert_kernel, hidden),
        grid=(rows // block,),
        in_specs=[row(model), row(model), pl.BlockSpec(w.shape, lambda i: (0, 0))],
        out_specs=[row(model), row(2 * hidden), row(hidden)],
        out_shape=[
            jax.ShapeDtypeStruct((rows, model), kind),
            jax.ShapeDtypeStruct((rows, 2 * hidden), BF),
            jax.ShapeDtypeStruct((rows, hidden), BF),
        ],
        compiler_params=pltpu.CompilerParams(vmem_limit_bytes=VMEM_LIMIT),
        cost_estimate=lasts(0.018 * rows),
    )(x, c, w)


MESH = pl.DeviceIdType.MESH
ANY = pl.BlockSpec(memory_space=pl.ANY)


def place(cores):
    dp, fs = lax.axis_index("dp"), lax.axis_index("fsdp")
    return dp, fs, fs // cores, fs % cores


def greet(peers):
    barrier = pltpu.get_barrier_semaphore()
    for peer in peers:
        pl.semaphore_signal(barrier, inc=1, device_id=peer, device_id_type=MESH)
    pl.semaphore_wait(barrier, len(peers))


def sequence_peers(dp, fs, fss):
    return [(dp, lax.rem(fs + k, fss)) for k in range(1, fss)]


def send(source, target, out, came, peer):
    return pltpu.make_async_remote_copy(
        src_ref=source, dst_ref=target, send_sem=out, recv_sem=came, device_id=peer, device_id_type=MESH
    )


class Chain:
    def __init__(self, own, full, lanes, cores, sems):
        self.own, self.full, self.lanes, self.cores = own, full, lanes, cores
        self.z_out, self.z_in, self.c_out, self.c_in, self.local = sems
        self.dp, self.fs, self.z, self.c = place(cores)

    def hop(self, side, step, block):
        by = self.cores if side == 0 else -self.cores
        source = self.own if step == 0 else self.full.at[block, self.c]
        return send(
            source, self.full.at[block, self.c], self.z_out.at[side, step], self.z_in.at[side, step],
            (self.dp, self.fs + by),
        )

    def across(self, m, block, source, core):
        return send(
            source, self.full.at[block, core], self.c_out.at[m - 1, block], self.c_in.at[m - 1, block],
            (self.dp, self.z * self.cores + lax.rem(self.c + m, self.cores)),
        )

    def keep(self):
        return pltpu.make_async_copy(self.own, self.full.at[self.z, self.c], self.local)

    def has_next(self, side):
        return self.z < self.lanes - 1 if side == 0 else self.z > 0

    def begin(self):
        for side in (0, 1):

            @pl.when(self.has_next(side))
            def _():
                self.hop(side, 0, self.z).start()

        for m in range(1, self.cores):
            self.across(m, self.z, self.own, self.c).start()
        self.keep().start()

    def came(self, side, step):
        block = self.z - step if side == 0 else self.z + step
        return block, (block >= 0) & (block < self.lanes)

    def advance(self, step):
        for side in (0, 1):
            block, there = self.came(side, step)

            @pl.when(there)
            def _():
                self.hop(side, step - 1, block).wait_recv()

            @pl.when(there & self.has_next(side))
            def _():
                self.hop(side, step, block).start()

            @pl.when(there)
            def _():
                for m in range(1, self.cores):
                    self.across(m, block, self.full.at[block, self.c], self.c).start()

    def finish(self):
        self.keep().wait()
        for m in range(1, self.cores):
            for block in range(self.lanes):
                self.across(m, block, self.own, lax.rem(self.c + self.cores - m, self.cores)).wait_recv()
        for side in (0, 1):
            for step in range(self.lanes - 1):
                block, there = self.came(side, step)

                @pl.when(there & self.has_next(side))
                def _():
                    self.hop(side, step, block).wait_send()

        for m in range(1, self.cores):
            for block in range(self.lanes):
                self.across(m, block, self.own, self.c).wait_send()


def chain_sems(lanes, cores):
    dma = pltpu.SemaphoreType.DMA
    hops = (2, max(lanes - 1, 1))
    ways = (max(cores - 1, 1), lanes)
    return [dma(hops), dma(hops), dma(ways), dma(ways), dma]


class Line:
    def __init__(self, own, buffer, lanes, cores, out, came):
        self.own, self.buffer, self.lanes, self.cores = own, buffer, lanes, cores
        self.out, self.into = out, came
        self.dp, self.fs, self.z, self.c = place(cores)

    def has_next(self, side):
        return self.z < self.lanes - 1 if side == 0 else self.z > 0

    def near(self, side):
        return (self.dp, self.fs + (self.cores if side == 0 else -self.cores))

    def hop(self, side, step, block):
        source = self.own if step == 0 else self.buffer.at[block]
        return send(
            source, self.buffer.at[block], self.out.at[side, step], self.into.at[side, step], self.near(side)
        )

    def begin(self):
        for side in (0, 1):

            @pl.when(self.has_next(side))
            def _():
                self.hop(side, 0, self.z).start()

    def came(self, side, step):
        block = self.z - step if side == 0 else self.z + step
        return block, (block >= 0) & (block < self.lanes)

    def advance(self, step, then):
        for side in (0, 1):
            block, there = self.came(side, step)

            @pl.when(there)
            def _():
                self.hop(side, step - 1, block).wait_recv()

            @pl.when(there & self.has_next(side))
            def _():
                self.hop(side, step, block).start()

            @pl.when(there)
            def _():
                then(block, self.buffer.at[block])

    def finish(self):
        for step in range(self.lanes - 1):
            for side in (0, 1):
                block, there = self.came(side, step)

                @pl.when(there & self.has_next(side))
                def _():
                    self.hop(side, step, block).wait_send()


class Spread:
    def __init__(self, stage, target, dps, lanes, cores, out, came, local):
        self.stage, self.target, self.dps, self.lanes = stage, target, dps, lanes
        self.out, self.into, self.local = out, came, local
        self.dp, self.fs, self.z, self.c = place(cores)

    def over(self, m, block):
        return send(
            self.stage.at[m, block], self.target.at[m, block], self.out.at[m - 1, block],
            self.into.at[m - 1, block], (lax.rem(self.dp + m, self.dps), self.fs),
        )

    def keep(self, block):
        return pltpu.make_async_copy(
            self.stage.at[0, block], self.target.at[0, block], self.local.at[block]
        )

    def go(self, m, block):
        if m:
            self.over(m, block).start()
        else:
            self.keep(block).start()

    def order(self):
        return list(range(1, self.dps)) + [0]

    def finish(self):
        for block in range(self.lanes):
            self.keep(block).wait()
            for m in range(1, self.dps):
                self.over(m, block).wait_recv()
        for block in range(self.lanes):
            for m in range(1, self.dps):
                self.over(m, block).wait_send()


def start_kernel(
    dps, lanes, cores, topk, x_ref, wh_ref, tab_ref, wo_ref, up_ref,
    full_ref, heads_ref, tabs_ref, out_ref, pick_ref, weigh_ref, c_ref, line_buf, stage,
    h_out, h_in, hd_out, hd_in, t_out, t_in, o_out, o_in, od_out, od_in, oc_out, oc_in, locals_,
    l_out, l_in, s_out, s_in, s_local, *sems,
):
    chain = Chain(x_ref, full_ref, lanes, cores, sems)
    dp, fs, z, c = chain.dp, chain.fs, chain.z, chain.c
    fss = lanes * cores
    line = Line(up_ref, line_buf, lanes, cores, l_out, l_in)
    spread = Spread(stage, c_ref, dps, lanes, cores, s_out, s_in, s_local)
    slots, tokens = pick_ref.shape[2:]
    greet(sequence_peers(dp, fs, fss) + [(lax.rem(dp + m, dps), fs) for m in range(1, dps)])
    chain.begin()
    kept = [
        pltpu.make_async_copy(wh_ref.at[fs], heads_ref.at[dp, fs], locals_.at[0]),
        pltpu.make_async_copy(tab_ref, tabs_ref.at[z], locals_.at[1]),
        pltpu.make_async_copy(wo_ref, out_ref.at[dp, z, c], locals_.at[2]),
    ]
    for copy in kept:
        copy.start()

    def heads_to(k):
        t = lax.rem(fs + k, fss)
        return send(wh_ref.at[t], heads_ref.at[dp, fs], h_out.at[k - 1], h_in.at[k - 1], (dp, t))

    def table_to(k):
        t = lax.rem(z + k, lanes) * cores + c
        return send(tab_ref, tabs_ref.at[z], t_out.at[k - 1], t_in.at[k - 1], (dp, t))

    def out_to(k):
        t = lax.rem(z + k, lanes) * cores + c
        return send(wo_ref, out_ref.at[dp, z, c], o_out.at[k - 1], o_in.at[k - 1], (dp, t))

    def heads_over(m, block):
        return send(
            heads_ref.at[block], heads_ref.at[block], hd_out.at[m - 1], hd_in.at[m - 1],
            (lax.rem(dp + m, dps), fs),
        )

    def out_over(m, block):
        piece = out_ref.at[block, :, c]
        return send(piece, piece, od_out.at[m - 1], od_in.at[m - 1], (lax.rem(dp + m, dps), fs))

    def out_across(m, core):
        piece = out_ref.at[:, :, core]
        return send(
            piece, piece, oc_out.at[m - 1], oc_in.at[m - 1], (dp, z * cores + lax.rem(c + m, cores))
        )

    for k in range(1, lanes):
        table_to(k).start()
    line.begin()
    for k in range(1, fss):
        heads_to(k).start()
    for k in range(1, lanes):
        out_to(k).start()
    for copy in kept:
        copy.wait()
    for k in range(1, lanes):
        table_to(k).wait_recv()

    triangle = (
        lax.broadcasted_iota(jnp.int32, (tokens, tokens), 0)
        <= lax.broadcasted_iota(jnp.int32, (tokens, tokens), 1)
    ).astype(BF)
    slot = lax.broadcasted_iota(jnp.int32, (slots, tokens), 0).astype(F32)
    for m in range(dps):
        name = (lax.rem(dp + m, dps) * lanes + z).astype(F32)
        for block in range(lanes):
            hit = tabs_ref[block, :topk, :] == name
            member = jnp.max(jnp.where(hit, 1.0, 0.0), axis=0, keepdims=True)
            gate = jnp.sum(jnp.where(hit, tabs_ref[block, topk : 2 * topk, :], 0.0), axis=0, keepdims=True)
            rank = dot_nn(jnp.broadcast_to(member, (8, tokens)).astype(BF), triangle)[:1] - 1.0
            match = (rank == slot) & (member > 0.5)
            pick_ref[m, block] = jnp.where(match, 1.0, 0.0).astype(BF)
            weigh_ref[m, block] = jnp.where(match, gate, 0.0).astype(BF)

    def pick(block, source):
        for m in spread.order():
            name = (lax.rem(dp + m, dps) * lanes + z).astype(F32)
            hit = tabs_ref[block, :topk, :] == name
            gate = jnp.sum(jnp.where(hit, tabs_ref[block, topk : 2 * topk, :], 0.0), axis=0, keepdims=True)
            one = pick_ref[m, block]
            scale = jnp.sum(one.astype(F32) * gate, axis=1, keepdims=True)
            stage[m, block] = (dot_nn(one, source[...]) * scale).astype(BF)
            spread.go(m, block)

    if lanes > 1:
        chain.advance(1)
    pick(z, up_ref)
    for k in range(1, fss):
        heads_to(k).wait_recv()
    for m in range(1, dps):
        heads_over(m, dp).start()
    for k in range(1, lanes):
        out_to(k).wait_recv()
    for m in range(1, dps):
        out_over(m, dp).start()
    if lanes > 1:
        line.advance(1, pick)
    for step in range(2, lanes):
        chain.advance(step)
        line.advance(step, pick)
    for m in range(1, dps):
        out_over(m, lax.rem(dp + dps - m, dps)).wait_recv()
    for m in range(1, cores):
        out_across(m, c).start()
    for m in range(1, dps):
        heads_over(m, lax.rem(dp + dps - m, dps)).wait_recv()
    chain.finish()
    line.finish()
    spread.finish()
    for m in range(1, cores):
        out_across(m, lax.rem(c + cores - m, cores)).wait_recv()
    for k in range(1, fss):
        heads_to(k).wait_send()
    for k in range(1, lanes):
        out_to(k).wait_send()
        table_to(k).wait_send()
    for m in range(1, dps):
        heads_over(m, dp).wait_send()
        out_over(m, dp).wait_send()
    for m in range(1, cores):
        out_across(m, c).wait_send()


def start(x, wh, table, w_out, upstream, topk, dps, lanes, cores):
    fss = lanes * cores
    tokens, model = x.shape
    slots = tokens // 2
    dma = pltpu.SemaphoreType.DMA
    pair = lambda n: [dma((max(n - 1, 1),)), dma((max(n - 1, 1),))]
    hops = (2, max(lanes - 1, 1))
    ways = (dps - 1, lanes)
    whole = pl.BlockSpec(memory_space=pltpu.VMEM)
    picks = jax.ShapeDtypeStruct((dps, lanes, slots, tokens), BF)
    shapes = [
        jax.ShapeDtypeStruct((lanes, cores) + x.shape, x.dtype),
        jax.ShapeDtypeStruct((dps,) + wh.shape, wh.dtype),
        jax.ShapeDtypeStruct((lanes,) + table.shape, table.dtype),
        jax.ShapeDtypeStruct((dps, lanes, cores) + w_out.shape, w_out.dtype),
        picks,
        picks,
        jax.ShapeDtypeStruct((dps, lanes, slots, model), BF),
    ]
    return pl.pallas_call(
        functools.partial(start_kernel, dps, lanes, cores, topk),
        in_specs=[ANY] * 4 + [whole],
        out_specs=[ANY, ANY, whole, ANY, whole, whole, ANY],
        out_shape=shapes,
        scratch_shapes=[
            pltpu.VMEM((lanes, tokens, model), BF),
            pltpu.VMEM((dps, lanes, slots, model), BF),
        ]
        + pair(fss) + pair(dps) + pair(lanes) + pair(lanes) + pair(dps) + pair(cores) + [dma((3,))]
        + [dma(hops), dma(hops), dma(ways), dma(ways), dma((lanes,))]
        + chain_sems(lanes, cores),
        cost_estimate=lasts(130),
        compiler_params=pltpu.CompilerParams(
            collective_id=0, has_side_effects=True, vmem_limit_bytes=VMEM_LIMIT
        ),
    )(x, wh, table, w_out, upstream)


def heads_kernel(lanes, cores, busy, o_ref, mix_ref, out, came, local):
    dp, fs, z, c = place(cores)
    fss = lanes * cores
    tokens, width = mix_ref.shape[0], o_ref.shape[1]
    greet(sequence_peers(dp, fs, fss))

    def columns(f):
        return mix_ref.at[:, pl.ds(pl.multiple_of(f * width, HD), width)]

    def rows(f):
        return o_ref.at[pl.ds(pl.multiple_of(f * tokens, tokens), tokens), :]

    def to(k, owner):
        t = lax.rem(fs + k, fss)
        return send(rows(t), columns(owner), out.at[k - 1], came.at[k - 1], (dp, t))

    keep = pltpu.make_async_copy(rows(fs), columns(fs), local)

    @pl.when(fs < busy)
    def _():
        for k in range(1, fss):
            to(k, fs).start()
        keep.start()

    for k in range(1, fss):
        owner = lax.rem(fs + fss - k, fss)

        @pl.when(owner < busy)
        def _():
            to(k, owner).wait_recv()

    @pl.when(fs < busy)
    def _():
        keep.wait()
        for k in range(1, fss):
            to(k, fs).wait_send()


def heads_home(o, tokens, lanes, cores, busy):
    fss = lanes * cores
    dma = pltpu.SemaphoreType.DMA
    return pl.pallas_call(
        functools.partial(heads_kernel, lanes, cores, busy),
        in_specs=[ANY],
        out_specs=ANY,
        out_shape=jax.ShapeDtypeStruct((tokens, busy * o.shape[1]), o.dtype),
        scratch_shapes=[dma((fss - 1,)), dma((fss - 1,)), dma],
        cost_estimate=lasts(25),
        compiler_params=pltpu.CompilerParams(collective_id=2, has_side_effects=True),
    )(o)


def greet_cross(line, dps, cores=1):
    barrier = pltpu.get_barrier_semaphore()
    for m in range(1, dps):
        peer = (lax.rem(line.dp + m, dps), line.fs)
        pl.semaphore_signal(barrier, inc=1, device_id=peer, device_id_type=MESH)
    for side in (0, 1):

        @pl.when(line.has_next(side))
        def _():
            pl.semaphore_signal(barrier, inc=1, device_id=line.near(side), device_id_type=MESH)

    for m in range(1, cores):
        peer = (line.dp, line.z * cores + lax.rem(line.c + m, cores))
        pl.semaphore_signal(barrier, inc=1, device_id=peer, device_id_type=MESH)
    ends = line.has_next(0).astype(jnp.int32) + line.has_next(1).astype(jnp.int32)
    pl.semaphore_wait(barrier, dps - 1 + cores - 1 + ends)


def dispatch_kernel(
    dps, lanes, cores, x_ref, pick_ref, rows_ref, out_ref, w_ref, buffer, stage,
    l_out, l_in, s_out, s_in, s_local, w_out, w_in, w_local,
):
    line = Line(x_ref, buffer, lanes, cores, l_out, l_in)
    spread = Spread(stage, out_ref, dps, lanes, cores, s_out, s_in, s_local)
    greet_cross(line, dps, cores)

    def across(m, core):
        peer = (line.dp, line.z * cores + lax.rem(line.c + m, cores))
        return send(rows_ref, w_ref.at[:, :, core], w_out.at[m - 1], w_in.at[m - 1], peer)

    keep = pltpu.make_async_copy(rows_ref, w_ref.at[:, :, line.c], w_local)

    def pick(block, source):
        for m in spread.order():
            stage[m, block] = dot_nn(pick_ref[m, block], source[...]).astype(BF)
            spread.go(m, block)

    line.begin()
    keep.start()
    for m in range(1, cores):
        across(m, line.c).start()
    pick(line.z, x_ref)
    for step in range(1, lanes):
        line.advance(step, pick)
    spread.finish()
    line.finish()
    keep.wait()
    for m in range(1, cores):
        across(m, lax.rem(line.c + cores - m, cores)).wait_recv()
        across(m, line.c).wait_send()


def dispatch(x, picks, rows, lanes, cores, number):
    dps, _, slots, tokens = picks.shape
    model = x.shape[1]
    dma = pltpu.SemaphoreType.DMA
    hops = (2, max(lanes - 1, 1))
    ways = (dps - 1, lanes)
    whole = pl.BlockSpec(memory_space=pltpu.VMEM)
    return pl.pallas_call(
        functools.partial(dispatch_kernel, dps, lanes, cores),
        in_specs=[whole, whole, ANY],
        out_specs=[ANY, ANY],
        out_shape=[
            jax.ShapeDtypeStruct((dps, lanes, slots, model), BF),
            jax.ShapeDtypeStruct((dps, lanes, cores) + rows.shape[2:], BF),
        ],
        scratch_shapes=[
            pltpu.VMEM((lanes, tokens, model), BF),
            pltpu.VMEM((dps, lanes, slots, model), BF),
            dma(hops), dma(hops), dma(ways), dma(ways), dma((lanes,)),
            dma((max(cores - 1, 1),)), dma((max(cores - 1, 1),)), dma,
        ],
        cost_estimate=lasts(70),
        compiler_params=pltpu.CompilerParams(
            collective_id=number, has_side_effects=True, vmem_limit_bytes=VMEM_LIMIT
        ),
    )(x, picks, rows)


class Combine:
    def __init__(self, parts, picks, result, scratch, dps, lanes, cores):
        self.parts, self.picks, self.result = parts, picks, result
        self.back, self.stage, self.inbox = scratch[:3]
        self.z_out, self.z_in, self.d_out, self.d_in, self.local = scratch[3:]
        self.dps, self.lanes, self.cores = dps, lanes, cores
        self.dp, self.fs, self.z, self.c = place(cores)

    def over(self, m, block):
        return send(
            self.parts.at[m, block], self.back.at[block, m], self.d_out.at[m - 1, block],
            self.d_in.at[m - 1, block], (lax.rem(self.dp + self.dps - m, self.dps), self.fs),
        )

    def keep(self, block):
        return pltpu.make_async_copy(
            self.parts.at[0, block], self.back.at[block, 0], self.local.at[block]
        )

    def hop(self, side, step):
        return send(
            self.stage.at[side, step - 1], self.inbox.at[side, step - 1], self.z_out.at[side, step - 1],
            self.z_in.at[side, step - 1],
            (self.dp, self.fs + (self.cores if side == 0 else -self.cores)),
        )

    def goal(self, side, step):
        block = self.z + self.lanes - step if side == 0 else self.z - self.lanes + step
        return block, (block >= 0) & (block < self.lanes)

    def fed(self, side):
        return self.z > 0 if side == 0 else self.z < self.lanes - 1

    def send_block(self, block):
        for m in range(1, self.dps):
            self.over(m, block).start()
        self.keep(block).start()

    def begin(self):
        for step in range(1, self.lanes):
            for side in (0, 1):
                block, there = self.goal(side, step)

                @pl.when(there)
                def _():
                    self.send_block(block)

        self.send_block(self.z)

    def partial_sum(self, block):
        self.keep(block).wait()
        total = dot_tn(self.picks[0, block], self.back[block, 0])
        for m in range(1, self.dps):
            self.over(m, block).wait_recv()
            total = total + dot_tn(self.picks[m, block], self.back[block, m])
        return total

    def advance(self, step):
        for side in (0, 1):
            block, there = self.goal(side, step)

            @pl.when(there)
            def _():
                total = self.partial_sum(block)
                self.stage[side, step - 1] = total.astype(BF)
                if step > 1:

                    @pl.when(self.fed(side))
                    def _():
                        self.hop(side, step - 1).wait_recv()
                        more = self.inbox[side, step - 2].astype(F32)
                        self.stage[side, step - 1] = (total + more).astype(BF)

                self.hop(side, step).start()

    def finish(self):
        self.result[...] = self.partial_sum(self.z)
        for side in (0, 1):

            @pl.when(self.fed(side))
            def _():
                self.hop(side, self.lanes - 1).wait_recv()
                self.result[...] += self.inbox[side, self.lanes - 2].astype(F32)

        for step in range(1, self.lanes):
            for side in (0, 1):
                block, there = self.goal(side, step)

                @pl.when(there)
                def _():
                    self.hop(side, step).wait_send()

        for block in range(self.lanes):
            for m in range(1, self.dps):
                self.over(m, block).wait_send()


def combine_scratch(dps, lanes, slots, tokens, model):
    dma = pltpu.SemaphoreType.DMA
    hops = (2, max(lanes - 1, 1))
    ways = (dps - 1, lanes)
    return [
        pltpu.VMEM((lanes, dps, slots, model), BF),
        pltpu.VMEM(hops + (tokens, model), BF),
        pltpu.VMEM(hops + (tokens, model), BF),
        dma(hops), dma(hops), dma(ways), dma(ways), dma((lanes,)),
    ]


def combine_kernel(dps, lanes, cores, part_ref, pick_ref, out_ref, *scratch):
    work = Combine(part_ref, pick_ref, out_ref, scratch, dps, lanes, cores)
    greet_cross(Line(None, None, lanes, cores, None, None), dps)
    work.begin()
    for step in range(1, lanes):
        work.advance(step)
    work.finish()


def combine(parts, picks, lanes, cores, number):
    dps, _, slots, model = parts.shape
    tokens = picks.shape[3]
    whole = pl.BlockSpec(memory_space=pltpu.VMEM)
    return pl.pallas_call(
        functools.partial(combine_kernel, dps, lanes, cores),
        in_specs=[ANY, whole],
        out_specs=whole,
        out_shape=jax.ShapeDtypeStruct((tokens, model), F32),
        scratch_shapes=combine_scratch(dps, lanes, slots, tokens, model),
        cost_estimate=lasts(70),
        compiler_params=pltpu.CompilerParams(
            collective_id=number, has_side_effects=True, vmem_limit_bytes=VMEM_LIMIT
        ),
    )(parts, picks)


def turn_kernel(
    dps, lanes, cores, x_ref, part_ref, pick_ref, g_ref, full_ref, out_ref, total_ref,
    own, from_core, from_dp, gc_out, gc_in, gd_out, gd_in, g_local, *scratch,
):
    work = Combine(part_ref, pick_ref, out_ref, scratch[:8], dps, lanes, cores)
    chain = Chain(x_ref, full_ref, lanes, cores, scratch[8:])
    dp, fs, z, c = chain.dp, chain.fs, chain.z, chain.c
    fss = lanes * cores

    def across(m):
        t = lax.rem(c + m, cores)
        return send(
            g_ref.at[:, :, t], from_core.at[m - 1], gc_out.at[m - 1], gc_in.at[m - 1], (dp, z * cores + t)
        )

    def over(m):
        t = lax.rem(dp + m, dps)
        return send(own.at[t], from_dp.at[m - 1], gd_out.at[m - 1], gd_in.at[m - 1], (t, fs))

    keep = pltpu.make_async_copy(g_ref.at[:, :, c], own, g_local)

    def cores_added():
        keep.wait()
        for m in range(1, cores):
            across(m).wait_recv()

        def add(i, carry):
            p, q = i // lanes, lax.rem(i, lanes)
            total = own[p, q].astype(F32)
            for m in range(1, cores):
                total = total + from_core[m - 1, p, q].astype(F32)
            own[p, q] = total.astype(BF)
            return carry

        lax.fori_loop(0, dps * lanes, add, 0)
        for m in range(1, dps):
            over(m).start()

    def dp_added():
        for m in range(1, dps):
            over(m).wait_recv()
        for q in range(lanes):
            total = own[dp, q].astype(F32)
            for m in range(1, dps):
                total = total + from_dp[m - 1, q].astype(F32)
            total_ref[q] = total.astype(BF)
        for m in range(1, cores):
            across(m).wait_send()
        for m in range(1, dps):
            over(m).wait_send()

    greet(sequence_peers(dp, fs, fss) + [(lax.rem(dp + m, dps), fs) for m in range(1, dps)])
    chain.begin()
    work.begin()
    keep.start()
    for m in range(1, cores):
        across(m).start()
    cores_added()
    for step in range(1, lanes):
        chain.advance(step)
        work.advance(step)
    chain.finish()
    work.finish()
    dp_added()


def turn(x, parts, picks, g, lanes, cores):
    dps, _, slots, model = parts.shape
    tokens = picks.shape[3]
    dma = pltpu.SemaphoreType.DMA
    whole = pl.BlockSpec(memory_space=pltpu.VMEM)
    return pl.pallas_call(
        functools.partial(turn_kernel, dps, lanes, cores),
        in_specs=[ANY, ANY, whole, ANY],
        out_specs=[ANY, whole, whole],
        out_shape=[
            jax.ShapeDtypeStruct((lanes, cores) + x.shape, x.dtype),
            jax.ShapeDtypeStruct((tokens, model), F32),
            jax.ShapeDtypeStruct((lanes,) + g.shape[3:], BF),
        ],
        scratch_shapes=[
            pltpu.VMEM((dps, lanes) + g.shape[3:], BF),
            pltpu.VMEM((max(cores - 1, 1), dps, lanes) + g.shape[3:], BF),
            pltpu.VMEM((dps - 1, lanes) + g.shape[3:], BF),
            dma((max(cores - 1, 1),)), dma((max(cores - 1, 1),)), dma((dps - 1,)), dma((dps - 1,)), dma,
        ]
        + combine_scratch(dps, lanes, slots, tokens, model) + chain_sems(lanes, cores),
        cost_estimate=lasts(100),
        compiler_params=pltpu.CompilerParams(
            collective_id=1, has_side_effects=True, vmem_limit_bytes=VMEM_LIMIT
        ),
    )(x, parts, picks, g)


def finish_kernel(
    dps, lanes, cores, busy, part_ref, g_ref, s_ref, out_ref, mix_ref, sum_ref,
    from_core, stage, inbox, from_dp, total_g, from_z,
    z_out, z_in, c_out, c_in, g_out, g_in, m_out, m_in, local, s_out, s_in,
):
    dp, fs, z, c = place(cores)
    fss = lanes * cores
    greet(sequence_peers(dp, fs, fss) + [(lax.rem(dp + m, dps), fs) for m in range(1, dps)])

    def has_next(side):
        return z < lanes - 1 if side == 0 else z > 0

    def over(m):
        t = lax.rem(dp + m, dps)
        return send(g_ref.at[t], from_dp.at[m - 1], g_out.at[m - 1], g_in.at[m - 1], (t, fs))

    def across(m, block):
        t = lax.rem(c + m, cores)
        return send(
            part_ref.at[block, t], from_core.at[m - 1, block], c_out.at[m - 1, block], c_in.at[m - 1, block],
            (dp, z * cores + t),
        )

    def hop(side, step):
        return send(
            stage.at[side, step - 1], inbox.at[side, step - 1], z_out.at[side, step - 1],
            z_in.at[side, step - 1], (dp, fs + (cores if side == 0 else -cores)),
        )

    def home(k, owner):
        t = lax.rem(fs + k, fss)
        return send(total_g.at[t], mix_ref.at[owner], m_out.at[k - 1], m_in.at[k - 1], (dp, t))

    def along(k):
        t = lax.rem(z + k, lanes)
        return send(
            s_ref.at[t], from_z.at[k - 1], s_out.at[k - 1], s_in.at[k - 1], (dp, t * cores + c)
        )

    def goal(side, step):
        block = z + lanes - step if side == 0 else z - lanes + step
        return block, (block >= 0) & (block < lanes)

    def begin(block):
        for m in range(1, cores):
            across(m, block).start()

    def partial_sum(block):
        total = part_ref[block, c].astype(F32)
        for m in range(1, cores):
            across(m, block).wait_recv()
            total = total + from_core[m - 1, block].astype(F32)
        return total

    def advance(step):
        for side in (0, 1):
            block, there = goal(side, step)
            fed = z > 0 if side == 0 else z < lanes - 1

            @pl.when(there)
            def _():
                total = partial_sum(block)
                stage[side, step - 1] = total.astype(BF)
                if step > 1:

                    @pl.when(fed)
                    def _():
                        hop(side, step - 1).wait_recv()
                        stage[side, step - 1] = (total + inbox[side, step - 2].astype(F32)).astype(BF)

                hop(side, step).start()

    for step in range(1, lanes):
        for side in (0, 1):
            block, there = goal(side, step)

            @pl.when(there)
            def _():
                begin(block)

    begin(z)
    for m in range(1, dps):
        over(m).start()
    for step in range(1, max(lanes - 1, 1)):
        advance(step)
    for k in range(1, lanes):
        along(k).start()
    for m in range(1, dps):
        over(m).wait_recv()
    for f in range(fss):
        total = g_ref[dp, f].astype(F32)
        for m in range(1, dps):
            total = total + from_dp[m - 1, f].astype(F32)
        total_g[f] = total.astype(BF)
    keep = pltpu.make_async_copy(total_g.at[fs], mix_ref.at[fs], local)

    @pl.when(fs < busy)
    def _():
        for k in range(1, fss):
            home(k, fs).start()
        keep.start()

    if lanes > 1:
        advance(lanes - 1)
    out_ref[...] = partial_sum(z)
    for side in (0, 1):
        fed = z > 0 if side == 0 else z < lanes - 1

        @pl.when(fed)
        def _():
            hop(side, lanes - 1).wait_recv()
            out_ref[...] += inbox[side, lanes - 2].astype(F32)

    total = s_ref[z].astype(F32)
    for k in range(1, lanes):
        along(k).wait_recv()
        total = total + from_z[k - 1].astype(F32)
    sum_ref[...] = total
    for k in range(1, lanes):
        along(k).wait_send()
    for k in range(1, fss):
        owner = lax.rem(fs + fss - k, fss)

        @pl.when(owner < busy)
        def _():
            home(k, owner).wait_recv()

    @pl.when(fs < busy)
    def _():
        keep.wait()
        for k in range(1, fss):
            home(k, fs).wait_send()

    for step in range(1, lanes):
        for side in (0, 1):
            block, there = goal(side, step)

            @pl.when(there)
            def _():
                hop(side, step).wait_send()

    for m in range(1, cores):
        for block in range(lanes):
            across(m, block).wait_send()
    for m in range(1, dps):
        over(m).wait_send()


def finish(part, g, g_line, lanes, cores, busy):
    dps, fss = g.shape[:2]
    tokens, model = part.shape[2:]
    dma = pltpu.SemaphoreType.DMA
    hops = (2, max(lanes - 1, 1))
    ways = (max(cores - 1, 1), lanes)
    whole = pl.BlockSpec(memory_space=pltpu.VMEM)
    return pl.pallas_call(
        functools.partial(finish_kernel, dps, lanes, cores, busy),
        in_specs=[whole, whole, whole],
        out_specs=[whole, ANY, whole],
        out_shape=[
            jax.ShapeDtypeStruct((tokens, model), F32),
            jax.ShapeDtypeStruct((busy,) + g.shape[2:], BF),
            jax.ShapeDtypeStruct(g_line.shape[1:], F32),
        ],
        scratch_shapes=[
            pltpu.VMEM(ways + (tokens, model), BF),
            pltpu.VMEM(hops + (tokens, model), BF),
            pltpu.VMEM(hops + (tokens, model), BF),
            pltpu.VMEM((dps - 1,) + g.shape[1:], BF),
            pltpu.VMEM(g.shape[1:], BF),
            pltpu.VMEM((max(lanes - 1, 1),) + g_line.shape[1:], BF),
            dma(hops), dma(hops), dma(ways), dma(ways), dma((dps - 1,)), dma((dps - 1,)),
            dma((fss - 1,)), dma((fss - 1,)), dma, dma((max(lanes - 1, 1),)), dma((max(lanes - 1, 1),)),
        ],
        cost_estimate=lasts(66),
        compiler_params=pltpu.CompilerParams(
            collective_id=6, has_side_effects=True, vmem_limit_bytes=VMEM_LIMIT
        ),
    )(part, g, g_line)


def per_device(x, w_qkv, w_out, w_shared, w_experts, gains, routes, gates, d_out):
    tokens, model = x.shape
    hidden = w_shared.shape[1] // 3
    experts, shard = w_experts.shape[:2]
    dps, fss = lax.axis_size("dp"), lax.axis_size("fsdp")
    cores = dps * fss // experts
    lanes = fss // cores
    seq = tokens * fss
    slots = tokens // 2
    per = -(-HEADS // fss)
    busy = -(-HEADS // per)
    width = per * HD
    dp, fs = lax.axis_index("dp"), lax.axis_index("fsdp")
    z, c = fs // cores, fs % cores

    def over_z(value, pairs):
        return lax.ppermute(
            value, "fsdp", [(a * cores + k, b * cores + k) for a, b in pairs for k in range(cores)]
        )

    def over_core(value, m):
        return lax.ppermute(
            value, "fsdp", [(a * cores + k, a * cores + (k ^ m)) for a in range(lanes) for k in range(cores)]
        )

    def over_dp(value, m):
        return lax.ppermute(value, "dp", [(a, (a + m) % dps) for a in range(dps)])

    cut = w_qkv.reshape(shard, 3, HEADS, HD)
    cut = jnp.pad(cut, ((0, 0), (0, 0), (0, fss * per - HEADS), (0, 0)))
    cut = cut.reshape(shard, 3, fss, width).transpose(2, 0, 1, 3).reshape(fss, shard, 3 * width)
    extra = jnp.broadcast_to(jnp.pad(gains, ((0, 0), (0, HD - 2))), (fss, shard, HD))
    slabs = jnp.concatenate([cut, extra], axis=2)
    topk = routes.shape[1]
    table = jnp.concatenate([routes.T.astype(F32), gates.T], axis=0)
    table = jnp.pad(table, ((0, -2 * topk % 8), (0, 0)))
    x_all, slabs, tables, out_all, picks, weigh, c_slots = start(
        x, slabs, table, w_out, d_out, topk, dps, lanes, cores
    )
    c_slots = c_slots.reshape(-1, model)
    x_all = x_all.reshape(seq, model)
    slabs = slabs.reshape(model, 3 * width + HD)
    out_all = out_all.reshape(model, model)
    w_heads = jnp.where(fs < busy, slabs[:, : 3 * width], 0)
    gain_rows = slabs[:, 3 * width : 3 * width + 2].astype(F32).T
    gain_one, gain_two = gain_rows[0:1], gain_rows[1:2]

    half = HD // 2
    frequency = 10000.0 ** (-jnp.arange(half, dtype=F32) / half)
    angles = jnp.arange(seq, dtype=jnp.int32).astype(F32)[:, None] * frequency[None, :]
    cosine, sine = jnp.cos(angles), jnp.sin(angles)
    cos = jnp.concatenate([cosine, cosine], axis=1)
    sin = jnp.concatenate([-sine, sine], axis=1)

    xn_one, q, k, v, kt, vt = project(x_all, gain_one, w_heads, cos, sin, seq)

    groups = [[e * cores + k for e in range(experts)] for k in range(cores)]

    def swap(value):
        return lax.all_to_all(
            value, ("dp", "fsdp"), split_axis=0, concat_axis=0, tiled=True, axis_index_groups=groups
        )

    rows_here = swap(after(w_experts, x_all)).reshape(dps, lanes, shard, 3 * hidden)

    o, lse = attend(q, k, vt, 256)

    heads = heads_home(o, tokens, lanes, cores, busy)[:, :model]
    middle = x.astype(F32) + dot_nt(heads, out_all)
    inv_two = lax.rsqrt(jnp.mean(middle * middle, axis=1, keepdims=True) + norm_eps)
    unit_two = middle * inv_two
    xn_two = (unit_two * gain_two).astype(BF)

    def reduce_cores(part):
        part = part.reshape(dps, lanes, cores, shard, part.shape[1])
        at = lambda k: lax.dynamic_index_in_dim(part, k, 2, keepdims=False)
        total = at(c)
        for m in range(1, cores):
            total = total + over_core(at(c ^ m).astype(BF), m).astype(F32)
        return total

    x_slots, w_own = dispatch(xn_two, picks, rows_here, lanes, cores, 3)
    x_slots = x_slots.reshape(-1, model)
    w_own = w_own.reshape(model, 3 * hidden)
    dx_slots, gu_slots, hid_slots = expert(x_slots, c_slots, w_own, BF)

    shared_all = lax.all_gather(after(w_shared, heads), ("dp", "fsdp"), axis=0, tiled=True)
    dx_shared, gu_shared, hid_shared = expert(xn_two, d_out, shared_all, F32)
    f_shared = dot_nt(hid_shared, shared_all[:, 2 * hidden :])

    shape = (dps, lanes, slots, model)
    g_own = jnp.concatenate([dot_tn(x_slots, gu_slots), dot_tn(c_slots, hid_slots)], axis=1)
    own = reduce_cores(g_own).astype(BF)
    dx_routed = combine(after(dx_slots, own).reshape(shape), picks, lanes, cores, 4)
    f_slots = dot_nt(hid_slots, w_own[:, 2 * hidden :]).astype(BF)
    dxn_two = dx_shared + dx_routed
    scaled = dxn_two * gain_two
    dx_two = d_out.astype(F32) + inv_two * (
        scaled - unit_two * jnp.mean(scaled * unit_two, axis=1, keepdims=True)
    )
    d_attn = dx_two.astype(BF)

    g_shared_part = jnp.concatenate([dot_tn(xn_two, gu_shared), dot_tn(d_out, hid_shared)], axis=1)
    g_shared_part = g_shared_part.astype(BF).reshape(dps, lanes, cores, shard, 3 * hidden)
    da_all, routed, g_line = turn(d_attn, f_slots.reshape(shape), weigh, g_shared_part, lanes, cores)
    da_all = da_all.reshape(seq, model)
    layer_out = (middle + f_shared + routed).astype(BF)
    out_cols = jnp.pad(out_all, ((0, 0), (0, fss * width - model)))
    out_cols = lax.dynamic_slice_in_dim(out_cols, fs * width, width, 1)
    d_o = dot_nn(da_all, out_cols).astype(BF)
    g_out_part = dot_tn(da_all, o)
    dq, dk, dv = attend_back(q, k, kt, v, o, d_o, lse, cos, sin, 256)
    d_qkv = jnp.concatenate([dq, dk, dv], axis=1)
    dxn_part = dot_nt(d_qkv, w_heads).astype(BF).reshape(lanes, cores, tokens, model)
    g_part = jnp.concatenate([dot_tn(xn_one, d_qkv), g_out_part], axis=1).astype(BF)
    g_part = g_part.reshape(dps, fss, shard, 4 * width)
    dxn_one, g_mix, g_shared = finish(dxn_part, g_part, g_line, lanes, cores, busy)
    inputs = x.astype(F32)
    inv_one = lax.rsqrt(jnp.mean(inputs * inputs, axis=1, keepdims=True) + norm_eps)
    unit_one = inputs * inv_one
    scaled = dxn_one * gain_one
    d_x = dx_two + inv_one * (scaled - unit_one * jnp.mean(scaled * unit_one, axis=1, keepdims=True))

    g_experts = swap(own.reshape(experts, shard, 3 * hidden)).astype(F32)

    g_mix = g_mix.reshape(busy, shard, 4, width).transpose(1, 2, 0, 3).reshape(shard, 4, busy * width)
    g_mix = g_mix[:, :, :model].astype(F32)
    g_qkv = g_mix[:, :3].reshape(shard, 3 * model)
    g_out = g_mix[:, 3]

    one = jnp.sum(w_qkv.astype(F32) * g_qkv, axis=1)
    two = jnp.sum(w_shared[:, : 2 * hidden].astype(F32) * g_shared[:, : 2 * hidden], axis=1)
    two = two + jnp.sum(
        w_experts[:, :, : 2 * hidden].astype(F32) * g_experts[:, :, : 2 * hidden], axis=(0, 2)
    )
    g_gains = jnp.stack([one, two], axis=1) / gains.astype(F32)
    return (layer_out, d_x, g_qkv, g_out, g_shared, g_experts, g_gains)


def solution(mesh):
    rows = P(("dp", "fsdp"), None)
    cube = P(None, ("dp", "fsdp"), None)
    return jax.shard_map(
        per_device,
        mesh=mesh,
        in_specs=(rows, rows, rows, rows, cube, rows, rows, rows, rows),
        out_specs=(rows, rows, rows, rows, rows, cube, rows),
        check_vma=False,
    )
```

```python
import functools
import math

import jax
import jax.numpy as jnp
from jax import lax
from jax.experimental import pallas as pl
from jax.experimental.pallas import tpu as pltpu
from jax.sharding import PartitionSpec as P

HEADS = 10
HD = 128
norm_eps = 1e-06
masked_score = -1000000000.0
BF = jnp.bfloat16
F32 = jnp.float32
VMEM_LIMIT = 60 * 2**20


def dot_nn(a, b):
    return lax.dot_general(a, b, (((1,), (0,)), ((), ())), preferred_element_type=F32)


def dot_nt(a, b):
    return lax.dot_general(a, b, (((1,), (1,)), ((), ())), preferred_element_type=F32)


def dot_tn(a, b):
    return lax.dot_general(a, b, (((0,), (0,)), ((), ())), preferred_element_type=F32)


def lasts(us):
    return pl.CostEstimate(flops=0, bytes_accessed=int(us * 3.6e6), transcendentals=0)


def after(value, *marks):
    return lax.optimization_barrier((value,) + marks)[0]


def put(buffer, value, *index):
    rest = buffer.ndim - len(index)
    starts = tuple(index) + (0,) * rest
    return lax.dynamic_update_slice(
        buffer, value.reshape((1,) * len(index) + buffer.shape[len(index) :]), starts
    )


def take(values, index):
    return lax.dynamic_index_in_dim(values, index, 0, keepdims=False)


def proj_kernel(x_ref, gain_ref, w_ref, cos_ref, sin_ref, xn_ref, q_ref, k_ref, v_ref, kt_ref, vt_ref):
    x = x_ref[...].astype(F32)
    inv = lax.rsqrt(jnp.mean(x * x, axis=1, keepdims=True) + norm_eps)
    xn = (x * inv * gain_ref[...]).astype(BF)
    xn_ref[...] = xn
    width = q_ref.shape[1]
    cos = cos_ref[...]
    sin = sin_ref[...]
    for part in range(3):
        for head in range(width // HD):
            lo = part * width + head * HD
            u = dot_nn(xn, w_ref[:, lo : lo + HD])
            cols = slice(head * HD, (head + 1) * HD)
            if part < 2:
                u = u * cos + pltpu.roll(u, HD // 2, 1) * sin
            low = u.astype(BF)
            if part == 0:
                q_ref[:, cols] = low
            elif part == 1:
                k_ref[:, cols] = low
                kt_ref[cols, :] = u.T.astype(BF)
            else:
                v_ref[:, cols] = low
                vt_ref[cols, :] = u.T.astype(BF)


def project(x_all, gain, w, cos, sin, seq):
    model = x_all.shape[1]
    width = w.shape[1] // 3
    block = 256
    row = lambda cols: pl.BlockSpec((block, cols), lambda i: (i, 0))
    col = pl.BlockSpec((width, block), lambda i: (0, i))
    flat = jax.ShapeDtypeStruct((seq, width), BF)
    turned = jax.ShapeDtypeStruct((width, seq), BF)
    return pl.pallas_call(
        proj_kernel,
        grid=(seq // block,),
        in_specs=[
            row(model),
            pl.BlockSpec((1, model), lambda i: (0, 0)),
            pl.BlockSpec(w.shape, lambda i: (0, 0)),
            row(HD),
            row(HD),
        ],
        out_specs=[row(model), row(width), row(width), row(width), col, col],
        out_shape=[jax.ShapeDtypeStruct((seq, model), BF), flat, flat, flat, turned, turned],
        compiler_params=pltpu.CompilerParams(vmem_limit_bytes=VMEM_LIMIT),
        cost_estimate=lasts(14),
    )(x_all, gain, w, cos, sin)


def causal(rows):
    shape = (rows, rows)
    key = lax.broadcasted_iota(jnp.int32, shape, 0)
    query = lax.broadcasted_iota(jnp.int32, shape, 1)
    return key <= query


def attend_kernel(block, count, scale, q_ref, k_ref, vt_ref, o_ref, lse_ref):
    step = pl.program_id(1)
    for j in range(count):

        @pl.when(step == j)
        def _():
            whole = j * block
            q = q_ref[...]
            tail = dot_nt(k_ref[whole : whole + block, :], q) * scale
            tail = jnp.where(causal(block), tail, masked_score)
            top = jnp.max(tail, axis=0, keepdims=True)
            if j:
                front = dot_nt(k_ref[:whole, :], q) * scale
                top = jnp.maximum(top, jnp.max(front, axis=0, keepdims=True))
            tail = jnp.exp(tail - top)
            total = jnp.sum(tail, axis=0, keepdims=True)
            mixed = dot_nn(vt_ref[:, whole : whole + block], tail.astype(BF))
            if j:
                front = jnp.exp(front - top)
                total = total + jnp.sum(front, axis=0, keepdims=True)
                mixed = mixed + dot_nn(vt_ref[:, :whole], front.astype(BF))
            o_ref[...] = (mixed / total).T.astype(BF)
            lse_ref[0] = top + jnp.log(total)


def attend(q, k, vt, block):
    seq, width = q.shape
    count = seq // block
    heads = width // HD
    scale = 1.0 / math.sqrt(HD)
    return pl.pallas_call(
        functools.partial(attend_kernel, block, count, scale),
        grid=(heads, count),
        in_specs=[
            pl.BlockSpec((block, HD), lambda h, i: (i, h)),
            pl.BlockSpec((seq, HD), lambda h, i: (0, h)),
            pl.BlockSpec((HD, seq), lambda h, i: (h, 0)),
        ],
        out_specs=[
            pl.BlockSpec((block, HD), lambda h, i: (i, h)),
            pl.BlockSpec((1, 1, block), lambda h, i: (h, 0, i)),
        ],
        out_shape=[
            jax.ShapeDtypeStruct((seq, width), BF),
            jax.ShapeDtypeStruct((heads, 1, seq), F32),
        ],
        compiler_params=pltpu.CompilerParams(vmem_limit_bytes=VMEM_LIMIT),
        cost_estimate=lasts(18),
    )(q, k, vt)


def unrotate(g, cos, sin):
    return g * cos - pltpu.roll(g, HD // 2, 1) * sin


def attend_back_kernel(
    block, count, scale,
    q_ref, k_ref, kt_ref, v_ref, o_ref, do_ref, lse_ref, cos_ref, sin_ref,
    dq_ref, dk_ref, dv_ref, dk_acc, dv_acc,
):
    step = pl.program_id(1)

    @pl.when(step == 0)
    def _():
        dk_acc[...] = jnp.zeros_like(dk_acc)
        dv_acc[...] = jnp.zeros_like(dv_acc)

    for j in range(count):

        @pl.when(step == j)
        def _():
            wide = (j + 1) * block
            here = slice(j * block, wide)
            q = q_ref[...]
            do = do_ref[...]
            row = jnp.sum((do.astype(F32) * o_ref[...].astype(F32)).T, axis=0, keepdims=True)
            lse = lse_ref[0]
            parts = [(slice(0, j * block), False)] if j else []
            parts.append((here, True))
            dq = None
            for span, edge in parts:
                p = jnp.exp(dot_nt(k_ref[span, :], q) * scale - lse)
                if edge:
                    p = jnp.where(causal(block), p, 0.0)
                ds = (p * (dot_nt(v_ref[span, :], do) - row)).astype(BF)
                dv_acc[span, :] += dot_nn(p.astype(BF), do)
                dk_acc[span, :] += dot_nn(ds, q)
                term = dot_nn(kt_ref[:, span], ds)
                dq = term if dq is None else dq + term
            dq_ref[...] = unrotate(dq.T * scale, cos_ref[here, :], sin_ref[here, :]).astype(BF)

    @pl.when(step == count - 1)
    def _():
        dk_ref[...] = unrotate(dk_acc[...] * scale, cos_ref[...], sin_ref[...]).astype(BF)
        dv_ref[...] = dv_acc[...].astype(BF)


def attend_back(q, k, kt, v, o, do, lse, cos, sin, block):
    seq, width = q.shape
    count = seq // block
    heads = width // HD
    scale = 1.0 / math.sqrt(HD)
    piece = pl.BlockSpec((block, HD), lambda h, i: (i, h))
    whole = pl.BlockSpec((seq, HD), lambda h, i: (0, h))
    turned = pl.BlockSpec((HD, seq), lambda h, i: (h, 0))
    table = pl.BlockSpec((seq, HD), lambda h, i: (0, 0))
    flat = jax.ShapeDtypeStruct((seq, width), BF)
    return pl.pallas_call(
        functools.partial(attend_back_kernel, block, count, scale),
        grid=(heads, count),
        in_specs=[
            piece, whole, turned, whole, piece, piece,
            pl.BlockSpec((1, 1, block), lambda h, i: (h, 0, i)), table, table,
        ],
        out_specs=[piece, whole, whole],
        out_shape=[flat, flat, flat],
        scratch_shapes=[pltpu.VMEM((seq, HD), F32), pltpu.VMEM((seq, HD), F32)],
        compiler_params=pltpu.CompilerParams(vmem_limit_bytes=VMEM_LIMIT),
        cost_estimate=lasts(25),
    )(q, k, kt, v, o, do, lse, cos, sin)


def feed(x, c, w_ref, hidden):
    gate = dot_nn(x, w_ref[:, :hidden])
    up = dot_nn(x, w_ref[:, hidden : 2 * hidden])
    down = dot_nn(c, w_ref[:, 2 * hidden :])
    sig = 1.0 / (1.0 + jnp.exp(-gate))
    act = gate * sig
    dup = (down * act).astype(BF)
    dgate = (down * up * sig * (1.0 + gate * (1.0 - sig))).astype(BF)
    dx = dot_nt(dgate, w_ref[:, :hidden]) + dot_nt(dup, w_ref[:, hidden : 2 * hidden])
    return dx, dgate, dup, (act * up).astype(BF)


def expert_kernel(hidden, x_ref, c_ref, w_ref, dx_ref, gu_ref, hid_ref):
    dx, dgate, dup, hid = feed(x_ref[...], c_ref[...], w_ref, hidden)
    dx_ref[...] = dx.astype(dx_ref.dtype)
    gu_ref[:, :hidden] = dgate
    gu_ref[:, hidden:] = dup
    hid_ref[...] = hid


def expert(x, c, w, kind):
    rows, model = x.shape
    hidden = w.shape[1] // 3
    block = min(256, rows)
    row = lambda cols: pl.BlockSpec((block, cols), lambda i: (i, 0))
    return pl.pallas_call(
        functools.partial(expert_kernel, hidden),
        grid=(rows // block,),
        in_specs=[row(model), row(model), pl.BlockSpec(w.shape, lambda i: (0, 0))],
        out_specs=[row(model), row(2 * hidden), row(hidden)],
        out_shape=[
            jax.ShapeDtypeStruct((rows, model), kind),
            jax.ShapeDtypeStruct((rows, 2 * hidden), BF),
            jax.ShapeDtypeStruct((rows, hidden), BF),
        ],
        compiler_params=pltpu.CompilerParams(vmem_limit_bytes=VMEM_LIMIT),
        cost_estimate=lasts(0.018 * rows),
    )(x, c, w)


MESH = pl.DeviceIdType.MESH
ANY = pl.BlockSpec(memory_space=pl.ANY)


def place(cores):
    dp, fs = lax.axis_index("dp"), lax.axis_index("fsdp")
    return dp, fs, fs // cores, fs % cores


def greet(peers):
    barrier = pltpu.get_barrier_semaphore()
    for peer in peers:
        pl.semaphore_signal(barrier, inc=1, device_id=peer, device_id_type=MESH)
    pl.semaphore_wait(barrier, len(peers))


def head_slot(f, lanes, cores):
    return lax.rem(f, cores) * lanes + f // cores


def sequence_peers(dp, fs, fss):
    return [(dp, lax.rem(fs + k, fss)) for k in range(1, fss)]


def send(source, target, out, came, peer):
    return pltpu.make_async_remote_copy(
        src_ref=source, dst_ref=target, send_sem=out, recv_sem=came, device_id=peer, device_id_type=MESH
    )


class Chain:
    def __init__(self, own, full, lanes, cores, sems):
        self.own, self.full, self.lanes, self.cores = own, full, lanes, cores
        self.z_out, self.z_in, self.c_out, self.c_in, self.local = sems
        self.dp, self.fs, self.z, self.c = place(cores)

    def hop(self, side, step, block):
        by = self.cores if side == 0 else -self.cores
        source = self.own if step == 0 else self.full.at[block, self.c]
        return send(
            source, self.full.at[block, self.c], self.z_out.at[side, step], self.z_in.at[side, step],
            (self.dp, self.fs + by),
        )

    def across(self, m, block, source, core):
        return send(
            source, self.full.at[block, core], self.c_out.at[m - 1, block], self.c_in.at[m - 1, block],
            (self.dp, self.z * self.cores + lax.rem(self.c + m, self.cores)),
        )

    def keep(self):
        return pltpu.make_async_copy(self.own, self.full.at[self.z, self.c], self.local)

    def has_next(self, side):
        return self.z < self.lanes - 1 if side == 0 else self.z > 0

    def begin(self):
        for side in (0, 1):

            @pl.when(self.has_next(side))
            def _():
                self.hop(side, 0, self.z).start()

        for m in range(1, self.cores):
            self.across(m, self.z, self.own, self.c).start()
        self.keep().start()

    def came(self, side, step):
        block = self.z - step if side == 0 else self.z + step
        return block, (block >= 0) & (block < self.lanes)

    def advance(self, step):
        for side in (0, 1):
            block, there = self.came(side, step)

            @pl.when(there)
            def _():
                self.hop(side, step - 1, block).wait_recv()

            @pl.when(there & self.has_next(side))
            def _():
                self.hop(side, step, block).start()

            @pl.when(there)
            def _():
                for m in range(1, self.cores):
                    self.across(m, block, self.full.at[block, self.c], self.c).start()

    def finish(self):
        self.keep().wait()
        for m in range(1, self.cores):
            for block in range(self.lanes):
                self.across(m, block, self.own, lax.rem(self.c + self.cores - m, self.cores)).wait_recv()
        for side in (0, 1):
            for step in range(self.lanes - 1):
                block, there = self.came(side, step)

                @pl.when(there & self.has_next(side))
                def _():
                    self.hop(side, step, block).wait_send()

        for m in range(1, self.cores):
            for block in range(self.lanes):
                self.across(m, block, self.own, self.c).wait_send()


def chain_sems(lanes, cores):
    dma = pltpu.SemaphoreType.DMA
    hops = (2, max(lanes - 1, 1))
    ways = (max(cores - 1, 1), lanes)
    return [dma(hops), dma(hops), dma(ways), dma(ways), dma]


class Line:
    def __init__(self, own, buffer, lanes, cores, out, came):
        self.own, self.buffer, self.lanes, self.cores = own, buffer, lanes, cores
        self.out, self.into = out, came
        self.dp, self.fs, self.z, self.c = place(cores)

    def has_next(self, side):
        return self.z < self.lanes - 1 if side == 0 else self.z > 0

    def near(self, side):
        return (self.dp, self.fs + (self.cores if side == 0 else -self.cores))

    def hop(self, side, step, block):
        source = self.own if step == 0 else self.buffer.at[block]
        return send(
            source, self.buffer.at[block], self.out.at[side, step], self.into.at[side, step], self.near(side)
        )

    def begin(self):
        for side in (0, 1):

            @pl.when(self.has_next(side))
            def _():
                self.hop(side, 0, self.z).start()

    def came(self, side, step):
        block = self.z - step if side == 0 else self.z + step
        return block, (block >= 0) & (block < self.lanes)

    def advance(self, step, then):
        for side in (0, 1):
            block, there = self.came(side, step)

            @pl.when(there)
            def _():
                self.hop(side, step - 1, block).wait_recv()

            @pl.when(there & self.has_next(side))
            def _():
                self.hop(side, step, block).start()

            @pl.when(there)
            def _():
                then(block, self.buffer.at[block])

    def finish(self):
        for step in range(self.lanes - 1):
            for side in (0, 1):
                block, there = self.came(side, step)

                @pl.when(there & self.has_next(side))
                def _():
                    self.hop(side, step, block).wait_send()


class Spread:
    def __init__(self, stage, target, dps, lanes, cores, out, came, local):
        self.stage, self.target, self.dps, self.lanes = stage, target, dps, lanes
        self.out, self.into, self.local = out, came, local
        self.dp, self.fs, self.z, self.c = place(cores)

    def over(self, m, block):
        return send(
            self.stage.at[m, block], self.target.at[m, block], self.out.at[m - 1, block],
            self.into.at[m - 1, block], (lax.rem(self.dp + m, self.dps), self.fs),
        )

    def keep(self, block):
        return pltpu.make_async_copy(
            self.stage.at[0, block], self.target.at[0, block], self.local.at[block]
        )

    def go(self, m, block):
        if m:
            self.over(m, block).start()
        else:
            self.keep(block).start()

    def order(self):
        return list(range(1, self.dps)) + [0]

    def finish(self):
        for block in range(self.lanes):
            self.keep(block).wait()
            for m in range(1, self.dps):
                self.over(m, block).wait_recv()
        for block in range(self.lanes):
            for m in range(1, self.dps):
                self.over(m, block).wait_send()


class Rows:
    def __init__(self, own, full, dps, lanes, cores, sems):
        self.own, self.full, self.dps, self.lanes, self.cores = own, full, dps, lanes, cores
        self.z_out, self.z_in, self.d_out, self.d_in, self.c_out, self.c_in, self.local = sems
        self.dp, self.fs, self.z, self.c = place(cores)

    def along(self, k):
        t = lax.rem(self.z + k, self.lanes) * self.cores + self.c
        return send(
            self.own, self.full.at[self.dp, self.z, self.c], self.z_out.at[k - 1], self.z_in.at[k - 1],
            (self.dp, t),
        )

    def over(self, m, block):
        piece = self.full.at[block, :, self.c]
        return send(
            piece, piece, self.d_out.at[m - 1], self.d_in.at[m - 1], (lax.rem(self.dp + m, self.dps), self.fs)
        )

    def across(self, m, core):
        piece = self.full.at[:, :, core]
        peer = (self.dp, self.z * self.cores + lax.rem(self.c + m, self.cores))
        return send(piece, piece, self.c_out.at[m - 1], self.c_in.at[m - 1], peer)

    def keep(self):
        return pltpu.make_async_copy(self.own, self.full.at[self.dp, self.z, self.c], self.local)

    def begin(self):
        for k in range(1, self.lanes):
            self.along(k).start()
        self.keep().start()

    def to_dp(self):
        self.keep().wait()
        for k in range(1, self.lanes):
            self.along(k).wait_recv()
        for m in range(1, self.dps):
            self.over(m, self.dp).start()

    def to_cores(self):
        for m in range(1, self.dps):
            self.over(m, lax.rem(self.dp + self.dps - m, self.dps)).wait_recv()
        for m in range(1, self.cores):
            self.across(m, self.c).start()

    def finish(self):
        for m in range(1, self.cores):
            self.across(m, lax.rem(self.c + self.cores - m, self.cores)).wait_recv()
        for k in range(1, self.lanes):
            self.along(k).wait_send()
        for m in range(1, self.dps):
            self.over(m, self.dp).wait_send()
        for m in range(1, self.cores):
            self.across(m, self.c).wait_send()


def pair(n):
    return [pltpu.SemaphoreType.DMA((max(n - 1, 1),)) for _ in range(2)]


def rows_sems(dps, lanes, cores):
    return pair(lanes) + pair(dps) + pair(cores) + [pltpu.SemaphoreType.DMA]


def start_kernel(
    dps, lanes, cores, topk, busy, x_ref, wh_ref, tab_ref, wo_ref,
    full_ref, heads_ref, tabs_ref, out_ref, pick_ref, weigh_ref,
    h_out, h_in, hd_out, hd_in, t_out, t_in, locals_, *sems,
):
    rows = Rows(wo_ref, out_ref, dps, lanes, cores, sems[:7])
    chain = Chain(x_ref, full_ref, lanes, cores, sems[7:])
    dp, fs, z, c = chain.dp, chain.fs, chain.z, chain.c
    fss = lanes * cores
    slots, tokens = pick_ref.shape[2:]
    greet(sequence_peers(dp, fs, fss) + [(lax.rem(dp + m, dps), fs) for m in range(1, dps)])
    chain.begin()
    kept = [
        pltpu.make_async_copy(wh_ref.at[fs], heads_ref.at[dp, fs], locals_.at[0]),
        pltpu.make_async_copy(tab_ref, tabs_ref.at[z], locals_.at[1]),
    ]
    for copy in kept:
        copy.start()

    def heads_to(k):
        t = lax.rem(fs + k, fss)
        return send(wh_ref.at[t], heads_ref.at[dp, fs], h_out.at[k - 1], h_in.at[k - 1], (dp, t))

    def table_to(k):
        t = lax.rem(z + k, lanes) * cores + c
        return send(tab_ref, tabs_ref.at[z], t_out.at[k - 1], t_in.at[k - 1], (dp, t))

    def heads_over(m, block):
        return send(
            heads_ref.at[block], heads_ref.at[block], hd_out.at[m - 1], hd_in.at[m - 1],
            (lax.rem(dp + m, dps), fs),
        )

    mine = head_slot(fs, lanes, cores) < busy
    for k in range(1, fss):

        @pl.when(head_slot(lax.rem(fs + k, fss), lanes, cores) < busy)
        def _():
            heads_to(k).start()

    for k in range(1, lanes):
        table_to(k).start()
    rows.begin()
    for copy in kept:
        copy.wait()
    if lanes > 1:
        chain.advance(1)
    @pl.when(mine)
    def _():
        for k in range(1, fss):
            heads_to(k).wait_recv()
        for m in range(1, dps):
            heads_over(m, dp).start()

    rows.to_dp()
    for step in range(2, lanes):
        chain.advance(step)
    for k in range(1, lanes):
        table_to(k).wait_recv()

    triangle = (
        lax.broadcasted_iota(jnp.int32, (tokens, tokens), 0)
        <= lax.broadcasted_iota(jnp.int32, (tokens, tokens), 1)
    ).astype(BF)
    slot = lax.broadcasted_iota(jnp.int32, (slots, tokens), 0).astype(F32)
    for m in range(dps):
        name = (lax.rem(dp + m, dps) * lanes + z).astype(F32)
        for block in range(lanes):
            hit = tabs_ref[block, :topk, :] == name
            member = jnp.max(jnp.where(hit, 1.0, 0.0), axis=0, keepdims=True)
            gate = jnp.sum(jnp.where(hit, tabs_ref[block, topk : 2 * topk, :], 0.0), axis=0, keepdims=True)
            rank = dot_nn(jnp.broadcast_to(member, (8, tokens)).astype(BF), triangle)[:1] - 1.0
            match = (rank == slot) & (member > 0.5)
            pick_ref[m, block] = jnp.where(match, 1.0, 0.0).astype(BF)
            weigh_ref[m, block] = jnp.where(match, gate, 0.0).astype(BF)

    rows.to_cores()
    chain.finish()
    rows.finish()
    for k in range(1, fss):

        @pl.when(head_slot(lax.rem(fs + k, fss), lanes, cores) < busy)
        def _():
            heads_to(k).wait_send()

    for k in range(1, lanes):
        table_to(k).wait_send()

    @pl.when(mine)
    def _():
        for m in range(1, dps):
            heads_over(m, lax.rem(dp + dps - m, dps)).wait_recv()
            heads_over(m, dp).wait_send()


def start(x, wh, table, w_out, topk, busy, dps, lanes, cores):
    fss = lanes * cores
    tokens = x.shape[0]
    dma = pltpu.SemaphoreType.DMA
    whole = pl.BlockSpec(memory_space=pltpu.VMEM)
    picks = jax.ShapeDtypeStruct((dps, lanes, tokens // 2, tokens), BF)
    shapes = [
        jax.ShapeDtypeStruct((lanes, cores) + x.shape, x.dtype),
        jax.ShapeDtypeStruct((dps,) + wh.shape, wh.dtype),
        jax.ShapeDtypeStruct((lanes,) + table.shape, table.dtype),
        jax.ShapeDtypeStruct((dps, lanes, cores) + w_out.shape, w_out.dtype),
        picks,
        picks,
    ]
    return pl.pallas_call(
        functools.partial(start_kernel, dps, lanes, cores, topk, busy),
        in_specs=[ANY] * 4,
        out_specs=[ANY, ANY, whole, ANY, whole, whole],
        out_shape=shapes,
        scratch_shapes=pair(fss) + pair(dps) + pair(lanes) + [dma((2,))]
        + rows_sems(dps, lanes, cores) + chain_sems(lanes, cores),
        cost_estimate=lasts(70),
        compiler_params=pltpu.CompilerParams(
            collective_id=0, has_side_effects=True, vmem_limit_bytes=VMEM_LIMIT
        ),
    )(x, wh, table, w_out)


def heads_kernel(dps, lanes, cores, busy, o_ref, sh_ref, mix_ref, all_ref, out, came, local, *sems):
    dp, fs, z, c = place(cores)
    fss = lanes * cores
    tokens, width = mix_ref.shape[0], o_ref.shape[1]
    shared = Rows(sh_ref, all_ref, dps, lanes, cores, sems)
    greet(sequence_peers(dp, fs, fss) + [(lax.rem(dp + m, dps), fs) for m in range(1, dps)])

    def columns(f):
        slot = head_slot(f, lanes, cores)
        return mix_ref.at[:, pl.ds(pl.multiple_of(slot * width, HD), width)]

    def rows(f):
        return o_ref.at[pl.ds(pl.multiple_of(f * tokens, tokens), tokens), :]

    def to(k, owner):
        t = lax.rem(fs + k, fss)
        return send(rows(t), columns(owner), out.at[k - 1], came.at[k - 1], (dp, t))

    keep = pltpu.make_async_copy(rows(fs), columns(fs), local)
    shared.begin()

    @pl.when(head_slot(fs, lanes, cores) < busy)
    def _():
        for k in range(1, fss):
            to(k, fs).start()
        keep.start()

    shared.to_dp()
    for k in range(1, fss):
        owner = lax.rem(fs + fss - k, fss)

        @pl.when(head_slot(owner, lanes, cores) < busy)
        def _():
            to(k, owner).wait_recv()

    shared.to_cores()

    @pl.when(head_slot(fs, lanes, cores) < busy)
    def _():
        keep.wait()
        for k in range(1, fss):
            to(k, fs).wait_send()

    shared.finish()


def heads_home(o, w_shared, tokens, dps, lanes, cores, busy):
    fss = lanes * cores
    dma = pltpu.SemaphoreType.DMA
    return pl.pallas_call(
        functools.partial(heads_kernel, dps, lanes, cores, busy),
        in_specs=[ANY, ANY],
        out_specs=[ANY, ANY],
        out_shape=[
            jax.ShapeDtypeStruct((tokens, busy * o.shape[1]), o.dtype),
            jax.ShapeDtypeStruct((dps, lanes, cores) + w_shared.shape, w_shared.dtype),
        ],
        scratch_shapes=[dma((fss - 1,)), dma((fss - 1,)), dma] + rows_sems(dps, lanes, cores),
        cost_estimate=lasts(45),
        compiler_params=pltpu.CompilerParams(collective_id=2, has_side_effects=True),
    )(o, w_shared)


def greet_cross(line, dps, cores=1):
    barrier = pltpu.get_barrier_semaphore()
    for m in range(1, dps):
        peer = (lax.rem(line.dp + m, dps), line.fs)
        pl.semaphore_signal(barrier, inc=1, device_id=peer, device_id_type=MESH)
    for side in (0, 1):

        @pl.when(line.has_next(side))
        def _():
            pl.semaphore_signal(barrier, inc=1, device_id=line.near(side), device_id_type=MESH)

    for m in range(1, cores):
        peer = (line.dp, line.z * cores + lax.rem(line.c + m, cores))
        pl.semaphore_signal(barrier, inc=1, device_id=peer, device_id_type=MESH)
    ends = line.has_next(0).astype(jnp.int32) + line.has_next(1).astype(jnp.int32)
    pl.semaphore_wait(barrier, dps - 1 + cores - 1 + ends)


def dispatch_kernel(
    dps, lanes, cores, topk, x_ref, up_ref, tabs_ref, pick_ref, rows_ref, shared_ref,
    out_ref, c_ref, w_ref, dx_ref, f_ref, g_ref, acts, acc, buffer, stage, up_buffer, up_stage, l_out, l_in, s_out, s_in, s_local,
    ul_out, ul_in, us_out, us_in, us_local, w_out, w_in, w_local,
):
    line = Line(x_ref, buffer, lanes, cores, l_out, l_in)
    spread = Spread(stage, out_ref, dps, lanes, cores, s_out, s_in, s_local)
    up_line = Line(up_ref, up_buffer, lanes, cores, ul_out, ul_in)
    up_spread = Spread(up_stage, c_ref, dps, lanes, cores, us_out, us_in, us_local)
    greet_cross(line, dps, cores)

    def across(m, core):
        peer = (line.dp, line.z * cores + lax.rem(line.c + m, cores))
        return send(rows_ref, w_ref.at[:, :, core], w_out.at[m - 1], w_in.at[m - 1], peer)

    keep = pltpu.make_async_copy(rows_ref, w_ref.at[:, :, line.c], w_local)

    def pick(block, source):
        for m in spread.order():
            stage[m, block] = dot_nn(pick_ref[m, block], source[...]).astype(BF)
            spread.go(m, block)

    def up_pick(block, source):
        for m in up_spread.order():
            name = (lax.rem(line.dp + m, dps) * lanes + line.z).astype(F32)
            hit = tabs_ref[block, :topk, :] == name
            gate = jnp.sum(jnp.where(hit, tabs_ref[block, topk : 2 * topk, :], 0.0), axis=0, keepdims=True)
            one = pick_ref[m, block]
            scale = jnp.sum(one.astype(F32) * gate, axis=1, keepdims=True)
            up_stage[m, block] = (dot_nn(one, source[...]) * scale).astype(BF)
            up_spread.go(m, block)

    line.begin()
    pick(line.z, x_ref)
    up_line.begin()
    up_pick(line.z, up_ref)
    keep.start()
    for m in range(1, cores):
        across(m, line.c).start()
    hidden = shared_ref.shape[1] // 3
    experts, shard = dps * lanes, g_ref.shape[3]

    def shared_forward():
        dx, gate, up, hid = feed(x_ref[...], up_ref[...], shared_ref, hidden)
        dx_ref[...] = dx
        acts[0] = gate
        acts[1] = up
        acts[2] = hid
        f_ref[...] = dot_nt(hid, shared_ref[:, 2 * hidden :])

    def shared_gradient(third):
        acc[...] = dot_tn((x_ref if third < 2 else up_ref)[...], acts[third])
        for e in range(experts):
            for k in range(cores):
                row = (e * cores + k) * shard
                piece = acc[row : row + shard, :].astype(BF)
                g_ref[e // lanes, e % lanes, k, :, third * hidden : (third + 1) * hidden] = piece

    work = [shared_forward] + [functools.partial(shared_gradient, third) for third in range(3)]
    for step in range(1, lanes):
        line.advance(step, pick)
        up_line.advance(step, up_pick)
        work.pop(0)()
    for left in work:
        left()
    spread.finish()
    line.finish()
    up_spread.finish()
    up_line.finish()
    keep.wait()
    for m in range(1, cores):
        across(m, lax.rem(line.c + cores - m, cores)).wait_recv()
        across(m, line.c).wait_send()


def dispatch(x, upstream, tables, picks, rows, shared, topk, lanes, cores):
    dps, _, slots, tokens = picks.shape
    model = x.shape[1]
    dma = pltpu.SemaphoreType.DMA
    hops = (2, max(lanes - 1, 1))
    ways = (dps - 1, lanes)
    whole = pl.BlockSpec(memory_space=pltpu.VMEM)
    buffers = [pltpu.VMEM((lanes, tokens, model), BF), pltpu.VMEM((dps, lanes, slots, model), BF)]
    moves = [dma(hops), dma(hops), dma(ways), dma(ways), dma((lanes,))]
    return pl.pallas_call(
        functools.partial(dispatch_kernel, dps, lanes, cores, topk),
        in_specs=[whole] * 4 + [ANY, whole],
        out_specs=[ANY, ANY, ANY, whole, whole, whole],
        out_shape=[
            jax.ShapeDtypeStruct((dps, lanes, slots, model), BF),
            jax.ShapeDtypeStruct((dps, lanes, slots, model), BF),
            jax.ShapeDtypeStruct((dps, lanes, cores) + rows.shape[2:], BF),
            jax.ShapeDtypeStruct((tokens, model), F32),
            jax.ShapeDtypeStruct((tokens, model), F32),
            jax.ShapeDtypeStruct((dps, lanes, cores) + rows.shape[2:], BF),
        ],
        scratch_shapes=[
            pltpu.VMEM((3, tokens, shared.shape[1] // 3), BF),
            pltpu.VMEM((model, shared.shape[1] // 3), F32),
        ]
        + buffers * 2 + moves * 2 + pair(cores) + [dma],
        cost_estimate=lasts(125),
        compiler_params=pltpu.CompilerParams(
            collective_id=3, has_side_effects=True, vmem_limit_bytes=VMEM_LIMIT
        ),
    )(x, upstream, tables, picks, rows, shared)


class Combine:
    def __init__(self, parts, picks, result, scratch, dps, lanes, cores):
        self.parts, self.picks, self.result = parts, picks, result
        self.back, self.stage, self.inbox = scratch[:3]
        self.z_out, self.z_in, self.d_out, self.d_in, self.local = scratch[3:]
        self.dps, self.lanes, self.cores = dps, lanes, cores
        self.dp, self.fs, self.z, self.c = place(cores)

    def over(self, m, block):
        return send(
            self.parts.at[m, block], self.back.at[block, m], self.d_out.at[m - 1, block],
            self.d_in.at[m - 1, block], (lax.rem(self.dp + self.dps - m, self.dps), self.fs),
        )

    def keep(self, block):
        return pltpu.make_async_copy(
            self.parts.at[0, block], self.back.at[block, 0], self.local.at[block]
        )

    def hop(self, side, step):
        return send(
            self.stage.at[side, step - 1], self.inbox.at[side, step - 1], self.z_out.at[side, step - 1],
            self.z_in.at[side, step - 1],
            (self.dp, self.fs + (self.cores if side == 0 else -self.cores)),
        )

    def goal(self, side, step):
        block = self.z + self.lanes - step if side == 0 else self.z - self.lanes + step
        return block, (block >= 0) & (block < self.lanes)

    def fed(self, side):
        return self.z > 0 if side == 0 else self.z < self.lanes - 1

    def send_block(self, block):
        for m in range(1, self.dps):
            self.over(m, block).start()
        self.keep(block).start()

    def begin(self):
        for step in range(1, self.lanes):
            for side in (0, 1):
                block, there = self.goal(side, step)

                @pl.when(there)
                def _():
                    self.send_block(block)

        self.send_block(self.z)

    def partial_sum(self, block):
        self.keep(block).wait()
        total = dot_tn(self.picks[0, block], self.back[block, 0])
        for m in range(1, self.dps):
            self.over(m, block).wait_recv()
            total = total + dot_tn(self.picks[m, block], self.back[block, m])
        return total

    def advance(self, step):
        for side in (0, 1):
            block, there = self.goal(side, step)

            @pl.when(there)
            def _():
                total = self.partial_sum(block)
                self.stage[side, step - 1] = total.astype(BF)
                if step > 1:

                    @pl.when(self.fed(side))
                    def _():
                        self.hop(side, step - 1).wait_recv()
                        more = self.inbox[side, step - 2].astype(F32)
                        self.stage[side, step - 1] = (total + more).astype(BF)

                self.hop(side, step).start()

    def finish(self):
        self.result[...] = self.partial_sum(self.z)
        for side in (0, 1):

            @pl.when(self.fed(side))
            def _():
                self.hop(side, self.lanes - 1).wait_recv()
                self.result[...] += self.inbox[side, self.lanes - 2].astype(F32)

        for step in range(1, self.lanes):
            for side in (0, 1):
                block, there = self.goal(side, step)

                @pl.when(there)
                def _():
                    self.hop(side, step).wait_send()

        for block in range(self.lanes):
            for m in range(1, self.dps):
                self.over(m, block).wait_send()


def combine_scratch(dps, lanes, slots, tokens, model):
    dma = pltpu.SemaphoreType.DMA
    hops = (2, max(lanes - 1, 1))
    ways = (dps - 1, lanes)
    return [
        pltpu.VMEM((lanes, dps, slots, model), BF),
        pltpu.VMEM(hops + (tokens, model), BF),
        pltpu.VMEM(hops + (tokens, model), BF),
        dma(hops), dma(hops), dma(ways), dma(ways), dma((lanes,)),
    ]


class SharedSum:
    def __init__(self, source, total, scratch, dps, lanes, cores):
        self.source, self.total = source, total
        self.own, self.from_core, self.from_dp = scratch[:3]
        self.c_out, self.c_in, self.d_out, self.d_in, self.local = scratch[3:]
        self.dps, self.lanes, self.cores = dps, lanes, cores
        self.dp, self.fs, self.z, self.c = place(cores)

    def across(self, m):
        t = lax.rem(self.c + m, self.cores)
        return send(
            self.source.at[:, :, t], self.from_core.at[m - 1], self.c_out.at[m - 1], self.c_in.at[m - 1],
            (self.dp, self.z * self.cores + t),
        )

    def over(self, m):
        t = lax.rem(self.dp + m, self.dps)
        return send(
            self.own.at[t], self.from_dp.at[m - 1], self.d_out.at[m - 1], self.d_in.at[m - 1], (t, self.fs)
        )

    def keep(self):
        return pltpu.make_async_copy(self.source.at[:, :, self.c], self.own, self.local)

    def begin(self):
        self.keep().start()
        for m in range(1, self.cores):
            self.across(m).start()

    def add_cores(self):
        self.keep().wait()
        for m in range(1, self.cores):
            self.across(m).wait_recv()

        def add(i, carry):
            p, q = i // self.lanes, lax.rem(i, self.lanes)
            total = self.own[p, q].astype(F32)
            for m in range(1, self.cores):
                total = total + self.from_core[m - 1, p, q].astype(F32)
            self.own[p, q] = total.astype(BF)
            return carry

        lax.fori_loop(0, self.dps * self.lanes, add, 0)
        for m in range(1, self.dps):
            self.over(m).start()

    def add_dp(self):
        for m in range(1, self.dps):
            self.over(m).wait_recv()
        for q in range(self.lanes):
            total = self.own[self.dp, q].astype(F32)
            for m in range(1, self.dps):
                total = total + self.from_dp[m - 1, q].astype(F32)
            self.total[q] = total.astype(BF)
        for m in range(1, self.cores):
            self.across(m).wait_send()
        for m in range(1, self.dps):
            self.over(m).wait_send()


def shared_scratch(g, dps, lanes, cores):
    return [
        pltpu.VMEM((dps, lanes) + g.shape[3:], BF),
        pltpu.VMEM((max(cores - 1, 1), dps, lanes) + g.shape[3:], BF),
        pltpu.VMEM((dps - 1, lanes) + g.shape[3:], BF),
    ] + pair(cores) + pair(dps) + [pltpu.SemaphoreType.DMA]


def combine_kernel(
    dps, lanes, cores, part_ref, pick_ref, hid_ref, w_ref, out_ref, f_ref, hid, down, load, *scratch
):
    work = Combine(part_ref, pick_ref, out_ref, scratch, dps, lanes, cores)
    hidden = hid.shape[1]
    slots = f_ref.shape[2]
    loads = [
        pltpu.make_async_copy(hid_ref, hid, load.at[0]),
        pltpu.make_async_copy(w_ref.at[:, 2 * hidden :], down, load.at[1]),
    ]
    for copy in loads:
        copy.start()
    greet_cross(Line(None, None, lanes, cores, None, None), dps)
    work.begin()
    for copy in loads:
        copy.wait()

    def forward(m):
        for block in range(lanes):
            row = (m * lanes + block) * slots
            f_ref[m, block] = dot_nt(hid[row : row + slots, :], down[...]).astype(BF)

    per = -(-dps // max(lanes - 1, 1))
    for step in range(1, max(lanes, 2)):
        for m in range((step - 1) * per, min(step * per, dps)):
            forward(m)
        if step < lanes:
            work.advance(step)
    work.finish()


def combine(parts, picks, hid, w, lanes, cores):
    dps, _, slots, model = parts.shape
    tokens = picks.shape[3]
    hidden = hid.shape[1]
    dma = pltpu.SemaphoreType.DMA
    whole = pl.BlockSpec(memory_space=pltpu.VMEM)
    return pl.pallas_call(
        functools.partial(combine_kernel, dps, lanes, cores),
        in_specs=[ANY, whole, ANY, ANY],
        out_specs=[whole, whole],
        out_shape=[
            jax.ShapeDtypeStruct((tokens, model), F32),
            jax.ShapeDtypeStruct(parts.shape, BF),
        ],
        scratch_shapes=[pltpu.VMEM(hid.shape, BF), pltpu.VMEM((model, hidden), BF), dma((2,))]
        + combine_scratch(dps, lanes, slots, tokens, model),
        cost_estimate=lasts(70),
        compiler_params=pltpu.CompilerParams(
            collective_id=4, has_side_effects=True, vmem_limit_bytes=VMEM_LIMIT
        ),
    )(parts, picks, hid, w)


class Gradient:
    def __init__(self, refs, total, scratch, experts, shard, cores):
        self.x, self.c_rows, self.gu, self.hid = refs
        self.total = total
        self.left, self.right, self.acc, self.stage, self.inbox, self.load, self.out, self.came = scratch
        self.experts, self.shard, self.cores = experts, shard, cores
        self.hidden = self.hid.shape[1]
        self.dp, self.fs, self.z, self.c = place(cores)

    def rows_in(self, third):
        source = self.x if third < 2 else self.c_rows
        return pltpu.make_async_copy(source, self.left, self.load.at[0])

    def columns_in(self, third):
        source = self.hid if third == 2 else self.gu.at[:, third * self.hidden : (third + 1) * self.hidden]
        return pltpu.make_async_copy(source, self.right, self.load.at[1])

    def across(self, third, m):
        t = lax.rem(self.c + m, self.cores)
        return send(
            self.stage.at[third, t], self.inbox.at[third, m - 1], self.out.at[third, m - 1],
            self.came.at[third, m - 1], (self.dp, self.z * self.cores + t),
        )

    def begin(self):
        self.rows_in(0).start()
        self.columns_in(0).start()

    def multiply(self, third):
        if third != 1:
            self.rows_in(third).wait()
        self.columns_in(third).wait()
        self.acc[...] = dot_tn(self.left[...], self.right[...])
        if third < 2:
            self.columns_in(third + 1).start()
        if third == 1:
            self.rows_in(2).start()
        for e in range(self.experts):
            for k in range(self.cores):
                row = (e * self.cores + k) * self.shard
                self.stage[third, k, e] = self.acc[row : row + self.shard, :].astype(BF)
        for m in range(1, self.cores):
            self.across(third, m).start()

    def collect(self, third):
        for m in range(1, self.cores):
            self.across(third, m).wait_recv()
        for e in range(self.experts):
            total = self.stage[third, self.c, e].astype(F32)
            for m in range(1, self.cores):
                total = total + self.inbox[third, m - 1, e].astype(F32)
            self.total[e, :, third * self.hidden : (third + 1) * self.hidden] = total.astype(BF)

    def finish(self):
        for third in range(3):
            for m in range(1, self.cores):
                self.across(third, m).wait_send()


def turn_kernel(
    dps, lanes, cores, x_ref, part_ref, pick_ref, xs_ref, cs_ref, gu_ref, hid_ref,
    full_ref, out_ref, g_ref, *scratch,
):
    work = Combine(part_ref, pick_ref, out_ref, scratch[:8], dps, lanes, cores)
    gradient = Gradient(
        (xs_ref, cs_ref, gu_ref, hid_ref), g_ref, scratch[8:16], g_ref.shape[0], g_ref.shape[1], cores
    )
    chain = Chain(x_ref, full_ref, lanes, cores, scratch[16:])
    dp, fs = chain.dp, chain.fs
    fss = lanes * cores
    gradient.begin()
    greet(sequence_peers(dp, fs, fss) + [(lax.rem(dp + m, dps), fs) for m in range(1, dps)])
    chain.begin()
    work.begin()
    gradient.multiply(0)
    for step in range(1, lanes):
        chain.advance(step)
        work.advance(step)
        if step == 1:
            gradient.multiply(1)
    if lanes == 1:
        gradient.multiply(1)
    gradient.multiply(2)
    chain.finish()
    work.finish()
    for third in range(3):
        gradient.collect(third)
    gradient.finish()


def turn(x, parts, picks, slots_in, grads, shard, lanes, cores):
    dps, _, slots, model = parts.shape
    tokens = picks.shape[3]
    xs, cs = slots_in
    gu, hid = grads
    experts = dps * lanes
    hidden = hid.shape[1]
    dma = pltpu.SemaphoreType.DMA
    others = max(cores - 1, 1)
    whole = pl.BlockSpec(memory_space=pltpu.VMEM)
    return pl.pallas_call(
        functools.partial(turn_kernel, dps, lanes, cores),
        in_specs=[ANY, ANY, whole] + [ANY] * 4,
        out_specs=[ANY, whole, whole],
        out_shape=[
            jax.ShapeDtypeStruct((lanes, cores) + x.shape, x.dtype),
            jax.ShapeDtypeStruct((tokens, model), F32),
            jax.ShapeDtypeStruct((experts, shard, 3 * hidden), BF),
        ],
        scratch_shapes=combine_scratch(dps, lanes, slots, tokens, model)
        + [
            pltpu.VMEM(xs.shape, BF),
            pltpu.VMEM(hid.shape, BF),
            pltpu.VMEM((model, hidden), F32),
            pltpu.VMEM((3, cores, experts, shard, hidden), BF),
            pltpu.VMEM((3, others, experts, shard, hidden), BF),
            dma((2,)), dma((3, others)), dma((3, others)),
        ]
        + chain_sems(lanes, cores),
        cost_estimate=lasts(90),
        compiler_params=pltpu.CompilerParams(
            collective_id=1, has_side_effects=True, vmem_limit_bytes=VMEM_LIMIT
        ),
    )(x, parts, picks, xs, cs, gu, hid)


def finish_kernel(
    dps, lanes, cores, busy, part_ref, g_ref, s_ref, out_ref, mix_ref, sum_ref,
    from_core, stage, inbox, from_dp, total_g, from_z, line_sum,
    z_out, z_in, c_out, c_in, g_out, g_in, m_out, m_in, local, s_out, s_in, *scratch,
):
    dp, fs, z, c = place(cores)
    fss = lanes * cores
    shared = SharedSum(s_ref, line_sum, scratch, dps, lanes, cores)
    greet(sequence_peers(dp, fs, fss) + [(lax.rem(dp + m, dps), fs) for m in range(1, dps)])

    def has_next(side):
        return z < lanes - 1 if side == 0 else z > 0

    def over(m):
        t = lax.rem(dp + m, dps)
        return send(g_ref.at[t], from_dp.at[m - 1], g_out.at[m - 1], g_in.at[m - 1], (t, fs))

    def across(m, block):
        t = lax.rem(c + m, cores)
        return send(
            part_ref.at[block, t], from_core.at[m - 1, block], c_out.at[m - 1, block], c_in.at[m - 1, block],
            (dp, z * cores + t),
        )

    def hop(side, step):
        return send(
            stage.at[side, step - 1], inbox.at[side, step - 1], z_out.at[side, step - 1],
            z_in.at[side, step - 1], (dp, fs + (cores if side == 0 else -cores)),
        )

    def home(k, owner):
        t = lax.rem(fs + k, fss)
        return send(total_g.at[t], mix_ref.at[head_slot(owner, lanes, cores)], m_out.at[k - 1], m_in.at[k - 1], (dp, t))

    def along(k):
        t = lax.rem(z + k, lanes)
        return send(
            line_sum.at[t], from_z.at[k - 1], s_out.at[k - 1], s_in.at[k - 1], (dp, t * cores + c)
        )

    def goal(side, step):
        block = z + lanes - step if side == 0 else z - lanes + step
        return block, (block >= 0) & (block < lanes)

    def begin(block):
        for m in range(1, cores):
            across(m, block).start()

    def partial_sum(block):
        total = part_ref[block, c].astype(F32)
        for m in range(1, cores):
            across(m, block).wait_recv()
            total = total + from_core[m - 1, block].astype(F32)
        return total

    def advance(step):
        for side in (0, 1):
            block, there = goal(side, step)
            fed = z > 0 if side == 0 else z < lanes - 1

            @pl.when(there)
            def _():
                total = partial_sum(block)
                stage[side, step - 1] = total.astype(BF)
                if step > 1:

                    @pl.when(fed)
                    def _():
                        hop(side, step - 1).wait_recv()
                        stage[side, step - 1] = (total + inbox[side, step - 2].astype(F32)).astype(BF)

                hop(side, step).start()

    for step in range(1, lanes):
        for side in (0, 1):
            block, there = goal(side, step)

            @pl.when(there)
            def _():
                begin(block)

    begin(z)
    shared.begin()
    for m in range(1, dps):
        over(m).start()
    for step in range(1, max(lanes - 1, 1)):
        advance(step)
        if step == 1:
            shared.add_cores()
    for m in range(1, dps):
        over(m).wait_recv()
    for f in range(fss):
        total = g_ref[dp, f].astype(F32)
        for m in range(1, dps):
            total = total + from_dp[m - 1, f].astype(F32)
        total_g[f] = total.astype(BF)
    keep = pltpu.make_async_copy(total_g.at[fs], mix_ref.at[head_slot(fs, lanes, cores)], local)

    @pl.when(head_slot(fs, lanes, cores) < busy)
    def _():
        for k in range(1, fss):
            home(k, fs).start()
        keep.start()

    if lanes > 1:
        advance(lanes - 1)
    shared.add_dp()
    for k in range(1, lanes):
        along(k).start()
    out_ref[...] = partial_sum(z)
    for side in (0, 1):
        fed = z > 0 if side == 0 else z < lanes - 1

        @pl.when(fed)
        def _():
            hop(side, lanes - 1).wait_recv()
            out_ref[...] += inbox[side, lanes - 2].astype(F32)

    total = line_sum[z].astype(F32)
    for k in range(1, lanes):
        along(k).wait_recv()
        total = total + from_z[k - 1].astype(F32)
    sum_ref[...] = total
    for k in range(1, lanes):
        along(k).wait_send()
    for k in range(1, fss):
        owner = lax.rem(fs + fss - k, fss)

        @pl.when(head_slot(owner, lanes, cores) < busy)
        def _():
            home(k, owner).wait_recv()

    @pl.when(head_slot(fs, lanes, cores) < busy)
    def _():
        keep.wait()
        for k in range(1, fss):
            home(k, fs).wait_send()

    for step in range(1, lanes):
        for side in (0, 1):
            block, there = goal(side, step)

            @pl.when(there)
            def _():
                hop(side, step).wait_send()

    for m in range(1, cores):
        for block in range(lanes):
            across(m, block).wait_send()
    for m in range(1, dps):
        over(m).wait_send()


def finish(part, g, g_shared, lanes, cores, busy):
    dps, fss = g.shape[:2]
    tokens, model = part.shape[2:]
    dma = pltpu.SemaphoreType.DMA
    hops = (2, max(lanes - 1, 1))
    ways = (max(cores - 1, 1), lanes)
    whole = pl.BlockSpec(memory_space=pltpu.VMEM)
    return pl.pallas_call(
        functools.partial(finish_kernel, dps, lanes, cores, busy),
        in_specs=[whole, whole, ANY],
        out_specs=[whole, ANY, whole],
        out_shape=[
            jax.ShapeDtypeStruct((tokens, model), F32),
            jax.ShapeDtypeStruct((busy,) + g.shape[2:], BF),
            jax.ShapeDtypeStruct(g_shared.shape[3:], F32),
        ],
        scratch_shapes=[
            pltpu.VMEM(ways + (tokens, model), BF),
            pltpu.VMEM(hops + (tokens, model), BF),
            pltpu.VMEM(hops + (tokens, model), BF),
            pltpu.VMEM((dps - 1,) + g.shape[1:], BF),
            pltpu.VMEM(g.shape[1:], BF),
            pltpu.VMEM((max(lanes - 1, 1),) + g_shared.shape[3:], BF),
            pltpu.VMEM((lanes,) + g_shared.shape[3:], BF),
            dma(hops), dma(hops), dma(ways), dma(ways), dma((dps - 1,)), dma((dps - 1,)),
            dma((fss - 1,)), dma((fss - 1,)), dma, dma((max(lanes - 1, 1),)), dma((max(lanes - 1, 1),)),
        ]
        + shared_scratch(g_shared, dps, lanes, cores),
        cost_estimate=lasts(66),
        compiler_params=pltpu.CompilerParams(
            collective_id=6, has_side_effects=True, vmem_limit_bytes=VMEM_LIMIT
        ),
    )(part, g, g_shared)


def per_device(x, w_qkv, w_out, w_shared, w_experts, gains, routes, gates, d_out):
    tokens, model = x.shape
    hidden = w_shared.shape[1] // 3
    experts, shard = w_experts.shape[:2]
    dps, fss = lax.axis_size("dp"), lax.axis_size("fsdp")
    cores = dps * fss // experts
    lanes = fss // cores
    seq = tokens * fss
    slots = tokens // 2
    per = -(-HEADS // fss)
    busy = -(-HEADS // per)
    width = per * HD
    dp, fs = lax.axis_index("dp"), lax.axis_index("fsdp")
    z, c = fs // cores, fs % cores

    def over_z(value, pairs):
        return lax.ppermute(
            value, "fsdp", [(a * cores + k, b * cores + k) for a, b in pairs for k in range(cores)]
        )

    cut = w_qkv.reshape(shard, 3, HEADS, HD)
    cut = jnp.pad(cut, ((0, 0), (0, 0), (0, fss * per - HEADS), (0, 0)))
    cut = cut.reshape(shard, 3, cores, lanes, width).transpose(3, 2, 0, 1, 4).reshape(fss, shard, 3 * width)
    w_out_gains = jnp.concatenate([w_out, jnp.pad(gains, ((0, 0), (0, HD - 2)))], axis=1)
    topk = routes.shape[1]
    table = jnp.concatenate([routes.T.astype(F32), gates.T], axis=0)
    table = jnp.pad(table, ((0, -2 * topk % 8), (0, 0)))
    x_all, slabs, tables, out_all, picks, weigh = start(
        x, cut, table, w_out_gains, topk, busy, dps, lanes, cores
    )
    x_all = x_all.reshape(seq, model)
    slabs = slabs.reshape(model, 3 * width)
    out_all = out_all.reshape(model, model + HD)
    gain_rows = out_all[:, model : model + 2].astype(F32).T
    out_all = out_all[:, :model]
    slot = c * lanes + z
    w_heads = jnp.where(slot < busy, slabs, 0)
    gain_one, gain_two = gain_rows[0:1], gain_rows[1:2]

    half = HD // 2
    frequency = 10000.0 ** (-jnp.arange(half, dtype=F32) / half)
    angles = jnp.arange(seq, dtype=jnp.int32).astype(F32)[:, None] * frequency[None, :]
    cosine, sine = jnp.cos(angles), jnp.sin(angles)
    cos = jnp.concatenate([cosine, cosine], axis=1)
    sin = jnp.concatenate([-sine, sine], axis=1)

    xn_one, q, k, v, kt, vt = project(x_all, gain_one, w_heads, cos, sin, seq)

    groups = [[e * cores + k for e in range(experts)] for k in range(cores)]

    def swap(value):
        return lax.all_to_all(
            value, ("dp", "fsdp"), split_axis=0, concat_axis=0, tiled=True, axis_index_groups=groups
        )

    rows_here = swap(after(w_experts, x_all)).reshape(dps, lanes, shard, 3 * hidden)

    o, lse = attend(q, k, vt, 256)

    heads, shared_all = heads_home(o, w_shared, tokens, dps, lanes, cores, busy)
    heads = heads[:, :model]
    shared_all = shared_all.reshape(model, 3 * hidden)
    middle = x.astype(F32) + dot_nt(heads, out_all)
    inv_two = lax.rsqrt(jnp.mean(middle * middle, axis=1, keepdims=True) + norm_eps)
    unit_two = middle * inv_two
    xn_two = (unit_two * gain_two).astype(BF)

    x_slots, c_slots, w_own, dx_shared, f_shared, g_shared_part = dispatch(
        xn_two, d_out, tables, picks, rows_here, shared_all, topk, lanes, cores
    )
    x_slots = x_slots.reshape(-1, model)
    c_slots = c_slots.reshape(-1, model)
    w_own = w_own.reshape(model, 3 * hidden)
    dx_slots, gu_slots, hid_slots = expert(x_slots, c_slots, w_own, BF)

    shape = (dps, lanes, slots, model)
    dx_routed, f_slots = combine(dx_slots.reshape(shape), picks, hid_slots, w_own, lanes, cores)
    dxn_two = dx_shared + dx_routed
    scaled = dxn_two * gain_two
    dx_two = d_out.astype(F32) + inv_two * (
        scaled - unit_two * jnp.mean(scaled * unit_two, axis=1, keepdims=True)
    )
    d_attn = dx_two.astype(BF)

    da_all, routed, g_own = turn(
        d_attn, f_slots, weigh, (x_slots, c_slots), (gu_slots, hid_slots), shard, lanes, cores
    )
    da_all = da_all.reshape(seq, model)
    layer_out = (middle + f_shared + routed).astype(BF)
    out_cols = jnp.pad(out_all, ((0, 0), (0, fss * width - model)))
    out_cols = lax.dynamic_slice_in_dim(out_cols, slot * width, width, 1)
    d_o = dot_nn(da_all, out_cols).astype(BF)
    g_out_part = dot_tn(da_all, o)
    dq, dk, dv = attend_back(q, k, kt, v, o, d_o, lse, cos, sin, 256)
    d_qkv = jnp.concatenate([dq, dk, dv], axis=1)
    dxn_part = dot_nt(d_qkv, w_heads).astype(BF).reshape(lanes, cores, tokens, model)
    g_part = jnp.concatenate([dot_tn(xn_one, d_qkv), g_out_part], axis=1).astype(BF)
    g_part = g_part.reshape(dps, fss, shard, 4 * width)
    dxn_one, g_mix, g_shared = finish(dxn_part, g_part, g_shared_part, lanes, cores, busy)
    inputs = x.astype(F32)
    inv_one = lax.rsqrt(jnp.mean(inputs * inputs, axis=1, keepdims=True) + norm_eps)
    unit_one = inputs * inv_one
    scaled = dxn_one * gain_one
    d_x = dx_two + inv_one * (scaled - unit_one * jnp.mean(scaled * unit_one, axis=1, keepdims=True))

    g_experts = swap(g_own).astype(F32)

    g_mix = g_mix.reshape(busy, shard, 4, width).transpose(1, 2, 0, 3).reshape(shard, 4, busy * width)
    g_mix = g_mix[:, :, :model].astype(F32)
    g_qkv = g_mix[:, :3].reshape(shard, 3 * model)
    g_out = g_mix[:, 3]

    one = jnp.sum(w_qkv.astype(F32) * g_qkv, axis=1)
    two = jnp.sum(w_shared[:, : 2 * hidden].astype(F32) * g_shared[:, : 2 * hidden], axis=1)
    two = two + jnp.sum(
        w_experts[:, :, : 2 * hidden].astype(F32) * g_experts[:, :, : 2 * hidden], axis=(0, 2)
    )
    g_gains = jnp.stack([one, two], axis=1) / gains.astype(F32)
    return (layer_out, d_x, g_qkv, g_out, g_shared, g_experts, g_gains)


def solution(mesh):
    rows = P(("dp", "fsdp"), None)
    cube = P(None, ("dp", "fsdp"), None)
    return jax.shard_map(
        per_device,
        mesh=mesh,
        in_specs=(rows, rows, rows, rows, cube, rows, rows, rows, rows),
        out_specs=(rows, rows, rows, rows, rows, cube, rows),
        check_vma=False,
    )
```

```python
import functools
import math

import jax
import jax.numpy as jnp
import numpy as np
from jax import lax
from jax.experimental import pallas as pl
from jax.experimental.pallas import tpu as pltpu
from jax.sharding import PartitionSpec as P

HEADS = 10
HD = 128
norm_eps = 1e-06
masked_score = -1000000000.0
BF = jnp.bfloat16
F32 = jnp.float32
VMEM_LIMIT = 60 * 2**20


def dot_nn(a, b):
    return lax.dot_general(a, b, (((1,), (0,)), ((), ())), preferred_element_type=F32)


def dot_nt(a, b):
    return lax.dot_general(a, b, (((1,), (1,)), ((), ())), preferred_element_type=F32)


def dot_tn(a, b):
    return lax.dot_general(a, b, (((0,), (0,)), ((), ())), preferred_element_type=F32)


def lasts(us):
    return pl.CostEstimate(flops=0, bytes_accessed=int(us * 3.6e6), transcendentals=0)


def causal(rows):
    shape = (rows, rows)
    key = lax.broadcasted_iota(jnp.int32, shape, 0)
    query = lax.broadcasted_iota(jnp.int32, shape, 1)
    return key <= query


def unrotate(g, cos, sin):
    return g * cos - pltpu.roll(g, HD // 2, 1) * sin


def feed(x, c, w_ref, down_ref, hidden):
    gate = dot_nn(x, w_ref[:, :hidden])
    up = dot_nn(x, w_ref[:, hidden : 2 * hidden])
    down = dot_nn(c, down_ref[...])
    sig = 1.0 / (1.0 + jnp.exp(-gate))
    act = gate * sig
    dup = (down * act).astype(BF)
    dgate = (down * up * sig * (1.0 + gate * (1.0 - sig))).astype(BF)
    dx = dot_nt(dgate, w_ref[:, :hidden]) + dot_nt(dup, w_ref[:, hidden : 2 * hidden])
    return dx, dgate, dup, (act * up).astype(BF)


def expert_kernel(hidden, x_ref, c_ref, w_ref, down_ref, dx_ref, gu_ref, hid_ref):
    dx, dgate, dup, hid = feed(x_ref[...], c_ref[...], w_ref, down_ref, hidden)
    dx_ref[...] = dx.astype(dx_ref.dtype)
    gu_ref[:, :hidden] = dgate
    gu_ref[:, hidden:] = dup
    hid_ref[...] = hid


def expert(x, c, w, down, kind):
    rows, model = x.shape
    hidden = down.shape[1]
    block = min(512, rows)
    row = lambda cols: pl.BlockSpec((block, cols), lambda i: (i, 0))
    return pl.pallas_call(
        functools.partial(expert_kernel, hidden),
        grid=(rows // block,),
        in_specs=[
            row(model),
            row(model),
            pl.BlockSpec(w.shape, lambda i: (0, 0)),
            pl.BlockSpec(down.shape, lambda i: (0, 0)),
        ],
        out_specs=[row(model), row(2 * hidden), row(hidden)],
        out_shape=[
            jax.ShapeDtypeStruct((rows, model), kind),
            jax.ShapeDtypeStruct((rows, 2 * hidden), BF),
            jax.ShapeDtypeStruct((rows, hidden), BF),
        ],
        compiler_params=pltpu.CompilerParams(vmem_limit_bytes=VMEM_LIMIT),
        cost_estimate=lasts(0.018 * rows),
    )(x, c, w, down)


MESH = pl.DeviceIdType.MESH
ANY = pl.BlockSpec(memory_space=pl.ANY)


def place(cores):
    dp, fs = lax.axis_index("dp"), lax.axis_index("fsdp")
    return dp, fs, fs // cores, fs % cores


def greet(peers):
    barrier = pltpu.get_barrier_semaphore()
    for peer in peers:
        pl.semaphore_signal(barrier, inc=1, device_id=peer, device_id_type=MESH)
    pl.semaphore_wait(barrier, len(peers))


def head_slot(f, lanes, cores):
    return lax.rem(f, cores) * lanes + f // cores


def sequence_peers(dp, fs, fss):
    return [(dp, lax.rem(fs + k, fss)) for k in range(1, fss)]


def send(source, target, out, came, peer):
    return pltpu.make_async_remote_copy(
        src_ref=source, dst_ref=target, send_sem=out, recv_sem=came, device_id=peer, device_id_type=MESH
    )


class Chain:
    def __init__(self, own, full, lanes, cores, sems):
        self.own, self.full, self.lanes, self.cores = own, full, lanes, cores
        self.z_out, self.z_in, self.c_out, self.c_in, self.local = sems
        self.dp, self.fs, self.z, self.c = place(cores)

    def hop(self, side, step, block):
        by = self.cores if side == 0 else -self.cores
        source = self.own if step == 0 else self.full.at[block, self.c]
        return send(
            source, self.full.at[block, self.c], self.z_out.at[side, step], self.z_in.at[side, step],
            (self.dp, self.fs + by),
        )

    def across(self, m, block, source, core):
        return send(
            source, self.full.at[block, core], self.c_out.at[m - 1, block], self.c_in.at[m - 1, block],
            (self.dp, self.z * self.cores + lax.rem(self.c + m, self.cores)),
        )

    def keep(self):
        return pltpu.make_async_copy(self.own, self.full.at[self.z, self.c], self.local)

    def has_next(self, side):
        return self.z < self.lanes - 1 if side == 0 else self.z > 0

    def begin(self):
        for side in (0, 1):

            @pl.when(self.has_next(side))
            def _():
                self.hop(side, 0, self.z).start()

        for m in range(1, self.cores):
            self.across(m, self.z, self.own, self.c).start()
        self.keep().start()

    def came(self, side, step):
        block = self.z - step if side == 0 else self.z + step
        return block, (block >= 0) & (block < self.lanes)

    def advance(self, step):
        for side in (0, 1):
            block, there = self.came(side, step)

            @pl.when(there)
            def _():
                self.hop(side, step - 1, block).wait_recv()

            @pl.when(there & self.has_next(side))
            def _():
                self.hop(side, step, block).start()

            @pl.when(there)
            def _():
                for m in range(1, self.cores):
                    self.across(m, block, self.full.at[block, self.c], self.c).start()

    def finish(self):
        self.keep().wait()
        for m in range(1, self.cores):
            for block in range(self.lanes):
                self.across(m, block, self.own, lax.rem(self.c + self.cores - m, self.cores)).wait_recv()
        for side in (0, 1):
            for step in range(self.lanes - 1):
                block, there = self.came(side, step)

                @pl.when(there & self.has_next(side))
                def _():
                    self.hop(side, step, block).wait_send()

        for m in range(1, self.cores):
            for block in range(self.lanes):
                self.across(m, block, self.own, self.c).wait_send()


def chain_sems(lanes, cores):
    dma = pltpu.SemaphoreType.DMA
    hops = (2, max(lanes - 1, 1))
    ways = (max(cores - 1, 1), lanes)
    return [dma(hops), dma(hops), dma(ways), dma(ways), dma]


class Line:
    def __init__(self, own, buffer, lanes, cores, out, came):
        self.own, self.buffer, self.lanes, self.cores = own, buffer, lanes, cores
        self.out, self.into = out, came
        self.dp, self.fs, self.z, self.c = place(cores)

    def has_next(self, side):
        return self.z < self.lanes - 1 if side == 0 else self.z > 0

    def near(self, side):
        return (self.dp, self.fs + (self.cores if side == 0 else -self.cores))

    def hop(self, side, step, block):
        source = self.own if step == 0 else self.buffer.at[block]
        return send(
            source, self.buffer.at[block], self.out.at[side, step], self.into.at[side, step], self.near(side)
        )

    def begin(self):
        for side in (0, 1):

            @pl.when(self.has_next(side))
            def _():
                self.hop(side, 0, self.z).start()

    def came(self, side, step):
        block = self.z - step if side == 0 else self.z + step
        return block, (block >= 0) & (block < self.lanes)

    def advance(self, step, then):
        for side in (0, 1):
            block, there = self.came(side, step)

            @pl.when(there)
            def _():
                self.hop(side, step - 1, block).wait_recv()

            @pl.when(there & self.has_next(side))
            def _():
                self.hop(side, step, block).start()

            @pl.when(there)
            def _():
                then(block, self.buffer.at[block])

    def finish(self):
        for step in range(self.lanes - 1):
            for side in (0, 1):
                block, there = self.came(side, step)

                @pl.when(there & self.has_next(side))
                def _():
                    self.hop(side, step, block).wait_send()


class Spread:
    def __init__(self, stage, target, dps, lanes, cores, out, came, local):
        self.stage, self.target, self.dps, self.lanes = stage, target, dps, lanes
        self.out, self.into, self.local = out, came, local
        self.dp, self.fs, self.z, self.c = place(cores)

    def over(self, m, block):
        return send(
            self.stage.at[m, block], self.target.at[m, block], self.out.at[m - 1, block],
            self.into.at[m - 1, block], (lax.rem(self.dp + m, self.dps), self.fs),
        )

    def keep(self, block):
        return pltpu.make_async_copy(
            self.stage.at[0, block], self.target.at[0, block], self.local.at[block]
        )

    def go(self, m, block):
        if m:
            self.over(m, block).start()
        else:
            self.keep(block).start()

    def order(self):
        return list(range(1, self.dps)) + [0]

    def finish(self):
        for block in range(self.lanes):
            self.keep(block).wait()
            for m in range(1, self.dps):
                self.over(m, block).wait_recv()
        for block in range(self.lanes):
            for m in range(1, self.dps):
                self.over(m, block).wait_send()


class Rows:
    def __init__(self, own, full, dps, lanes, cores, sems):
        self.own, self.full, self.dps, self.lanes, self.cores = own, full, dps, lanes, cores
        self.z_out, self.z_in, self.d_out, self.d_in, self.c_out, self.c_in, self.local = sems
        self.dp, self.fs, self.z, self.c = place(cores)

    def along(self, k):
        t = lax.rem(self.z + k, self.lanes) * self.cores + self.c
        return send(
            self.own, self.full.at[self.dp, self.z, self.c], self.z_out.at[k - 1], self.z_in.at[k - 1],
            (self.dp, t),
        )

    def over(self, m, block):
        piece = self.full.at[block, :, self.c]
        return send(
            piece, piece, self.d_out.at[m - 1], self.d_in.at[m - 1], (lax.rem(self.dp + m, self.dps), self.fs)
        )

    def across(self, m, core):
        piece = self.full.at[:, :, core]
        peer = (self.dp, self.z * self.cores + lax.rem(self.c + m, self.cores))
        return send(piece, piece, self.c_out.at[m - 1], self.c_in.at[m - 1], peer)

    def keep(self):
        return pltpu.make_async_copy(self.own, self.full.at[self.dp, self.z, self.c], self.local)

    def begin(self):
        for k in range(1, self.lanes):
            self.along(k).start()
        self.keep().start()

    def to_dp(self):
        self.keep().wait()
        for k in range(1, self.lanes):
            self.along(k).wait_recv()
        for m in range(1, self.dps):
            self.over(m, self.dp).start()

    def to_cores(self):
        for m in range(1, self.dps):
            self.over(m, lax.rem(self.dp + self.dps - m, self.dps)).wait_recv()
        for m in range(1, self.cores):
            self.across(m, self.c).start()

    def finish(self):
        for m in range(1, self.cores):
            self.across(m, lax.rem(self.c + self.cores - m, self.cores)).wait_recv()
        for k in range(1, self.lanes):
            self.along(k).wait_send()
        for m in range(1, self.dps):
            self.over(m, self.dp).wait_send()
        for m in range(1, self.cores):
            self.across(m, self.c).wait_send()


def pair(n):
    return [pltpu.SemaphoreType.DMA((max(n - 1, 1),)) for _ in range(2)]


def rows_sems(dps, lanes, cores):
    return pair(lanes) + pair(dps) + pair(cores) + [pltpu.SemaphoreType.DMA]


def start_kernel(
    dps, lanes, cores, topk, busy, x_ref, wh_ref, tab_ref, wo_ref, gn_ref,
    full_ref, heads_ref, tabs_ref, out_ref, gains_ref, pick_ref, weigh_ref,
    h_out, h_in, hd_out, hd_in, t_out, t_in, locals_, *sems,
):
    rows = Rows(wo_ref, out_ref, dps, lanes, cores, sems[:7])
    gains = Rows(gn_ref, gains_ref, dps, lanes, cores, sems[7:14])
    chain = Chain(x_ref, full_ref, lanes, cores, sems[14:])
    dp, fs, z, c = chain.dp, chain.fs, chain.z, chain.c
    fss = lanes * cores
    slots, tokens = pick_ref.shape[2:]
    greet(sequence_peers(dp, fs, fss) + [(lax.rem(dp + m, dps), fs) for m in range(1, dps)])
    chain.begin()
    kept = [
        pltpu.make_async_copy(wh_ref.at[fs], heads_ref.at[dp, fs], locals_.at[0]),
        pltpu.make_async_copy(tab_ref, tabs_ref.at[z], locals_.at[1]),
    ]
    for copy in kept:
        copy.start()

    def heads_to(k):
        t = lax.rem(fs + k, fss)
        return send(wh_ref.at[t], heads_ref.at[dp, fs], h_out.at[k - 1], h_in.at[k - 1], (dp, t))

    def table_to(k):
        t = lax.rem(z + k, lanes) * cores + c
        return send(tab_ref, tabs_ref.at[z], t_out.at[k - 1], t_in.at[k - 1], (dp, t))

    def heads_over(m, block):
        return send(
            heads_ref.at[block], heads_ref.at[block], hd_out.at[m - 1], hd_in.at[m - 1],
            (lax.rem(dp + m, dps), fs),
        )

    mine = head_slot(fs, lanes, cores) < busy
    for k in range(1, fss):

        @pl.when(head_slot(lax.rem(fs + k, fss), lanes, cores) < busy)
        def _():
            heads_to(k).start()

    for k in range(1, lanes):
        table_to(k).start()
    gains.begin()
    rows.begin()
    for copy in kept:
        copy.wait()
    if lanes > 1:
        chain.advance(1)
    @pl.when(mine)
    def _():
        for k in range(1, fss):
            heads_to(k).wait_recv()
        for m in range(1, dps):
            heads_over(m, dp).start()

    gains.to_dp()
    rows.to_dp()
    for step in range(2, lanes):
        chain.advance(step)
    for k in range(1, lanes):
        table_to(k).wait_recv()

    triangle = (
        lax.broadcasted_iota(jnp.int32, (tokens, tokens), 0)
        <= lax.broadcasted_iota(jnp.int32, (tokens, tokens), 1)
    ).astype(BF)
    slot = lax.broadcasted_iota(jnp.int32, (slots, tokens), 0).astype(F32)
    for m in range(dps):
        name = (lax.rem(dp + m, dps) * lanes + z).astype(F32)
        for block in range(lanes):
            hit = tabs_ref[block, :topk, :] == name
            member = jnp.max(jnp.where(hit, 1.0, 0.0), axis=0, keepdims=True)
            gate = jnp.sum(jnp.where(hit, tabs_ref[block, topk : 2 * topk, :], 0.0), axis=0, keepdims=True)
            rank = dot_nn(jnp.broadcast_to(member, (8, tokens)).astype(BF), triangle)[:1] - 1.0
            match = (rank == slot) & (member > 0.5)
            pick_ref[m, block] = jnp.where(match, 1.0, 0.0).astype(BF)
            weigh_ref[m, block] = jnp.where(match, gate, 0.0).astype(BF)

    gains.to_cores()
    rows.to_cores()
    chain.finish()
    gains.finish()
    rows.finish()
    for k in range(1, fss):

        @pl.when(head_slot(lax.rem(fs + k, fss), lanes, cores) < busy)
        def _():
            heads_to(k).wait_send()

    for k in range(1, lanes):
        table_to(k).wait_send()

    @pl.when(mine)
    def _():
        for m in range(1, dps):
            heads_over(m, lax.rem(dp + dps - m, dps)).wait_recv()
            heads_over(m, dp).wait_send()


def start(x, wh, table, w_out, gains, topk, busy, dps, lanes, cores):
    fss = lanes * cores
    tokens = x.shape[0]
    dma = pltpu.SemaphoreType.DMA
    whole = pl.BlockSpec(memory_space=pltpu.VMEM)
    picks = jax.ShapeDtypeStruct((dps, lanes, tokens // 2, tokens), BF)
    shapes = [
        jax.ShapeDtypeStruct((lanes, cores) + x.shape, x.dtype),
        jax.ShapeDtypeStruct((dps,) + wh.shape, wh.dtype),
        jax.ShapeDtypeStruct((lanes,) + table.shape, table.dtype),
        jax.ShapeDtypeStruct((dps, lanes, cores) + w_out.shape, w_out.dtype),
        jax.ShapeDtypeStruct((dps, lanes, cores) + gains.shape, gains.dtype),
        picks,
        picks,
    ]
    return pl.pallas_call(
        functools.partial(start_kernel, dps, lanes, cores, topk, busy),
        in_specs=[ANY] * 5,
        out_specs=[ANY, ANY, whole, ANY, ANY, whole, whole],
        out_shape=shapes,
        scratch_shapes=pair(fss) + pair(dps) + pair(lanes) + [dma((2,))]
        + rows_sems(dps, lanes, cores) * 2 + chain_sems(lanes, cores),
        cost_estimate=lasts(70),
        compiler_params=pltpu.CompilerParams(
            collective_id=0, has_side_effects=True, vmem_limit_bytes=VMEM_LIMIT
        ),
    )(x, wh, table, w_out, gains)


class Slabs:
    def __init__(self, source, columns, target, dps, lanes, cores, sems):
        self.source, self.columns, self.target = source, columns, target
        self.lanes, self.cores, self.experts = lanes, cores, dps * lanes
        self.out, self.came, self.local = sems
        self.dp, self.fs, self.z, self.c = place(cores)
        self.me = self.dp * lanes + self.z

    def peer(self, k):
        e = lax.rem(self.me + k, self.experts)
        return (e // self.lanes, lax.rem(e, self.lanes) * self.cores + self.c)

    def to(self, k):
        e = lax.rem(self.me + k, self.experts)
        return send(
            self.source.at[e, :, self.columns], self.target.at[self.dp, self.z], self.out.at[k - 1],
            self.came.at[k - 1], self.peer(k),
        )

    def keep(self):
        return pltpu.make_async_copy(
            self.source.at[self.me, :, self.columns], self.target.at[self.dp, self.z], self.local
        )

    def begin(self):
        for k in range(1, self.experts):
            self.to(k).start()
        self.keep().start()

    def arrive(self):
        self.keep().wait()
        for k in range(1, self.experts):
            self.to(k).wait_recv()

    def finish(self):
        for k in range(1, self.experts):
            self.to(k).wait_send()


def slab_sems(experts):
    return pair(experts) + [pltpu.SemaphoreType.DMA]


def layer_peers(slabs):
    others = [
        (slabs.dp, lax.rem(slabs.z + a, slabs.lanes) * slabs.cores + lax.rem(slabs.c + m, slabs.cores))
        for a in range(slabs.lanes)
        for m in range(1, slabs.cores)
    ]
    return [slabs.peer(k) for k in range(1, slabs.experts)] + others


def attend_kernel(
    dps, lanes, cores, busy, block, scale,
    x_ref, gain_ref, w_ref, cos_ref, sin_ref, we_ref, sh_ref,
    xn_ref, q_ref, k_ref, v_ref, kt_ref, vt_ref, o_ref, lse_ref, mix_ref, all_ref, rows_ref, low_ref,
    out, came, local, *sems,
):
    dp, fs, z, c = place(cores)
    fss = lanes * cores
    tokens, width = mix_ref.shape[0], o_ref.shape[1]
    seq = x_ref.shape[0]
    up_width, low_width = rows_ref.shape[3], low_ref.shape[3]
    slabs = Slabs(we_ref, pl.ds(0, up_width), rows_ref, dps, lanes, cores, sems[:3])
    low_slabs = Slabs(we_ref, pl.ds(up_width, low_width), low_ref, dps, lanes, cores, sems[3:6])
    shared = Rows(sh_ref, all_ref, dps, lanes, cores, sems[6:])
    greet(layer_peers(slabs))
    shared.begin()
    slabs.begin()

    def project(i, carry):
        rows = pl.ds(pl.multiple_of(i * block, block), block)
        x = x_ref[rows, :].astype(F32)
        inv = lax.rsqrt(jnp.mean(x * x, axis=1, keepdims=True) + norm_eps)
        xn = (x * inv * gain_ref[...]).astype(BF)
        xn_ref[rows, :] = xn
        cos, sin = cos_ref[rows, :], sin_ref[rows, :]
        for part in range(3):
            wide = dot_nn(xn, w_ref[:, part * width : (part + 1) * width])
            for head in range(width // HD):
                cols = slice(head * HD, (head + 1) * HD)
                u = wide[:, cols]
                if part < 2:
                    u = u * cos + pltpu.roll(u, HD // 2, 1) * sin
                low = u.astype(BF)
                if part == 0:
                    q_ref[rows, cols] = low
                elif part == 1:
                    k_ref[rows, cols] = low
                    kt_ref[cols, rows] = u.T.astype(BF)
                else:
                    v_ref[rows, cols] = low
                    vt_ref[cols, rows] = u.T.astype(BF)
        return carry

    mine = head_slot(fs, lanes, cores) < busy

    @pl.when(mine)
    def _():
        lax.fori_loop(0, seq // block, project, 0)

    shared.to_dp()

    def head_rows(h, carry):
        cols = pl.ds(pl.multiple_of(h * HD, HD), HD)
        for j in range(seq // block):
            whole = j * block
            here = slice(whole, whole + block)
            q = q_ref[here, cols]
            tail = dot_nt(k_ref[here, cols], q) * scale
            tail = jnp.where(causal(block), tail, masked_score)
            top = jnp.max(tail, axis=0, keepdims=True)
            if j:
                front = dot_nt(k_ref[:whole, cols], q) * scale
                top = jnp.maximum(top, jnp.max(front, axis=0, keepdims=True))
            tail = jnp.exp(tail - top)
            total = jnp.sum(tail, axis=0, keepdims=True)
            mixed = dot_nn(vt_ref[cols, here], tail.astype(BF))
            if j:
                front = jnp.exp(front - top)
                total = total + jnp.sum(front, axis=0, keepdims=True)
                mixed = mixed + dot_nn(vt_ref[cols, :whole], front.astype(BF))
            o_ref[here, cols] = (mixed / total).T.astype(BF)
            lse_ref[h, :, here] = top + jnp.log(total)
        return carry

    @pl.when(mine)
    def _():
        lax.fori_loop(0, width // HD, head_rows, 0)

    def columns(f):
        slot = head_slot(f, lanes, cores)
        return mix_ref.at[:, pl.ds(pl.multiple_of(slot * width, HD), width)]

    def rows(f):
        return o_ref.at[pl.ds(pl.multiple_of(f * tokens, tokens), tokens), :]

    def to(k, owner):
        t = lax.rem(fs + k, fss)
        return send(rows(t), columns(owner), out.at[k - 1], came.at[k - 1], (dp, t))

    keep = pltpu.make_async_copy(rows(fs), columns(fs), local)

    @pl.when(head_slot(fs, lanes, cores) < busy)
    def _():
        for k in range(1, fss):
            to(k, fs).start()
        keep.start()

    low_slabs.begin()
    shared.to_cores()
    for k in range(1, fss):
        owner = lax.rem(fs + fss - k, fss)

        @pl.when(head_slot(owner, lanes, cores) < busy)
        def _():
            to(k, owner).wait_recv()

    @pl.when(head_slot(fs, lanes, cores) < busy)
    def _():
        keep.wait()
        for k in range(1, fss):
            to(k, fs).wait_send()

    shared.finish()
    slabs.arrive()
    slabs.finish()
    low_slabs.arrive()
    low_slabs.finish()


def attend(x_all, gain, w, cos, sin, w_experts, w_shared, tokens, busy, dps, lanes, cores):
    seq, model = x_all.shape
    width = w.shape[1] // 3
    experts, shard, thrice = w_experts.shape
    block = seq // 8
    fss = lanes * cores
    dma = pltpu.SemaphoreType.DMA
    whole = pl.BlockSpec(memory_space=pltpu.VMEM)
    flat = jax.ShapeDtypeStruct((seq, width), BF)
    turned = jax.ShapeDtypeStruct((width, seq), BF)
    return pl.pallas_call(
        functools.partial(attend_kernel, dps, lanes, cores, busy, block, 1.0 / math.sqrt(HD)),
        in_specs=[whole] * 5 + [ANY, ANY],
        out_specs=[whole] * 8 + [ANY] * 4,
        out_shape=[
            jax.ShapeDtypeStruct((seq, model), BF),
            flat, flat, flat, turned, turned, flat,
            jax.ShapeDtypeStruct((width // HD, 1, seq), F32),
            jax.ShapeDtypeStruct((tokens, busy * width), BF),
            jax.ShapeDtypeStruct((dps, lanes, cores) + w_shared.shape, BF),
            jax.ShapeDtypeStruct((dps, lanes, shard, thrice // 3 * 2), BF),
            jax.ShapeDtypeStruct((dps, lanes, shard, thrice // 3), BF),
        ],
        scratch_shapes=[dma((fss - 1,)), dma((fss - 1,)), dma]
        + slab_sems(experts) * 2 + rows_sems(dps, lanes, cores),
        cost_estimate=lasts(100),
        compiler_params=pltpu.CompilerParams(
            collective_id=2, has_side_effects=True, vmem_limit_bytes=VMEM_LIMIT
        ),
    )(x_all, gain, w, cos, sin, w_experts, w_shared)


def greet_cross(line, dps, cores=1):
    barrier = pltpu.get_barrier_semaphore()
    for m in range(1, dps):
        peer = (lax.rem(line.dp + m, dps), line.fs)
        pl.semaphore_signal(barrier, inc=1, device_id=peer, device_id_type=MESH)
    for side in (0, 1):

        @pl.when(line.has_next(side))
        def _():
            pl.semaphore_signal(barrier, inc=1, device_id=line.near(side), device_id_type=MESH)

    for m in range(1, cores):
        peer = (line.dp, line.z * cores + lax.rem(line.c + m, cores))
        pl.semaphore_signal(barrier, inc=1, device_id=peer, device_id_type=MESH)
    ends = line.has_next(0).astype(jnp.int32) + line.has_next(1).astype(jnp.int32)
    pl.semaphore_wait(barrier, dps - 1 + cores - 1 + ends)


def dispatch_kernel(
    dps, lanes, cores, topk, x_ref, up_ref, tabs_ref, pick_ref, rows_ref, low_ref, shared_ref,
    out_ref, c_ref, w_ref, wd_ref, dx_ref, f_ref, g_ref, acts, acc, buffer, stage, up_buffer, up_stage, l_out, l_in, s_out, s_in, s_local,
    ul_out, ul_in, us_out, us_in, us_local, w_out, w_in, w_local, wd_out, wd_in, wd_local,
):
    line = Line(x_ref, buffer, lanes, cores, l_out, l_in)
    spread = Spread(stage, out_ref, dps, lanes, cores, s_out, s_in, s_local)
    up_line = Line(up_ref, up_buffer, lanes, cores, ul_out, ul_in)
    up_spread = Spread(up_stage, c_ref, dps, lanes, cores, us_out, us_in, us_local)
    hidden = shared_ref.shape[1] // 3
    greet_cross(line, dps, cores)

    def across(m, core):
        peer = (line.dp, line.z * cores + lax.rem(line.c + m, cores))
        return send(rows_ref, w_ref.at[:, :, core], w_out.at[m - 1], w_in.at[m - 1], peer)

    def across_down(m, core):
        peer = (line.dp, line.z * cores + lax.rem(line.c + m, cores))
        return send(low_ref, wd_ref.at[:, :, core], wd_out.at[m - 1], wd_in.at[m - 1], peer)

    keep = pltpu.make_async_copy(rows_ref, w_ref.at[:, :, line.c], w_local)
    keep_down = pltpu.make_async_copy(low_ref, wd_ref.at[:, :, line.c], wd_local)

    def pick(block, source):
        for m in spread.order():
            stage[m, block] = dot_nn(pick_ref[m, block], source[...]).astype(BF)
            spread.go(m, block)

    def up_pick(block, source):
        for m in up_spread.order():
            name = (lax.rem(line.dp + m, dps) * lanes + line.z).astype(F32)
            hit = tabs_ref[block, :topk, :] == name
            gate = jnp.sum(jnp.where(hit, tabs_ref[block, topk : 2 * topk, :], 0.0), axis=0, keepdims=True)
            one = pick_ref[m, block]
            scale = jnp.sum(one.astype(F32) * gate, axis=1, keepdims=True)
            up_stage[m, block] = (dot_nn(one, source[...]) * scale).astype(BF)
            up_spread.go(m, block)

    line.begin()
    pick(line.z, x_ref)
    up_line.begin()
    up_pick(line.z, up_ref)
    keep.start()
    keep_down.start()
    for m in range(1, cores):
        across(m, line.c).start()
        across_down(m, line.c).start()
    experts, shard = dps * lanes, g_ref.shape[3]

    def shared_forward():
        down_ref = shared_ref.at[:, 2 * hidden :]
        dx, gate, up, hid = feed(x_ref[...], up_ref[...], shared_ref, down_ref, hidden)
        dx_ref[...] = dx
        acts[0] = gate
        acts[1] = up
        acts[2] = hid
        f_ref[...] = dot_nt(hid, down_ref[...])

    def shared_gradient(third):
        acc[...] = dot_tn((x_ref if third < 2 else up_ref)[...], acts[third])
        for e in range(experts):
            for k in range(cores):
                row = (e * cores + k) * shard
                piece = acc[row : row + shard, :].astype(BF)
                g_ref[e // lanes, e % lanes, k, :, third * hidden : (third + 1) * hidden] = piece

    work = [shared_forward] + [functools.partial(shared_gradient, third) for third in range(3)]
    for step in range(1, lanes):
        line.advance(step, pick)
        up_line.advance(step, up_pick)
        work.pop(0)()
    for left in work:
        left()
    spread.finish()
    line.finish()
    up_spread.finish()
    up_line.finish()
    keep.wait()
    keep_down.wait()
    for m in range(1, cores):
        across(m, lax.rem(line.c + cores - m, cores)).wait_recv()
        across(m, line.c).wait_send()
        across_down(m, lax.rem(line.c + cores - m, cores)).wait_recv()
        across_down(m, line.c).wait_send()


def dispatch(x, upstream, tables, picks, rows, low, shared, topk, lanes, cores):
    dps, _, slots, tokens = picks.shape
    model = x.shape[1]
    shard, hidden = low.shape[2:]
    dma = pltpu.SemaphoreType.DMA
    hops = (2, max(lanes - 1, 1))
    ways = (dps - 1, lanes)
    whole = pl.BlockSpec(memory_space=pltpu.VMEM)
    buffers = [pltpu.VMEM((lanes, tokens, model), BF), pltpu.VMEM((dps, lanes, slots, model), BF)]
    moves = [dma(hops), dma(hops), dma(ways), dma(ways), dma((lanes,))]
    return pl.pallas_call(
        functools.partial(dispatch_kernel, dps, lanes, cores, topk),
        in_specs=[whole] * 4 + [ANY, ANY, whole],
        out_specs=[ANY] * 4 + [whole] * 3,
        out_shape=[
            jax.ShapeDtypeStruct((dps, lanes, slots, model), BF),
            jax.ShapeDtypeStruct((dps, lanes, slots, model), BF),
            jax.ShapeDtypeStruct((dps, lanes, cores) + rows.shape[2:], BF),
            jax.ShapeDtypeStruct((dps, lanes, cores, shard, hidden), BF),
            jax.ShapeDtypeStruct((tokens, model), F32),
            jax.ShapeDtypeStruct((tokens, model), F32),
            jax.ShapeDtypeStruct((dps, lanes, cores, shard, 3 * hidden), BF),
        ],
        scratch_shapes=[
            pltpu.VMEM((3, tokens, shared.shape[1] // 3), BF),
            pltpu.VMEM((model, shared.shape[1] // 3), F32),
        ]
        + buffers * 2 + moves * 2 + (pair(cores) + [dma]) * 2,
        cost_estimate=lasts(125),
        compiler_params=pltpu.CompilerParams(
            collective_id=3, has_side_effects=True, vmem_limit_bytes=VMEM_LIMIT
        ),
    )(x, upstream, tables, picks, rows, low, shared)


class Combine:
    def __init__(self, parts, picks, result, scratch, dps, lanes, cores):
        self.parts, self.picks, self.result = parts, picks, result
        self.back, self.stage, self.inbox = scratch[:3]
        self.z_out, self.z_in, self.d_out, self.d_in, self.local = scratch[3:]
        self.dps, self.lanes, self.cores = dps, lanes, cores
        self.dp, self.fs, self.z, self.c = place(cores)

    def over(self, m, block):
        return send(
            self.parts.at[m, block], self.back.at[block, m], self.d_out.at[m - 1, block],
            self.d_in.at[m - 1, block], (lax.rem(self.dp + self.dps - m, self.dps), self.fs),
        )

    def keep(self, block):
        return pltpu.make_async_copy(
            self.parts.at[0, block], self.back.at[block, 0], self.local.at[block]
        )

    def hop(self, side, step):
        return send(
            self.stage.at[side, step - 1], self.inbox.at[side, step - 1], self.z_out.at[side, step - 1],
            self.z_in.at[side, step - 1],
            (self.dp, self.fs + (self.cores if side == 0 else -self.cores)),
        )

    def goal(self, side, step):
        block = self.z + self.lanes - step if side == 0 else self.z - self.lanes + step
        return block, (block >= 0) & (block < self.lanes)

    def fed(self, side):
        return self.z > 0 if side == 0 else self.z < self.lanes - 1

    def send_block(self, block):
        for m in range(1, self.dps):
            self.over(m, block).start()
        self.keep(block).start()

    def begin(self):
        for step in range(1, self.lanes):
            for side in (0, 1):
                block, there = self.goal(side, step)

                @pl.when(there)
                def _():
                    self.send_block(block)

        self.send_block(self.z)

    def partial_sum(self, block):
        self.keep(block).wait()
        total = dot_tn(self.picks[0, block], self.back[block, 0])
        for m in range(1, self.dps):
            self.over(m, block).wait_recv()
            total = total + dot_tn(self.picks[m, block], self.back[block, m])
        return total

    def advance(self, step):
        for side in (0, 1):
            block, there = self.goal(side, step)

            @pl.when(there)
            def _():
                total = self.partial_sum(block)
                self.stage[side, step - 1] = total.astype(BF)
                if step > 1:

                    @pl.when(self.fed(side))
                    def _():
                        self.hop(side, step - 1).wait_recv()
                        more = self.inbox[side, step - 2].astype(F32)
                        self.stage[side, step - 1] = (total + more).astype(BF)

                self.hop(side, step).start()

    def finish(self):
        self.result[...] = self.partial_sum(self.z)
        for side in (0, 1):

            @pl.when(self.fed(side))
            def _():
                self.hop(side, self.lanes - 1).wait_recv()
                self.result[...] += self.inbox[side, self.lanes - 2].astype(F32)

        for step in range(1, self.lanes):
            for side in (0, 1):
                block, there = self.goal(side, step)

                @pl.when(there)
                def _():
                    self.hop(side, step).wait_send()

        for block in range(self.lanes):
            for m in range(1, self.dps):
                self.over(m, block).wait_send()


def combine_scratch(dps, lanes, slots, tokens, model):
    dma = pltpu.SemaphoreType.DMA
    hops = (2, max(lanes - 1, 1))
    ways = (dps - 1, lanes)
    return [
        pltpu.VMEM((lanes, dps, slots, model), BF),
        pltpu.VMEM(hops + (tokens, model), BF),
        pltpu.VMEM(hops + (tokens, model), BF),
        dma(hops), dma(hops), dma(ways), dma(ways), dma((lanes,)),
    ]


def combine_kernel(
    dps, lanes, cores, part_ref, pick_ref, hid_ref, w_ref, out_ref, f_ref, hid, down, load, *scratch
):
    work = Combine(part_ref, pick_ref, out_ref, scratch, dps, lanes, cores)
    hidden = hid.shape[1]
    slots = f_ref.shape[2]
    loads = [
        pltpu.make_async_copy(hid_ref, hid, load.at[0]),
        pltpu.make_async_copy(w_ref, down, load.at[1]),
    ]
    for copy in loads:
        copy.start()
    greet_cross(Line(None, None, lanes, cores, None, None), dps)
    work.begin()
    for copy in loads:
        copy.wait()

    def forward(m):
        for block in range(lanes):
            row = (m * lanes + block) * slots
            f_ref[m, block] = dot_nt(hid[row : row + slots, :], down[...]).astype(BF)

    per = -(-dps // max(lanes - 1, 1))
    for step in range(1, max(lanes, 2)):
        for m in range((step - 1) * per, min(step * per, dps)):
            forward(m)
        if step < lanes:
            work.advance(step)
    work.finish()


def combine(parts, picks, hid, w, lanes, cores):
    dps, _, slots, model = parts.shape
    tokens = picks.shape[3]
    hidden = hid.shape[1]
    dma = pltpu.SemaphoreType.DMA
    whole = pl.BlockSpec(memory_space=pltpu.VMEM)
    return pl.pallas_call(
        functools.partial(combine_kernel, dps, lanes, cores),
        in_specs=[ANY, whole, ANY, ANY],
        out_specs=[whole, whole],
        out_shape=[
            jax.ShapeDtypeStruct((tokens, model), F32),
            jax.ShapeDtypeStruct(parts.shape, BF),
        ],
        scratch_shapes=[pltpu.VMEM(hid.shape, BF), pltpu.VMEM((model, hidden), BF), dma((2,))]
        + combine_scratch(dps, lanes, slots, tokens, model),
        cost_estimate=lasts(70),
        compiler_params=pltpu.CompilerParams(
            collective_id=4, has_side_effects=True, vmem_limit_bytes=VMEM_LIMIT
        ),
    )(parts, picks, hid, w)


class Gradient:
    def __init__(self, refs, total, scratch, experts, shard, cores):
        self.x, self.c_rows, self.gu, self.hid = refs
        self.total = total
        self.left, self.right, self.acc, self.stage, self.inbox, self.load, self.out, self.came = scratch
        self.experts, self.shard, self.cores = experts, shard, cores
        self.hidden = self.hid.shape[1]
        self.dp, self.fs, self.z, self.c = place(cores)

    def rows_in(self, third):
        source = self.x if third < 2 else self.c_rows
        return pltpu.make_async_copy(source, self.left, self.load.at[0])

    def columns_in(self, third):
        source = self.hid if third == 2 else self.gu.at[:, third * self.hidden : (third + 1) * self.hidden]
        return pltpu.make_async_copy(source, self.right, self.load.at[1])

    def across(self, third, m):
        t = lax.rem(self.c + m, self.cores)
        return send(
            self.stage.at[third, t], self.inbox.at[third, m - 1], self.out.at[third, m - 1],
            self.came.at[third, m - 1], (self.dp, self.z * self.cores + t),
        )

    def begin(self):
        self.rows_in(0).start()
        self.columns_in(0).start()

    def multiply(self, third):
        if third != 1:
            self.rows_in(third).wait()
        self.columns_in(third).wait()
        self.acc[...] = dot_tn(self.left[...], self.right[...])
        if third < 2:
            self.columns_in(third + 1).start()
        if third == 1:
            self.rows_in(2).start()
        for e in range(self.experts):
            for k in range(self.cores):
                row = (e * self.cores + k) * self.shard
                self.stage[third, k, e] = self.acc[row : row + self.shard, :].astype(BF)
        for m in range(1, self.cores):
            self.across(third, m).start()

    def collect(self, third):
        for m in range(1, self.cores):
            self.across(third, m).wait_recv()
        for e in range(self.experts):
            total = self.stage[third, self.c, e].astype(F32)
            for m in range(1, self.cores):
                total = total + self.inbox[third, m - 1, e].astype(F32)
            self.total[e, :, third * self.hidden : (third + 1) * self.hidden] = total.astype(BF)

    def finish(self):
        for third in range(3):
            for m in range(1, self.cores):
                self.across(third, m).wait_send()


def turn_kernel(
    dps, lanes, cores, x_ref, part_ref, pick_ref, xs_ref, cs_ref, gu_ref, hid_ref,
    full_ref, out_ref, g_ref, *scratch,
):
    work = Combine(part_ref, pick_ref, out_ref, scratch[:8], dps, lanes, cores)
    gradient = Gradient(
        (xs_ref, cs_ref, gu_ref, hid_ref), g_ref, scratch[8:16], g_ref.shape[0], g_ref.shape[1], cores
    )
    chain = Chain(x_ref, full_ref, lanes, cores, scratch[16:])
    dp, fs = chain.dp, chain.fs
    gradient.begin()
    greet(sequence_peers(dp, fs, lanes * cores) + [(lax.rem(dp + m, dps), fs) for m in range(1, dps)])
    chain.begin()
    work.begin()
    gradient.multiply(0)
    for step in range(1, lanes):
        chain.advance(step)
        work.advance(step)
        if step == 1:
            gradient.multiply(1)
    if lanes == 1:
        gradient.multiply(1)
    gradient.multiply(2)
    chain.finish()
    work.finish()
    for third in range(3):
        gradient.collect(third)
    gradient.finish()


def turn(x, parts, picks, slots_in, grads, shard, lanes, cores):
    dps, _, slots, model = parts.shape
    tokens = picks.shape[3]
    xs, cs = slots_in
    gu, hid = grads
    experts = dps * lanes
    hidden = hid.shape[1]
    dma = pltpu.SemaphoreType.DMA
    others = max(cores - 1, 1)
    whole = pl.BlockSpec(memory_space=pltpu.VMEM)
    return pl.pallas_call(
        functools.partial(turn_kernel, dps, lanes, cores),
        in_specs=[ANY, ANY, whole] + [ANY] * 4,
        out_specs=[ANY, whole, whole],
        out_shape=[
            jax.ShapeDtypeStruct((lanes, cores) + x.shape, x.dtype),
            jax.ShapeDtypeStruct((tokens, model), F32),
            jax.ShapeDtypeStruct((experts, shard, 3 * hidden), BF),
        ],
        scratch_shapes=combine_scratch(dps, lanes, slots, tokens, model)
        + [
            pltpu.VMEM(xs.shape, BF),
            pltpu.VMEM(hid.shape, BF),
            pltpu.VMEM((model, hidden), F32),
            pltpu.VMEM((3, cores, experts, shard, hidden), BF),
            pltpu.VMEM((3, others, experts, shard, hidden), BF),
            dma((2,)), dma((3, others)), dma((3, others)),
        ]
        + chain_sems(lanes, cores),
        cost_estimate=lasts(90),
        compiler_params=pltpu.CompilerParams(
            collective_id=1, has_side_effects=True, vmem_limit_bytes=VMEM_LIMIT
        ),
    )(x, parts, picks, xs, cs, gu, hid)


class LineSum:
    def __init__(self, source, total, scratch, dps, lanes, cores):
        self.source, self.total = source, total
        self.own, self.from_core, self.from_dp = scratch[:3]
        self.c_out, self.c_in, self.d_out, self.d_in, self.local = scratch[3:]
        self.dps, self.lanes, self.cores = dps, lanes, cores
        self.dp, self.fs, self.z, self.c = place(cores)

    def across(self, m):
        t = lax.rem(self.c + m, self.cores)
        return send(
            self.source.at[:, :, t], self.from_core.at[m - 1], self.c_out.at[m - 1], self.c_in.at[m - 1],
            (self.dp, self.z * self.cores + t),
        )

    def over(self, m):
        t = lax.rem(self.dp + m, self.dps)
        return send(
            self.own.at[t], self.from_dp.at[m - 1], self.d_out.at[m - 1], self.d_in.at[m - 1], (t, self.fs)
        )

    def keep(self):
        return pltpu.make_async_copy(self.source.at[:, :, self.c], self.own, self.local)

    def begin(self):
        self.keep().start()
        for m in range(1, self.cores):
            self.across(m).start()

    def add(self):
        self.keep().wait()
        for m in range(1, self.cores):
            self.across(m).wait_recv()

        def add(i, carry):
            p, q = i // self.lanes, lax.rem(i, self.lanes)
            total = self.own[p, q].astype(F32)
            for m in range(1, self.cores):
                total = total + self.from_core[m - 1, p, q].astype(F32)
            self.own[p, q] = total.astype(BF)
            return carry

        lax.fori_loop(0, self.dps * self.lanes, add, 0)
        for m in range(1, self.dps):
            self.over(m).start()

    def add_dp(self):
        for m in range(1, self.dps):
            self.over(m).wait_recv()
        for q in range(self.lanes):
            total = self.own[self.dp, q].astype(F32)
            for m in range(1, self.dps):
                total = total + self.from_dp[m - 1, q].astype(F32)
            self.total[q] = total.astype(BF)
        for m in range(1, self.cores):
            self.across(m).wait_send()
        for m in range(1, self.dps):
            self.over(m).wait_send()


def attend_back_kernel(
    dps, lanes, cores, busy, block, scale,
    da_ref, xn_ref, out_ref, q_ref, k_ref, kt_ref, v_ref, o_ref, lse_ref, cos_ref, sin_ref, w_ref, g_ref,
    part_ref, prod_ref, line_ref, left, d_ref, acc, stage, cols, do_all, dk_acc, dv_acc,
    load, stored, *scratch,
):
    dp, fs, z, c = place(cores)
    shared = LineSum(g_ref, line_ref, scratch, dps, lanes, cores)
    seq, width = q_ref.shape
    tokens = part_ref.shape[2]
    slot = jnp.minimum(head_slot(fs, lanes, cores), busy - 1)
    fetch = pltpu.make_async_copy(
        out_ref.at[:, pl.ds(pl.multiple_of(slot * width, HD), width)], cols, load.at[0]
    )
    fetch.start()
    first, second = [pltpu.make_async_copy(ref, left, load.at[1]) for ref in (da_ref, xn_ref)]
    first.start()
    shard = prod_ref.shape[2]

    def place_rows(lo, hi):
        for p in range(dps):
            for f in range(lanes * cores):
                row = (p * lanes * cores + f) * shard
                prod_ref[p, f, :, lo:hi] = acc[row : row + shard, : hi - lo].astype(BF)

    greet(
        [(lax.rem(dp + m, dps), fs) for m in range(1, dps)]
        + [(dp, z * cores + lax.rem(c + m, cores)) for m in range(1, cores)]
    )
    shared.begin()
    fetch.wait()
    first.wait()

    def upstream(i, carry):
        rows = pl.ds(pl.multiple_of(i * block, block), block)
        do_all[rows, :] = dot_nn(left[rows, :], cols[...]).astype(BF)
        return carry

    mine = head_slot(fs, lanes, cores) < busy

    @pl.when(mine)
    def _():
        lax.fori_loop(0, seq // block, upstream, 0)

    shared.add()

    @pl.when(mine)
    def _():
        acc[:, :width] = dot_tn(left[...], o_ref[...])
        place_rows(3 * width, 4 * width)

    second.start()

    def head_rows(h, carry):
        lane = pl.ds(pl.multiple_of(h * HD, HD), HD)
        k_lane = pl.ds(pl.multiple_of(width + h * HD, HD), HD)
        v_lane = pl.ds(pl.multiple_of(2 * width + h * HD, HD), HD)
        dk_acc[...] = jnp.zeros_like(dk_acc)
        dv_acc[...] = jnp.zeros_like(dv_acc)
        for j in range(seq // block):
            here = slice(j * block, (j + 1) * block)
            q = q_ref[here, lane]
            do = do_all[here, lane]
            row = jnp.sum((do.astype(F32) * o_ref[here, lane].astype(F32)).T, axis=0, keepdims=True)
            lse = lse_ref[h, :, here]
            dq = None
            for span, edge in ([(slice(0, j * block), False)] if j else []) + [(here, True)]:
                p = jnp.exp(dot_nt(k_ref[span, lane], q) * scale - lse)
                if edge:
                    p = jnp.where(causal(block), p, 0.0)
                ds = (p * (dot_nt(v_ref[span, lane], do) - row)).astype(BF)
                dv_acc[span, :] += dot_nn(p.astype(BF), do)
                dk_acc[span, :] += dot_nn(ds, q)
                term = dot_nn(kt_ref[lane, span], ds)
                dq = term if dq is None else dq + term
            d_ref[here, lane] = unrotate(dq.T * scale, cos_ref[here, :], sin_ref[here, :]).astype(BF)
        d_ref[:, k_lane] = unrotate(dk_acc[...] * scale, cos_ref[...], sin_ref[...]).astype(BF)
        d_ref[:, v_lane] = dv_acc[...].astype(BF)
        return carry

    @pl.when(mine)
    def _():
        lax.fori_loop(0, width // HD, head_rows, 0)

    blocks = [(a, b) for a in range(lanes) for b in range(cores)]
    saves = [
        pltpu.make_async_copy(stage.at[n % 2], part_ref.at[a, b], stored.at[n % 2])
        for n, (a, b) in enumerate(blocks)
    ]
    for n in range(len(blocks)):
        if n >= 2:
            saves[n - 2].wait()

        @pl.when(mine)
        def _():
            stage[n % 2] = dot_nt(d_ref[n * tokens : (n + 1) * tokens, :], w_ref[...]).astype(BF)

        @pl.when(jnp.logical_not(mine))
        def _():
            stage[n % 2] = jnp.zeros(stage.shape[1:], BF)

        saves[n].start()
    second.wait()

    @pl.when(mine)
    def _():
        acc[...] = dot_tn(left[...], d_ref[...])
        place_rows(0, 3 * width)

    for save in saves[-2:]:
        save.wait()
    shared.add_dp()


def attend_back(da_all, xn, out_all, saved, tables, w, g, tokens, busy, dps, lanes, cores):
    q, k, kt, v, o, lse = saved
    cos, sin = tables
    seq, width = q.shape
    model = w.shape[0]
    block = 256
    dma = pltpu.SemaphoreType.DMA
    whole = pl.BlockSpec(memory_space=pltpu.VMEM)
    return pl.pallas_call(
        functools.partial(attend_back_kernel, dps, lanes, cores, busy, block, 1.0 / math.sqrt(HD)),
        in_specs=[ANY] * 3 + [whole] * 9 + [ANY],
        out_specs=[ANY, whole, whole],
        out_shape=[
            jax.ShapeDtypeStruct((lanes, cores, tokens, model), BF),
            jax.ShapeDtypeStruct((dps, lanes * cores, g.shape[3], 4 * width), BF),
            jax.ShapeDtypeStruct((lanes,) + g.shape[3:], BF),
        ],
        scratch_shapes=[
            pltpu.VMEM((seq, model), BF),
            pltpu.VMEM((seq, 3 * width), BF),
            pltpu.VMEM((model, 3 * width), F32),
            pltpu.VMEM((2, tokens, model), BF),
            pltpu.VMEM((model, width), BF),
            pltpu.VMEM((seq, width), BF),
            pltpu.VMEM((seq, HD), F32),
            pltpu.VMEM((seq, HD), F32),
            dma((2,)),
            dma((2,)),
            pltpu.VMEM((dps, lanes) + g.shape[3:], BF),
            pltpu.VMEM((max(cores - 1, 1), dps, lanes) + g.shape[3:], BF),
            pltpu.VMEM((dps - 1, lanes) + g.shape[3:], BF),
        ]
        + pair(cores) + pair(dps) + [dma],
        cost_estimate=lasts(50),
        compiler_params=pltpu.CompilerParams(
            collective_id=5, has_side_effects=True, vmem_limit_bytes=VMEM_LIMIT
        ),
    )(da_all, xn, out_all, q, k, kt, v, o, lse, cos, sin, w, g)


def finish_kernel(
    dps, lanes, cores, busy, part_ref, g_ref, line_sum, x_ref, gain_ref, dx_ref, wq_ref,
    out_ref, gq_ref, go_ref, sum_ref, one_ref, mix_ref,
    from_core, stage, inbox, from_dp, total_g, from_z,
    z_out, z_in, c_out, c_in, g_out, g_in, m_out, m_in, local, s_out, s_in,
):
    dp, fs, z, c = place(cores)
    fss = lanes * cores
    greet(sequence_peers(dp, fs, fss) + [(lax.rem(dp + m, dps), fs) for m in range(1, dps)])

    def has_next(side):
        return z < lanes - 1 if side == 0 else z > 0

    def over(m):
        t = lax.rem(dp + m, dps)
        return send(g_ref.at[t], from_dp.at[m - 1], g_out.at[m - 1], g_in.at[m - 1], (t, fs))

    def across(m, block):
        t = lax.rem(c + m, cores)
        return send(
            part_ref.at[block, t], from_core.at[m - 1, block], c_out.at[m - 1, block], c_in.at[m - 1, block],
            (dp, z * cores + t),
        )

    def hop(side, step):
        return send(
            stage.at[side, step - 1], inbox.at[side, step - 1], z_out.at[side, step - 1],
            z_in.at[side, step - 1], (dp, fs + (cores if side == 0 else -cores)),
        )

    def home(k, owner):
        t = lax.rem(fs + k, fss)
        return send(total_g.at[t], mix_ref.at[head_slot(owner, lanes, cores)], m_out.at[k - 1], m_in.at[k - 1], (dp, t))

    def along(k):
        t = lax.rem(z + k, lanes)
        return send(
            line_sum.at[t], from_z.at[k - 1], s_out.at[k - 1], s_in.at[k - 1], (dp, t * cores + c)
        )

    def goal(side, step):
        block = z + lanes - step if side == 0 else z - lanes + step
        return block, (block >= 0) & (block < lanes)

    def begin(block):
        for m in range(1, cores):
            across(m, block).start()

    def partial_sum(block):
        total = part_ref[block, c].astype(F32)
        for m in range(1, cores):
            across(m, block).wait_recv()
            total = total + from_core[m - 1, block].astype(F32)
        return total

    def advance(step):
        for side in (0, 1):
            block, there = goal(side, step)
            fed = z > 0 if side == 0 else z < lanes - 1

            @pl.when(there)
            def _():
                total = partial_sum(block)
                stage[side, step - 1] = total.astype(BF)
                if step > 1:

                    @pl.when(fed)
                    def _():
                        hop(side, step - 1).wait_recv()
                        stage[side, step - 1] = (total + inbox[side, step - 2].astype(F32)).astype(BF)

                hop(side, step).start()

    for step in range(1, lanes):
        for side in (0, 1):
            block, there = goal(side, step)

            @pl.when(there)
            def _():
                begin(block)

    begin(z)
    for m in range(1, dps):
        over(m).start()
    for k in range(1, lanes):
        along(k).start()
    for step in range(1, max(lanes - 1, 1)):
        advance(step)
    for m in range(1, dps):
        over(m).wait_recv()
    for f in range(fss):
        total = g_ref[dp, f].astype(F32)
        for m in range(1, dps):
            total = total + from_dp[m - 1, f].astype(F32)
        total_g[f] = total.astype(BF)
    keep = pltpu.make_async_copy(total_g.at[fs], mix_ref.at[head_slot(fs, lanes, cores)], local)

    @pl.when(head_slot(fs, lanes, cores) < busy)
    def _():
        for k in range(1, fss):
            home(k, fs).start()
        keep.start()

    if lanes > 1:
        advance(lanes - 1)
    out_ref[...] = partial_sum(z)
    for side in (0, 1):
        fed = z > 0 if side == 0 else z < lanes - 1

        @pl.when(fed)
        def _():
            hop(side, lanes - 1).wait_recv()
            out_ref[...] += inbox[side, lanes - 2].astype(F32)

    total = line_sum[z].astype(F32)
    for k in range(1, lanes):
        along(k).wait_recv()
        total = total + from_z[k - 1].astype(F32)
    sum_ref[...] = total
    for k in range(1, lanes):
        along(k).wait_send()
    for k in range(1, fss):
        owner = lax.rem(fs + fss - k, fss)

        @pl.when(head_slot(owner, lanes, cores) < busy)
        def _():
            home(k, owner).wait_recv()

    @pl.when(head_slot(fs, lanes, cores) < busy)
    def _():
        keep.wait()
        for k in range(1, fss):
            home(k, fs).wait_send()

    model = out_ref.shape[1]
    width = mix_ref.shape[2] // 4
    one = None
    for slot in range(busy):
        lo = slot * width
        wide = min(width, model - lo)
        for p in range(3):
            piece = mix_ref[slot, :, p * width : p * width + wide].astype(F32)
            gq_ref[:, p * model + lo : p * model + lo + wide] = piece
            weight = wq_ref[:, p * model + lo : p * model + lo + wide].astype(F32)
            term = jnp.sum(weight * piece, axis=1, keepdims=True)
            one = term if one is None else one + term
        go_ref[:, lo : lo + wide] = mix_ref[slot, :, 3 * width : 3 * width + wide].astype(F32)
    one_ref[...] = one
    x = x_ref[...].astype(F32)
    inv = lax.rsqrt(jnp.mean(x * x, axis=1, keepdims=True) + norm_eps)
    unit = x * inv
    scaled = out_ref[...] * gain_ref[...]
    out_ref[...] = dx_ref[...] + inv * (scaled - unit * jnp.mean(scaled * unit, axis=1, keepdims=True))
    for step in range(1, lanes):
        for side in (0, 1):
            block, there = goal(side, step)

            @pl.when(there)
            def _():
                hop(side, step).wait_send()

    for m in range(1, cores):
        for block in range(lanes):
            across(m, block).wait_send()
    for m in range(1, dps):
        over(m).wait_send()


def finish(part, g, g_line, x, gain, dx, w_qkv, lanes, cores, busy):
    dps, fss = g.shape[:2]
    tokens, model = part.shape[2:]
    dma = pltpu.SemaphoreType.DMA
    hops = (2, max(lanes - 1, 1))
    ways = (max(cores - 1, 1), lanes)
    whole = pl.BlockSpec(memory_space=pltpu.VMEM)
    return pl.pallas_call(
        functools.partial(finish_kernel, dps, lanes, cores, busy),
        in_specs=[whole] * 7,
        out_specs=[whole] * 5,
        out_shape=[
            jax.ShapeDtypeStruct((tokens, model), F32),
            jax.ShapeDtypeStruct(w_qkv.shape, F32),
            jax.ShapeDtypeStruct((w_qkv.shape[0], model), F32),
            jax.ShapeDtypeStruct(g_line.shape[1:], F32),
            jax.ShapeDtypeStruct((w_qkv.shape[0], 1), F32),
        ],
        scratch_shapes=[
            pltpu.VMEM((busy,) + g.shape[2:], BF),
            pltpu.VMEM(ways + (tokens, model), BF),
            pltpu.VMEM(hops + (tokens, model), BF),
            pltpu.VMEM(hops + (tokens, model), BF),
            pltpu.VMEM((dps - 1,) + g.shape[1:], BF),
            pltpu.VMEM(g.shape[1:], BF),
            pltpu.VMEM((max(lanes - 1, 1),) + g_line.shape[1:], BF),
            dma(hops), dma(hops), dma(ways), dma(ways), dma((dps - 1,)), dma((dps - 1,)),
            dma((fss - 1,)), dma((fss - 1,)), dma, dma((max(lanes - 1, 1),)), dma((max(lanes - 1, 1),)),
        ],
        cost_estimate=lasts(66),
        compiler_params=pltpu.CompilerParams(
            collective_id=6, has_side_effects=True, vmem_limit_bytes=VMEM_LIMIT
        ),
    )(part, g, g_line, x, gain, dx, w_qkv)


def per_device(x, w_qkv, w_out, w_shared, w_experts, gains, routes, gates, d_out):
    tokens, model = x.shape
    hidden = w_shared.shape[1] // 3
    experts, shard = w_experts.shape[:2]
    dps, fss = lax.axis_size("dp"), lax.axis_size("fsdp")
    cores = dps * fss // experts
    lanes = fss // cores
    seq = tokens * fss
    slots = tokens // 2
    per = -(-HEADS // fss)
    busy = -(-HEADS // per)
    width = per * HD
    dp, fs = lax.axis_index("dp"), lax.axis_index("fsdp")
    z, c = fs // cores, fs % cores

    def over_z(value, pairs):
        return lax.ppermute(
            value, "fsdp", [(a * cores + k, b * cores + k) for a, b in pairs for k in range(cores)]
        )

    cut = w_qkv.reshape(shard, 3, HEADS, HD)
    cut = jnp.pad(cut, ((0, 0), (0, 0), (0, fss * per - HEADS), (0, 0)))
    cut = cut.reshape(shard, 3, cores, lanes, width).transpose(3, 2, 0, 1, 4).reshape(fss, shard, 3 * width)
    wide_gains = jnp.pad(gains, ((0, 0), (0, HD - 2)))
    topk = routes.shape[1]
    table = jnp.concatenate([routes.T.astype(F32), gates.T], axis=0)
    table = jnp.pad(table, ((0, -2 * topk % 8), (0, 0)))
    x_all, slabs, tables, out_all, gains_all, picks, weigh = start(
        x, cut, table, w_out, wide_gains, topk, busy, dps, lanes, cores
    )
    x_all = x_all.reshape(seq, model)
    slabs = slabs.reshape(model, 3 * width)
    out_all = out_all.reshape(model, model)
    gain_rows = gains_all.reshape(model, HD)[:, :2].astype(F32).T
    w_heads = slabs
    gain_one, gain_two = gain_rows[0:1], gain_rows[1:2]

    half = HD // 2
    frequency = np.float32(10000.0) ** (-np.arange(half, dtype=np.float32) / np.float32(half))
    angles = np.arange(seq, dtype=np.float32)[:, None] * frequency[None, :]
    cosine, sine = np.cos(angles), np.sin(angles)
    cos = jnp.asarray(np.concatenate([cosine, cosine], axis=1), F32)
    sin = jnp.asarray(np.concatenate([-sine, sine], axis=1), F32)

    xn_one, q, k, v, kt, vt, o, lse, heads, shared_all, rows_here, rows_low = attend(
        x_all, gain_one, w_heads, cos, sin, w_experts, w_shared, tokens, busy, dps, lanes, cores
    )
    heads = heads[:, :model]
    shared_all = shared_all.reshape(model, 3 * hidden)

    middle = x.astype(F32) + dot_nt(heads, out_all)
    inv_two = lax.rsqrt(jnp.mean(middle * middle, axis=1, keepdims=True) + norm_eps)
    unit_two = middle * inv_two
    xn_two = (unit_two * gain_two).astype(BF)

    x_slots, c_slots, w_own, w_down, dx_shared, f_shared, g_shared_part = dispatch(
        xn_two, d_out, tables, picks, rows_here, rows_low, shared_all, topk, lanes, cores
    )
    x_slots = x_slots.reshape(-1, model)
    c_slots = c_slots.reshape(-1, model)
    w_own = w_own.reshape(model, 2 * hidden)
    w_down = w_down.reshape(model, hidden)
    dx_slots, gu_slots, hid_slots = expert(x_slots, c_slots, w_own, w_down, BF)

    shape = (dps, lanes, slots, model)
    dx_routed, f_slots = combine(dx_slots.reshape(shape), picks, hid_slots, w_down, lanes, cores)
    dxn_two = dx_shared + dx_routed
    scaled = dxn_two * gain_two
    dx_two = d_out.astype(F32) + inv_two * (
        scaled - unit_two * jnp.mean(scaled * unit_two, axis=1, keepdims=True)
    )
    d_attn = dx_two.astype(BF)

    da_all, routed, g_own = turn(
        d_attn, f_slots, weigh, (x_slots, c_slots), (gu_slots, hid_slots), shard, lanes, cores
    )
    da_all = da_all.reshape(seq, model)
    layer_out = (middle + f_shared + routed).astype(BF)
    dxn_part, g_part, g_line = attend_back(
        da_all, xn_one, out_all, (q, k, kt, v, o, lse), (cos, sin), w_heads, g_shared_part,
        tokens, busy, dps, lanes, cores,
    )
    d_x, g_qkv, g_out, g_shared, one = finish(
        dxn_part, g_part, g_line, x, gain_one, dx_two, w_qkv, lanes, cores, busy
    )

    groups = [[e * cores + k for e in range(experts)] for k in range(cores)]
    g_experts = lax.all_to_all(
        g_own, ("dp", "fsdp"), split_axis=0, concat_axis=0, tiled=True, axis_index_groups=groups
    ).astype(F32)

    two = jnp.sum(w_shared[:, : 2 * hidden].astype(F32) * g_shared[:, : 2 * hidden], axis=1)
    two = two + jnp.sum(
        w_experts[:, :, : 2 * hidden].astype(F32) * g_experts[:, :, : 2 * hidden], axis=(0, 2)
    )
    g_gains = jnp.concatenate([one, two[:, None]], axis=1) / gains.astype(F32)
    return (layer_out, d_x, g_qkv, g_out, g_shared, g_experts, g_gains)


def solution(mesh):
    rows = P(("dp", "fsdp"), None)
    cube = P(None, ("dp", "fsdp"), None)
    return jax.shard_map(
        per_device,
        mesh=mesh,
        in_specs=(rows, rows, rows, rows, cube, rows, rows, rows, rows),
        out_specs=(rows, rows, rows, rows, rows, cube, rows),
        check_vma=False,
    )
```

```python
import functools
import math

import jax
import jax.numpy as jnp
import numpy as np
from jax import lax
from jax.experimental import pallas as pl
from jax.experimental.pallas import tpu as pltpu
from jax.sharding import PartitionSpec as P

HEADS = 10
HD = 128
norm_eps = 1e-06
masked_score = -1000000000.0
BF = jnp.bfloat16
F32 = jnp.float32
VMEM_LIMIT = 60 * 2**20


def dot_nn(a, b):
    return lax.dot_general(a, b, (((1,), (0,)), ((), ())), preferred_element_type=F32)


def dot_nt(a, b):
    return lax.dot_general(a, b, (((1,), (1,)), ((), ())), preferred_element_type=F32)


def dot_tn(a, b):
    return lax.dot_general(a, b, (((0,), (0,)), ((), ())), preferred_element_type=F32)


def lasts(us):
    return pl.CostEstimate(flops=0, bytes_accessed=int(us * 3.6e6), transcendentals=0)


def causal(rows):
    shape = (rows, rows)
    key = lax.broadcasted_iota(jnp.int32, shape, 0)
    query = lax.broadcasted_iota(jnp.int32, shape, 1)
    return key <= query


def unrotate(g, cos, sin):
    return g * cos - pltpu.roll(g, HD // 2, 1) * sin


def feed(x, c, w_ref, down_ref, hidden):
    gate = dot_nn(x, w_ref[:, :hidden])
    up = dot_nn(x, w_ref[:, hidden : 2 * hidden])
    down = dot_nn(c, down_ref[...])
    sig = 1.0 / (1.0 + jnp.exp(-gate))
    act = gate * sig
    dup = (down * act).astype(BF)
    dgate = (down * up * sig * (1.0 + gate * (1.0 - sig))).astype(BF)
    dx = dot_nt(dgate, w_ref[:, :hidden]) + dot_nt(dup, w_ref[:, hidden : 2 * hidden])
    return dx, dgate, dup, (act * up).astype(BF)


MESH = pl.DeviceIdType.MESH
ANY = pl.BlockSpec(memory_space=pl.ANY)


def place(cores):
    dp, fs = lax.axis_index("dp"), lax.axis_index("fsdp")
    return dp, fs, fs // cores, fs % cores


def greet(peers):
    barrier = pltpu.get_barrier_semaphore()
    for peer in peers:
        pl.semaphore_signal(barrier, inc=1, device_id=peer, device_id_type=MESH)
    pl.semaphore_wait(barrier, len(peers))


def head_slot(f, lanes, cores):
    return lax.rem(f, cores) * lanes + f // cores


def sequence_peers(dp, fs, fss):
    return [(dp, lax.rem(fs + k, fss)) for k in range(1, fss)]


def send(source, target, out, came, peer):
    return pltpu.make_async_remote_copy(
        src_ref=source, dst_ref=target, send_sem=out, recv_sem=came, device_id=peer, device_id_type=MESH
    )


class Chain:
    def __init__(self, own, full, lanes, cores, sems):
        self.own, self.full, self.lanes, self.cores = own, full, lanes, cores
        self.z_out, self.z_in, self.c_out, self.c_in, self.local = sems
        self.dp, self.fs, self.z, self.c = place(cores)

    def hop(self, side, step, block):
        by = self.cores if side == 0 else -self.cores
        source = self.own if step == 0 else self.full.at[block, self.c]
        return send(
            source, self.full.at[block, self.c], self.z_out.at[side, step], self.z_in.at[side, step],
            (self.dp, self.fs + by),
        )

    def across(self, m, block, source, core):
        return send(
            source, self.full.at[block, core], self.c_out.at[m - 1, block], self.c_in.at[m - 1, block],
            (self.dp, self.z * self.cores + lax.rem(self.c + m, self.cores)),
        )

    def keep(self):
        return pltpu.make_async_copy(self.own, self.full.at[self.z, self.c], self.local)

    def has_next(self, side):
        return self.z < self.lanes - 1 if side == 0 else self.z > 0

    def begin(self):
        for side in (0, 1):

            @pl.when(self.has_next(side))
            def _():
                self.hop(side, 0, self.z).start()

        for m in range(1, self.cores):
            self.across(m, self.z, self.own, self.c).start()
        self.keep().start()

    def came(self, side, step):
        block = self.z - step if side == 0 else self.z + step
        return block, (block >= 0) & (block < self.lanes)

    def advance(self, step):
        for side in (0, 1):
            block, there = self.came(side, step)

            @pl.when(there)
            def _():
                self.hop(side, step - 1, block).wait_recv()

            @pl.when(there & self.has_next(side))
            def _():
                self.hop(side, step, block).start()

            @pl.when(there)
            def _():
                for m in range(1, self.cores):
                    self.across(m, block, self.full.at[block, self.c], self.c).start()

    def finish(self):
        self.keep().wait()
        for m in range(1, self.cores):
            for block in range(self.lanes):
                self.across(m, block, self.own, lax.rem(self.c + self.cores - m, self.cores)).wait_recv()
        for side in (0, 1):
            for step in range(self.lanes - 1):
                block, there = self.came(side, step)

                @pl.when(there & self.has_next(side))
                def _():
                    self.hop(side, step, block).wait_send()

        for m in range(1, self.cores):
            for block in range(self.lanes):
                self.across(m, block, self.own, self.c).wait_send()


def chain_sems(lanes, cores):
    dma = pltpu.SemaphoreType.DMA
    hops = (2, max(lanes - 1, 1))
    ways = (max(cores - 1, 1), lanes)
    return [dma(hops), dma(hops), dma(ways), dma(ways), dma]


class Line:
    def __init__(self, own, buffer, lanes, cores, out, came):
        self.own, self.buffer, self.lanes, self.cores = own, buffer, lanes, cores
        self.out, self.into = out, came
        self.dp, self.fs, self.z, self.c = place(cores)

    def has_next(self, side):
        return self.z < self.lanes - 1 if side == 0 else self.z > 0

    def near(self, side):
        return (self.dp, self.fs + (self.cores if side == 0 else -self.cores))

    def hop(self, side, step, block):
        source = self.own if step == 0 else self.buffer.at[block]
        return send(
            source, self.buffer.at[block], self.out.at[side, step], self.into.at[side, step], self.near(side)
        )

    def begin(self):
        for side in (0, 1):

            @pl.when(self.has_next(side))
            def _():
                self.hop(side, 0, self.z).start()

    def came(self, side, step):
        block = self.z - step if side == 0 else self.z + step
        return block, (block >= 0) & (block < self.lanes)

    def advance(self, step, then):
        for side in (0, 1):
            block, there = self.came(side, step)

            @pl.when(there)
            def _():
                self.hop(side, step - 1, block).wait_recv()

            @pl.when(there & self.has_next(side))
            def _():
                self.hop(side, step, block).start()

            @pl.when(there)
            def _():
                then(block, self.buffer.at[block])

    def finish(self):
        for step in range(self.lanes - 1):
            for side in (0, 1):
                block, there = self.came(side, step)

                @pl.when(there & self.has_next(side))
                def _():
                    self.hop(side, step, block).wait_send()


class Spread:
    def __init__(self, stage, target, dps, lanes, cores, out, came, local):
        self.stage, self.target, self.dps, self.lanes = stage, target, dps, lanes
        self.out, self.into, self.local = out, came, local
        self.dp, self.fs, self.z, self.c = place(cores)

    def over(self, m, block):
        return send(
            self.stage.at[m, block], self.target.at[m, block], self.out.at[m - 1, block],
            self.into.at[m - 1, block], (lax.rem(self.dp + m, self.dps), self.fs),
        )

    def keep(self, block):
        return pltpu.make_async_copy(
            self.stage.at[0, block], self.target.at[0, block], self.local.at[block]
        )

    def go(self, m, block):
        if m:
            self.over(m, block).start()
        else:
            self.keep(block).start()

    def order(self):
        return list(range(1, self.dps)) + [0]

    def finish(self):
        for block in range(self.lanes):
            self.keep(block).wait()
            for m in range(1, self.dps):
                self.over(m, block).wait_recv()
        for block in range(self.lanes):
            for m in range(1, self.dps):
                self.over(m, block).wait_send()


class Rows:
    def __init__(self, own, full, dps, lanes, cores, sems):
        self.own, self.full, self.dps, self.lanes, self.cores = own, full, dps, lanes, cores
        self.z_out, self.z_in, self.d_out, self.d_in, self.c_out, self.c_in, self.local = sems
        self.dp, self.fs, self.z, self.c = place(cores)

    def along(self, k):
        t = lax.rem(self.z + k, self.lanes) * self.cores + self.c
        return send(
            self.own, self.full.at[self.dp, self.z, self.c], self.z_out.at[k - 1], self.z_in.at[k - 1],
            (self.dp, t),
        )

    def over(self, m, block):
        piece = self.full.at[block, :, self.c]
        return send(
            piece, piece, self.d_out.at[m - 1], self.d_in.at[m - 1], (lax.rem(self.dp + m, self.dps), self.fs)
        )

    def across(self, m, core):
        piece = self.full.at[:, :, core]
        peer = (self.dp, self.z * self.cores + lax.rem(self.c + m, self.cores))
        return send(piece, piece, self.c_out.at[m - 1], self.c_in.at[m - 1], peer)

    def keep(self):
        return pltpu.make_async_copy(self.own, self.full.at[self.dp, self.z, self.c], self.local)

    def begin(self):
        for k in range(1, self.lanes):
            self.along(k).start()
        self.keep().start()

    def to_dp(self):
        self.keep().wait()
        for k in range(1, self.lanes):
            self.along(k).wait_recv()
        for m in range(1, self.dps):
            self.over(m, self.dp).start()

    def to_cores(self):
        for m in range(1, self.dps):
            self.over(m, lax.rem(self.dp + self.dps - m, self.dps)).wait_recv()
        for m in range(1, self.cores):
            self.across(m, self.c).start()

    def finish(self):
        for m in range(1, self.cores):
            self.across(m, lax.rem(self.c + self.cores - m, self.cores)).wait_recv()
        for k in range(1, self.lanes):
            self.along(k).wait_send()
        for m in range(1, self.dps):
            self.over(m, self.dp).wait_send()
        for m in range(1, self.cores):
            self.across(m, self.c).wait_send()


def pair(n):
    return [pltpu.SemaphoreType.DMA((max(n - 1, 1),)) for _ in range(2)]


def rows_sems(dps, lanes, cores):
    return pair(lanes) + pair(dps) + pair(cores) + [pltpu.SemaphoreType.DMA]


def start_kernel(
    dps, lanes, cores, topk, busy, x_ref, wh_ref, tab_ref, wo_ref, gn_ref,
    full_ref, heads_ref, tabs_ref, out_ref, gains_ref, pick_ref, weigh_ref,
    h_out, h_in, hd_out, hd_in, t_out, t_in, locals_, *sems,
):
    rows = Rows(wo_ref, out_ref, dps, lanes, cores, sems[:7])
    gains = Rows(gn_ref, gains_ref, dps, lanes, cores, sems[7:14])
    chain = Chain(x_ref, full_ref, lanes, cores, sems[14:])
    dp, fs, z, c = chain.dp, chain.fs, chain.z, chain.c
    fss = lanes * cores
    slots, tokens = pick_ref.shape[2:]
    greet(sequence_peers(dp, fs, fss) + [(lax.rem(dp + m, dps), fs) for m in range(1, dps)])
    chain.begin()
    kept = [
        pltpu.make_async_copy(wh_ref.at[fs], heads_ref.at[dp, fs], locals_.at[0]),
        pltpu.make_async_copy(tab_ref, tabs_ref.at[z], locals_.at[1]),
    ]
    for copy in kept:
        copy.start()

    def heads_to(k):
        t = lax.rem(fs + k, fss)
        return send(wh_ref.at[t], heads_ref.at[dp, fs], h_out.at[k - 1], h_in.at[k - 1], (dp, t))

    def table_to(k):
        t = lax.rem(z + k, lanes) * cores + c
        return send(tab_ref, tabs_ref.at[z], t_out.at[k - 1], t_in.at[k - 1], (dp, t))

    def heads_over(m, block):
        return send(
            heads_ref.at[block], heads_ref.at[block], hd_out.at[m - 1], hd_in.at[m - 1],
            (lax.rem(dp + m, dps), fs),
        )

    mine = head_slot(fs, lanes, cores) < busy
    for k in range(1, fss):

        @pl.when(head_slot(lax.rem(fs + k, fss), lanes, cores) < busy)
        def _():
            heads_to(k).start()

    for k in range(1, lanes):
        table_to(k).start()
    gains.begin()
    rows.begin()
    for copy in kept:
        copy.wait()
    if lanes > 1:
        chain.advance(1)
    @pl.when(mine)
    def _():
        for k in range(1, fss):
            heads_to(k).wait_recv()
        for m in range(1, dps):
            heads_over(m, dp).start()

    gains.to_dp()
    rows.to_dp()
    for step in range(2, lanes):
        chain.advance(step)
    for k in range(1, lanes):
        table_to(k).wait_recv()

    triangle = (
        lax.broadcasted_iota(jnp.int32, (tokens, tokens), 0)
        <= lax.broadcasted_iota(jnp.int32, (tokens, tokens), 1)
    ).astype(BF)
    slot = lax.broadcasted_iota(jnp.int32, (slots, tokens), 0).astype(F32)
    for m in range(dps):
        name = (lax.rem(dp + m, dps) * lanes + z).astype(F32)
        for block in range(lanes):
            hit = tabs_ref[block, :topk, :] == name
            member = jnp.max(jnp.where(hit, 1.0, 0.0), axis=0, keepdims=True)
            gate = jnp.sum(jnp.where(hit, tabs_ref[block, topk : 2 * topk, :], 0.0), axis=0, keepdims=True)
            rank = dot_nn(jnp.broadcast_to(member, (8, tokens)).astype(BF), triangle)[:1] - 1.0
            match = (rank == slot) & (member > 0.5)
            pick_ref[m, block] = jnp.where(match, 1.0, 0.0).astype(BF)
            weigh_ref[m, block] = jnp.where(match, gate, 0.0).astype(BF)

    gains.to_cores()
    rows.to_cores()
    chain.finish()
    gains.finish()
    rows.finish()
    for k in range(1, fss):

        @pl.when(head_slot(lax.rem(fs + k, fss), lanes, cores) < busy)
        def _():
            heads_to(k).wait_send()

    for k in range(1, lanes):
        table_to(k).wait_send()

    @pl.when(mine)
    def _():
        for m in range(1, dps):
            heads_over(m, lax.rem(dp + dps - m, dps)).wait_recv()
            heads_over(m, dp).wait_send()


def start(x, wh, table, w_out, gains, topk, busy, dps, lanes, cores):
    fss = lanes * cores
    tokens = x.shape[0]
    dma = pltpu.SemaphoreType.DMA
    whole = pl.BlockSpec(memory_space=pltpu.VMEM)
    picks = jax.ShapeDtypeStruct((dps, lanes, tokens // 2, tokens), BF)
    shapes = [
        jax.ShapeDtypeStruct((lanes, cores) + x.shape, x.dtype),
        jax.ShapeDtypeStruct((dps,) + wh.shape, wh.dtype),
        jax.ShapeDtypeStruct((lanes,) + table.shape, table.dtype),
        jax.ShapeDtypeStruct((dps, lanes, cores) + w_out.shape, w_out.dtype),
        jax.ShapeDtypeStruct((dps, lanes, cores) + gains.shape, gains.dtype),
        picks,
        picks,
    ]
    return pl.pallas_call(
        functools.partial(start_kernel, dps, lanes, cores, topk, busy),
        in_specs=[ANY] * 5,
        out_specs=[ANY, ANY, whole, ANY, ANY, whole, whole],
        out_shape=shapes,
        scratch_shapes=pair(fss) + pair(dps) + pair(lanes) + [dma((2,))]
        + rows_sems(dps, lanes, cores) * 2 + chain_sems(lanes, cores),
        cost_estimate=lasts(70),
        compiler_params=pltpu.CompilerParams(
            collective_id=0, has_side_effects=True, vmem_limit_bytes=VMEM_LIMIT
        ),
    )(x, wh, table, w_out, gains)


class Slabs:
    def __init__(self, source, columns, target, dps, lanes, cores, sems):
        self.source, self.columns, self.target = source, columns, target
        self.lanes, self.cores, self.experts = lanes, cores, dps * lanes
        self.out, self.came, self.local = sems
        self.dp, self.fs, self.z, self.c = place(cores)
        self.me = self.dp * lanes + self.z

    def peer(self, k):
        e = lax.rem(self.me + k, self.experts)
        return (e // self.lanes, lax.rem(e, self.lanes) * self.cores + self.c)

    def to(self, k):
        e = lax.rem(self.me + k, self.experts)
        return send(
            self.source.at[e, :, self.columns], self.target.at[self.dp, self.z], self.out.at[k - 1],
            self.came.at[k - 1], self.peer(k),
        )

    def keep(self):
        return pltpu.make_async_copy(
            self.source.at[self.me, :, self.columns], self.target.at[self.dp, self.z], self.local
        )

    def begin(self):
        for k in range(1, self.experts):
            self.to(k).start()
        self.keep().start()

    def arrive(self):
        self.keep().wait()
        for k in range(1, self.experts):
            self.to(k).wait_recv()

    def finish(self):
        for k in range(1, self.experts):
            self.to(k).wait_send()


def slab_sems(experts):
    return pair(experts) + [pltpu.SemaphoreType.DMA]


def layer_peers(slabs):
    others = [
        (slabs.dp, lax.rem(slabs.z + a, slabs.lanes) * slabs.cores + lax.rem(slabs.c + m, slabs.cores))
        for a in range(slabs.lanes)
        for m in range(1, slabs.cores)
    ]
    return [slabs.peer(k) for k in range(1, slabs.experts)] + others


def attend_kernel(
    dps, lanes, cores, busy, block, scale,
    x_ref, gain_ref, w_ref, cos_ref, sin_ref, we_ref, sh_ref,
    xn_ref, q_ref, k_ref, v_ref, kt_ref, vt_ref, o_ref, lse_ref, mix_ref, all_ref, rows_ref, low_ref,
    out, came, local, *sems,
):
    dp, fs, z, c = place(cores)
    fss = lanes * cores
    tokens, width = mix_ref.shape[0], o_ref.shape[1]
    seq = x_ref.shape[0]
    up_width, low_width = rows_ref.shape[3], low_ref.shape[3]
    slabs = Slabs(we_ref, pl.ds(0, up_width), rows_ref, dps, lanes, cores, sems[:3])
    low_slabs = Slabs(we_ref, pl.ds(up_width, low_width), low_ref, dps, lanes, cores, sems[3:6])
    shared = Rows(sh_ref, all_ref, dps, lanes, cores, sems[6:])
    greet(layer_peers(slabs))
    shared.begin()
    slabs.begin()

    def project(i, carry):
        rows = pl.ds(pl.multiple_of(i * block, block), block)
        x = x_ref[rows, :].astype(F32)
        inv = lax.rsqrt(jnp.mean(x * x, axis=1, keepdims=True) + norm_eps)
        xn = (x * inv * gain_ref[...]).astype(BF)
        xn_ref[rows, :] = xn
        cos, sin = cos_ref[rows, :], sin_ref[rows, :]
        for part in range(3):
            wide = dot_nn(xn, w_ref[:, part * width : (part + 1) * width])
            for head in range(width // HD):
                cols = slice(head * HD, (head + 1) * HD)
                u = wide[:, cols]
                if part < 2:
                    u = u * cos + pltpu.roll(u, HD // 2, 1) * sin
                low = u.astype(BF)
                if part == 0:
                    q_ref[rows, cols] = low
                elif part == 1:
                    k_ref[rows, cols] = low
                    kt_ref[cols, rows] = u.T.astype(BF)
                else:
                    v_ref[rows, cols] = low
                    vt_ref[cols, rows] = u.T.astype(BF)
        return carry

    mine = head_slot(fs, lanes, cores) < busy

    @pl.when(mine)
    def _():
        lax.fori_loop(0, seq // block, project, 0)

    shared.to_dp()

    def head_rows(h, carry):
        cols = pl.ds(pl.multiple_of(h * HD, HD), HD)
        for j in range(seq // block):
            whole = j * block
            here = slice(whole, whole + block)
            q = q_ref[here, cols]
            tail = dot_nt(k_ref[here, cols], q) * scale
            tail = jnp.where(causal(block), tail, masked_score)
            top = jnp.max(tail, axis=0, keepdims=True)
            if j:
                front = dot_nt(k_ref[:whole, cols], q) * scale
                top = jnp.maximum(top, jnp.max(front, axis=0, keepdims=True))
            tail = jnp.exp(tail - top)
            total = jnp.sum(tail, axis=0, keepdims=True)
            mixed = dot_nn(vt_ref[cols, here], tail.astype(BF))
            if j:
                front = jnp.exp(front - top)
                total = total + jnp.sum(front, axis=0, keepdims=True)
                mixed = mixed + dot_nn(vt_ref[cols, :whole], front.astype(BF))
            o_ref[here, cols] = (mixed / total).T.astype(BF)
            lse_ref[h, :, here] = top + jnp.log(total)
        return carry

    @pl.when(mine)
    def _():
        lax.fori_loop(0, width // HD, head_rows, 0)

    def columns(f):
        slot = head_slot(f, lanes, cores)
        return mix_ref.at[:, pl.ds(pl.multiple_of(slot * width, HD), width)]

    def rows(f):
        return o_ref.at[pl.ds(pl.multiple_of(f * tokens, tokens), tokens), :]

    def to(k, owner):
        t = lax.rem(fs + k, fss)
        return send(rows(t), columns(owner), out.at[k - 1], came.at[k - 1], (dp, t))

    keep = pltpu.make_async_copy(rows(fs), columns(fs), local)

    @pl.when(head_slot(fs, lanes, cores) < busy)
    def _():
        for k in range(1, fss):
            to(k, fs).start()
        keep.start()

    low_slabs.begin()
    shared.to_cores()
    for k in range(1, fss):
        owner = lax.rem(fs + fss - k, fss)

        @pl.when(head_slot(owner, lanes, cores) < busy)
        def _():
            to(k, owner).wait_recv()

    @pl.when(head_slot(fs, lanes, cores) < busy)
    def _():
        keep.wait()
        for k in range(1, fss):
            to(k, fs).wait_send()

    shared.finish()
    slabs.arrive()
    slabs.finish()
    low_slabs.arrive()
    low_slabs.finish()


def attend(x_all, gain, w, cos, sin, w_experts, w_shared, tokens, busy, dps, lanes, cores):
    seq, model = x_all.shape
    width = w.shape[1] // 3
    experts, shard, thrice = w_experts.shape
    block = seq // 8
    fss = lanes * cores
    dma = pltpu.SemaphoreType.DMA
    whole = pl.BlockSpec(memory_space=pltpu.VMEM)
    flat = jax.ShapeDtypeStruct((seq, width), BF)
    turned = jax.ShapeDtypeStruct((width, seq), BF)
    return pl.pallas_call(
        functools.partial(attend_kernel, dps, lanes, cores, busy, block, 1.0 / math.sqrt(HD)),
        in_specs=[whole] * 5 + [ANY, ANY],
        out_specs=[whole] * 8 + [ANY] * 4,
        out_shape=[
            jax.ShapeDtypeStruct((seq, model), BF),
            flat, flat, flat, turned, turned, flat,
            jax.ShapeDtypeStruct((width // HD, 1, seq), F32),
            jax.ShapeDtypeStruct((tokens, busy * width), BF),
            jax.ShapeDtypeStruct((dps, lanes, cores) + w_shared.shape, BF),
            jax.ShapeDtypeStruct((dps, lanes, shard, thrice // 3 * 2), BF),
            jax.ShapeDtypeStruct((dps, lanes, shard, thrice // 3), BF),
        ],
        scratch_shapes=[dma((fss - 1,)), dma((fss - 1,)), dma]
        + slab_sems(experts) * 2 + rows_sems(dps, lanes, cores),
        cost_estimate=lasts(100),
        compiler_params=pltpu.CompilerParams(
            collective_id=2, has_side_effects=True, vmem_limit_bytes=VMEM_LIMIT
        ),
    )(x_all, gain, w, cos, sin, w_experts, w_shared)


def greet_cross(line, dps, cores=1):
    barrier = pltpu.get_barrier_semaphore()
    for m in range(1, dps):
        peer = (lax.rem(line.dp + m, dps), line.fs)
        pl.semaphore_signal(barrier, inc=1, device_id=peer, device_id_type=MESH)
    for side in (0, 1):

        @pl.when(line.has_next(side))
        def _():
            pl.semaphore_signal(barrier, inc=1, device_id=line.near(side), device_id_type=MESH)

    for m in range(1, cores):
        peer = (line.dp, line.z * cores + lax.rem(line.c + m, cores))
        pl.semaphore_signal(barrier, inc=1, device_id=peer, device_id_type=MESH)
    ends = line.has_next(0).astype(jnp.int32) + line.has_next(1).astype(jnp.int32)
    pl.semaphore_wait(barrier, dps - 1 + cores - 1 + ends)


class CoreSum:
    def __init__(self, source, own, scratch, dps, lanes, cores):
        self.source, self.own = source, own
        self.from_core, self.out, self.came = scratch
        self.dps, self.lanes, self.cores = dps, lanes, cores
        self.dp, self.fs, self.z, self.c = place(cores)

    def across(self, m):
        t = lax.rem(self.c + m, self.cores)
        return send(
            self.source.at[t], self.from_core.at[m - 1], self.out.at[m - 1], self.came.at[m - 1],
            (self.dp, self.z * self.cores + t),
        )

    def begin(self):
        for m in range(1, self.cores):
            self.across(m).start()

    def finish(self):
        for m in range(1, self.cores):
            self.across(m).wait_recv()

        def add(i, carry):
            p, q = i // self.lanes, lax.rem(i, self.lanes)
            total = self.source[self.c, p, q].astype(F32)
            for m in range(1, self.cores):
                total = total + self.from_core[m - 1, p, q].astype(F32)
            self.own[p, q] = total.astype(BF)
            return carry

        lax.fori_loop(0, self.dps * self.lanes, add, 0)
        for m in range(1, self.cores):
            self.across(m).wait_send()


def dispatch_kernel(
    dps, lanes, cores, topk, x_ref, up_ref, tabs_ref, pick_ref, rows_ref, low_ref, shared_ref,
    out_ref, c_ref, w_ref, wd_ref, dx_ref, f_ref, own_ref, g_ref, acts, acc, buffer, stage, up_buffer, up_stage, l_out, l_in, s_out, s_in, s_local,
    ul_out, ul_in, us_out, us_in, us_local, w_out, w_in, w_local, wd_out, wd_in, wd_local, *core,
):
    line = Line(x_ref, buffer, lanes, cores, l_out, l_in)
    spread = Spread(stage, out_ref, dps, lanes, cores, s_out, s_in, s_local)
    up_line = Line(up_ref, up_buffer, lanes, cores, ul_out, ul_in)
    up_spread = Spread(up_stage, c_ref, dps, lanes, cores, us_out, us_in, us_local)
    hidden = shared_ref.shape[1] // 3
    greet_cross(line, dps, cores)

    def across(m, core):
        peer = (line.dp, line.z * cores + lax.rem(line.c + m, cores))
        return send(rows_ref, w_ref.at[:, :, core], w_out.at[m - 1], w_in.at[m - 1], peer)

    def across_down(m, core):
        peer = (line.dp, line.z * cores + lax.rem(line.c + m, cores))
        return send(low_ref, wd_ref.at[:, :, core], wd_out.at[m - 1], wd_in.at[m - 1], peer)

    keep = pltpu.make_async_copy(rows_ref, w_ref.at[:, :, line.c], w_local)
    keep_down = pltpu.make_async_copy(low_ref, wd_ref.at[:, :, line.c], wd_local)

    def pick(block, source):
        for m in spread.order():
            stage[m, block] = dot_nn(pick_ref[m, block], source[...]).astype(BF)
            spread.go(m, block)

    def up_pick(block, source):
        for m in up_spread.order():
            name = (lax.rem(line.dp + m, dps) * lanes + line.z).astype(F32)
            hit = tabs_ref[block, :topk, :] == name
            gate = jnp.sum(jnp.where(hit, tabs_ref[block, topk : 2 * topk, :], 0.0), axis=0, keepdims=True)
            one = pick_ref[m, block]
            scale = jnp.sum(one.astype(F32) * gate, axis=1, keepdims=True)
            up_stage[m, block] = (dot_nn(one, source[...]) * scale).astype(BF)
            up_spread.go(m, block)

    line.begin()
    pick(line.z, x_ref)
    up_line.begin()
    up_pick(line.z, up_ref)
    keep.start()
    keep_down.start()
    for m in range(1, cores):
        across(m, line.c).start()
        across_down(m, line.c).start()
    experts, shard = dps * lanes, g_ref.shape[3]
    summed = CoreSum(g_ref, own_ref, core, dps, lanes, cores)

    def shared_forward():
        down_ref = shared_ref.at[:, 2 * hidden :]
        dx, gate, up, hid = feed(x_ref[...], up_ref[...], shared_ref, down_ref, hidden)
        dx_ref[...] = dx
        acts[0] = gate
        acts[1] = up
        acts[2] = hid
        f_ref[...] = dot_nt(hid, down_ref[...])

    def shared_gradient(third):
        acc[...] = dot_tn((x_ref if third < 2 else up_ref)[...], acts[third])
        for e in range(experts):
            for k in range(cores):
                row = (e * cores + k) * shard
                piece = acc[row : row + shard, :].astype(BF)
                g_ref[k, e // lanes, e % lanes, :, third * hidden : (third + 1) * hidden] = piece
        if third == 2:
            summed.begin()

    work = [shared_forward] + [functools.partial(shared_gradient, third) for third in range(3)]
    for step in range(1, lanes):
        line.advance(step, pick)
        up_line.advance(step, up_pick)
        work.pop(0)()
    for left in work:
        left()
    spread.finish()
    line.finish()
    up_spread.finish()
    up_line.finish()
    summed.finish()
    keep.wait()
    keep_down.wait()
    for m in range(1, cores):
        across(m, lax.rem(line.c + cores - m, cores)).wait_recv()
        across(m, line.c).wait_send()
        across_down(m, lax.rem(line.c + cores - m, cores)).wait_recv()
        across_down(m, line.c).wait_send()


def dispatch(x, upstream, tables, picks, rows, low, shared, topk, lanes, cores):
    dps, _, slots, tokens = picks.shape
    model = x.shape[1]
    shard, hidden = low.shape[2:]
    dma = pltpu.SemaphoreType.DMA
    hops = (2, max(lanes - 1, 1))
    ways = (dps - 1, lanes)
    whole = pl.BlockSpec(memory_space=pltpu.VMEM)
    buffers = [pltpu.VMEM((lanes, tokens, model), BF), pltpu.VMEM((dps, lanes, slots, model), BF)]
    moves = [dma(hops), dma(hops), dma(ways), dma(ways), dma((lanes,))]
    return pl.pallas_call(
        functools.partial(dispatch_kernel, dps, lanes, cores, topk),
        in_specs=[whole] * 4 + [ANY, ANY, whole],
        out_specs=[ANY] * 4 + [whole] * 3,
        out_shape=[
            jax.ShapeDtypeStruct((dps, lanes, slots, model), BF),
            jax.ShapeDtypeStruct((dps, lanes, slots, model), BF),
            jax.ShapeDtypeStruct((dps, lanes, cores) + rows.shape[2:], BF),
            jax.ShapeDtypeStruct((dps, lanes, cores, shard, hidden), BF),
            jax.ShapeDtypeStruct((tokens, model), F32),
            jax.ShapeDtypeStruct((tokens, model), F32),
            jax.ShapeDtypeStruct((dps, lanes, shard, 3 * hidden), BF),
        ],
        scratch_shapes=[
            pltpu.VMEM((cores, dps, lanes, shard, 3 * hidden), BF),
            pltpu.VMEM((3, tokens, shared.shape[1] // 3), BF),
            pltpu.VMEM((model, shared.shape[1] // 3), F32),
        ]
        + buffers * 2 + moves * 2 + (pair(cores) + [dma]) * 2
        + [pltpu.VMEM((max(cores - 1, 1), dps, lanes, shard, 3 * hidden), BF)] + pair(cores),
        cost_estimate=lasts(125),
        compiler_params=pltpu.CompilerParams(
            collective_id=3, has_side_effects=True, vmem_limit_bytes=VMEM_LIMIT
        ),
    )(x, upstream, tables, picks, rows, low, shared)


def expert_kernel(
    steps, dps, lanes, cores, hidden, x_ref, c_ref, w_ref, down_ref, own_ref,
    dx_ref, gu_ref, hid_ref, line_ref, mine, from_dp, out, came, local,
):
    dp, fs, z, c = place(cores)
    step = pl.program_id(0)

    def over(m):
        t = lax.rem(dp + m, dps)
        return send(own_ref.at[t], from_dp.at[m - 1], out.at[m - 1], came.at[m - 1], (t, fs))

    keep = pltpu.make_async_copy(own_ref.at[dp], mine, local)

    @pl.when(step == 0)
    def _():
        greet([(lax.rem(dp + m, dps), fs) for m in range(1, dps)])
        for m in range(1, dps):
            over(m).start()
        keep.start()

    dx, dgate, dup, hid = feed(x_ref[...], c_ref[...], w_ref, down_ref, hidden)
    dx_ref[...] = dx.astype(dx_ref.dtype)
    gu_ref[:, :hidden] = dgate
    gu_ref[:, hidden:] = dup
    hid_ref[...] = hid

    @pl.when(step == steps - 1)
    def _():
        keep.wait()
        for m in range(1, dps):
            over(m).wait_recv()
        for q in range(lanes):
            total = mine[q].astype(F32)
            for m in range(1, dps):
                total = total + from_dp[m - 1, q].astype(F32)
            line_ref[q] = total.astype(BF)
        for m in range(1, dps):
            over(m).wait_send()


def expert(x, c, w, down, own, cores):
    rows, model = x.shape
    hidden = down.shape[1]
    dps, lanes = own.shape[:2]
    block = min(512, rows)
    dma = pltpu.SemaphoreType.DMA
    row = lambda cols: pl.BlockSpec((block, cols), lambda i: (i, 0))
    return pl.pallas_call(
        functools.partial(expert_kernel, rows // block, dps, lanes, cores, hidden),
        grid=(rows // block,),
        in_specs=[
            row(model),
            row(model),
            pl.BlockSpec(w.shape, lambda i: (0, 0)),
            pl.BlockSpec(down.shape, lambda i: (0, 0)),
            ANY,
        ],
        out_specs=[
            row(model), row(2 * hidden), row(hidden), pl.BlockSpec(own.shape[1:], lambda i: (0, 0, 0)),
        ],
        out_shape=[
            jax.ShapeDtypeStruct((rows, model), BF),
            jax.ShapeDtypeStruct((rows, 2 * hidden), BF),
            jax.ShapeDtypeStruct((rows, hidden), BF),
            jax.ShapeDtypeStruct(own.shape[1:], BF),
        ],
        scratch_shapes=[
            pltpu.VMEM(own.shape[1:], BF),
            pltpu.VMEM((dps - 1,) + own.shape[1:], BF),
        ]
        + pair(dps) + [dma],
        cost_estimate=lasts(40),
        compiler_params=pltpu.CompilerParams(
            collective_id=7, has_side_effects=True, vmem_limit_bytes=VMEM_LIMIT
        ),
    )(x, c, w, down, own)


class Combine:
    def __init__(self, parts, picks, result, scratch, dps, lanes, cores):
        self.parts, self.picks, self.result = parts, picks, result
        self.back, self.stage, self.inbox = scratch[:3]
        self.z_out, self.z_in, self.d_out, self.d_in, self.local = scratch[3:]
        self.dps, self.lanes, self.cores = dps, lanes, cores
        self.dp, self.fs, self.z, self.c = place(cores)

    def over(self, m, block):
        return send(
            self.parts.at[m, block], self.back.at[block, m], self.d_out.at[m - 1, block],
            self.d_in.at[m - 1, block], (lax.rem(self.dp + self.dps - m, self.dps), self.fs),
        )

    def keep(self, block):
        return pltpu.make_async_copy(
            self.parts.at[0, block], self.back.at[block, 0], self.local.at[block]
        )

    def hop(self, side, step):
        return send(
            self.stage.at[side, step - 1], self.inbox.at[side, step - 1], self.z_out.at[side, step - 1],
            self.z_in.at[side, step - 1],
            (self.dp, self.fs + (self.cores if side == 0 else -self.cores)),
        )

    def goal(self, side, step):
        block = self.z + self.lanes - step if side == 0 else self.z - self.lanes + step
        return block, (block >= 0) & (block < self.lanes)

    def fed(self, side):
        return self.z > 0 if side == 0 else self.z < self.lanes - 1

    def send_block(self, block):
        for m in range(1, self.dps):
            self.over(m, block).start()
        self.keep(block).start()

    def begin(self):
        for step in range(1, self.lanes):
            for side in (0, 1):
                block, there = self.goal(side, step)

                @pl.when(there)
                def _():
                    self.send_block(block)

        self.send_block(self.z)

    def partial_sum(self, block):
        self.keep(block).wait()
        total = dot_tn(self.picks[0, block], self.back[block, 0])
        for m in range(1, self.dps):
            self.over(m, block).wait_recv()
            total = total + dot_tn(self.picks[m, block], self.back[block, m])
        return total

    def advance(self, step):
        for side in (0, 1):
            block, there = self.goal(side, step)

            @pl.when(there)
            def _():
                total = self.partial_sum(block)
                self.stage[side, step - 1] = total.astype(BF)
                if step > 1:

                    @pl.when(self.fed(side))
                    def _():
                        self.hop(side, step - 1).wait_recv()
                        more = self.inbox[side, step - 2].astype(F32)
                        self.stage[side, step - 1] = (total + more).astype(BF)

                self.hop(side, step).start()

    def finish(self):
        self.result[...] = self.partial_sum(self.z)
        for side in (0, 1):

            @pl.when(self.fed(side))
            def _():
                self.hop(side, self.lanes - 1).wait_recv()
                self.result[...] += self.inbox[side, self.lanes - 2].astype(F32)

        for step in range(1, self.lanes):
            for side in (0, 1):
                block, there = self.goal(side, step)

                @pl.when(there)
                def _():
                    self.hop(side, step).wait_send()

        for block in range(self.lanes):
            for m in range(1, self.dps):
                self.over(m, block).wait_send()


def combine_scratch(dps, lanes, slots, tokens, model):
    dma = pltpu.SemaphoreType.DMA
    hops = (2, max(lanes - 1, 1))
    ways = (dps - 1, lanes)
    return [
        pltpu.VMEM((lanes, dps, slots, model), BF),
        pltpu.VMEM(hops + (tokens, model), BF),
        pltpu.VMEM(hops + (tokens, model), BF),
        dma(hops), dma(hops), dma(ways), dma(ways), dma((lanes,)),
    ]


def combine_kernel(
    dps, lanes, cores, part_ref, pick_ref, hid_ref, w_ref, line_ref, out_ref, f_ref, sum_ref,
    hid, down, load, from_z, s_out, s_in, *scratch,
):
    work = Combine(part_ref, pick_ref, out_ref, scratch, dps, lanes, cores)
    dp, fs, z, c = place(cores)
    hidden = hid.shape[1]
    slots = f_ref.shape[2]
    loads = [
        pltpu.make_async_copy(hid_ref, hid, load.at[0]),
        pltpu.make_async_copy(w_ref, down, load.at[1]),
    ]
    for copy in loads:
        copy.start()

    def along(k):
        t = lax.rem(z + k, lanes)
        return send(
            line_ref.at[t], from_z.at[k - 1], s_out.at[k - 1], s_in.at[k - 1], (dp, t * cores + c)
        )

    greet(
        [(lax.rem(dp + m, dps), fs) for m in range(1, dps)]
        + [(dp, lax.rem(z + k, lanes) * cores + c) for k in range(1, lanes)]
    )
    work.begin()
    for k in range(1, lanes):
        along(k).start()
    for copy in loads:
        copy.wait()

    def forward(m):
        for block in range(lanes):
            row = (m * lanes + block) * slots
            f_ref[m, block] = dot_nt(hid[row : row + slots, :], down[...]).astype(BF)

    per = -(-dps // max(lanes - 1, 1))
    for step in range(1, max(lanes, 2)):
        for m in range((step - 1) * per, min(step * per, dps)):
            forward(m)
        if step < lanes:
            work.advance(step)
    total = line_ref[z].astype(F32)
    for k in range(1, lanes):
        along(k).wait_recv()
        total = total + from_z[k - 1].astype(F32)
    sum_ref[...] = total
    work.finish()
    for k in range(1, lanes):
        along(k).wait_send()


def combine(parts, picks, hid, w, line, lanes, cores):
    dps, _, slots, model = parts.shape
    tokens = picks.shape[3]
    hidden = hid.shape[1]
    dma = pltpu.SemaphoreType.DMA
    whole = pl.BlockSpec(memory_space=pltpu.VMEM)
    return pl.pallas_call(
        functools.partial(combine_kernel, dps, lanes, cores),
        in_specs=[ANY, whole, ANY, ANY, whole],
        out_specs=[whole] * 3,
        out_shape=[
            jax.ShapeDtypeStruct((tokens, model), F32),
            jax.ShapeDtypeStruct(parts.shape, BF),
            jax.ShapeDtypeStruct(line.shape[1:], F32),
        ],
        scratch_shapes=[
            pltpu.VMEM(hid.shape, BF),
            pltpu.VMEM((model, hidden), BF),
            dma((2,)),
            pltpu.VMEM((max(lanes - 1, 1),) + line.shape[1:], BF),
        ]
        + pair(lanes)
        + combine_scratch(dps, lanes, slots, tokens, model),
        cost_estimate=lasts(70),
        compiler_params=pltpu.CompilerParams(
            collective_id=4, has_side_effects=True, vmem_limit_bytes=VMEM_LIMIT
        ),
    )(parts, picks, hid, w, line)


class Gradient:
    def __init__(self, refs, total, scratch, experts, shard, cores):
        self.x, self.c_rows, self.gu, self.hid = refs
        self.total = total
        self.left, self.right, self.acc, self.stage, self.inbox, self.load, self.out, self.came = scratch
        self.experts, self.shard, self.cores = experts, shard, cores
        self.hidden = self.hid.shape[1]
        self.dp, self.fs, self.z, self.c = place(cores)

    def rows_in(self, third):
        source = self.x if third < 2 else self.c_rows
        return pltpu.make_async_copy(source, self.left, self.load.at[0])

    def columns_in(self, third):
        source = self.hid if third == 2 else self.gu.at[:, third * self.hidden : (third + 1) * self.hidden]
        return pltpu.make_async_copy(source, self.right, self.load.at[1])

    def across(self, third, m):
        t = lax.rem(self.c + m, self.cores)
        return send(
            self.stage.at[third, t], self.inbox.at[third, m - 1], self.out.at[third, m - 1],
            self.came.at[third, m - 1], (self.dp, self.z * self.cores + t),
        )

    def begin(self):
        self.rows_in(0).start()
        self.columns_in(0).start()

    def multiply(self, third):
        if third != 1:
            self.rows_in(third).wait()
        self.columns_in(third).wait()
        self.acc[...] = dot_tn(self.left[...], self.right[...])
        if third < 2:
            self.columns_in(third + 1).start()
        if third == 1:
            self.rows_in(2).start()
        for e in range(self.experts):
            for k in range(self.cores):
                row = (e * self.cores + k) * self.shard
                self.stage[third, k, e] = self.acc[row : row + self.shard, :].astype(BF)
        for m in range(1, self.cores):
            self.across(third, m).start()

    def collect(self, third):
        for m in range(1, self.cores):
            self.across(third, m).wait_recv()
        for e in range(self.experts):
            total = self.stage[third, self.c, e].astype(F32)
            for m in range(1, self.cores):
                total = total + self.inbox[third, m - 1, e].astype(F32)
            self.total[e, :, third * self.hidden : (third + 1) * self.hidden] = total.astype(BF)

    def finish(self):
        for third in range(3):
            for m in range(1, self.cores):
                self.across(third, m).wait_send()


def turn_kernel(
    dps, lanes, cores, x_ref, part_ref, pick_ref, xs_ref, cs_ref, gu_ref, hid_ref,
    full_ref, out_ref, g_ref, *scratch,
):
    work = Combine(part_ref, pick_ref, out_ref, scratch[:8], dps, lanes, cores)
    gradient = Gradient(
        (xs_ref, cs_ref, gu_ref, hid_ref), g_ref, scratch[8:16], g_ref.shape[0], g_ref.shape[1], cores
    )
    chain = Chain(x_ref, full_ref, lanes, cores, scratch[16:])
    dp, fs = chain.dp, chain.fs
    gradient.begin()
    greet(sequence_peers(dp, fs, lanes * cores) + [(lax.rem(dp + m, dps), fs) for m in range(1, dps)])
    chain.begin()
    work.begin()
    gradient.multiply(0)
    for step in range(1, lanes):
        chain.advance(step)
        work.advance(step)
        if step == 1:
            gradient.multiply(1)
    if lanes == 1:
        gradient.multiply(1)
    gradient.multiply(2)
    chain.finish()
    work.finish()
    for third in range(3):
        gradient.collect(third)
    gradient.finish()


def turn(x, parts, picks, slots_in, grads, shard, lanes, cores):
    dps, _, slots, model = parts.shape
    tokens = picks.shape[3]
    xs, cs = slots_in
    gu, hid = grads
    experts = dps * lanes
    hidden = hid.shape[1]
    dma = pltpu.SemaphoreType.DMA
    others = max(cores - 1, 1)
    whole = pl.BlockSpec(memory_space=pltpu.VMEM)
    return pl.pallas_call(
        functools.partial(turn_kernel, dps, lanes, cores),
        in_specs=[ANY, ANY, whole] + [ANY] * 4,
        out_specs=[ANY, whole, whole],
        out_shape=[
            jax.ShapeDtypeStruct((lanes, cores) + x.shape, x.dtype),
            jax.ShapeDtypeStruct((tokens, model), F32),
            jax.ShapeDtypeStruct((experts, shard, 3 * hidden), BF),
        ],
        scratch_shapes=combine_scratch(dps, lanes, slots, tokens, model)
        + [
            pltpu.VMEM(xs.shape, BF),
            pltpu.VMEM(hid.shape, BF),
            pltpu.VMEM((model, hidden), F32),
            pltpu.VMEM((3, cores, experts, shard, hidden), BF),
            pltpu.VMEM((3, others, experts, shard, hidden), BF),
            dma((2,)), dma((3, others)), dma((3, others)),
        ]
        + chain_sems(lanes, cores),
        cost_estimate=lasts(90),
        compiler_params=pltpu.CompilerParams(
            collective_id=1, has_side_effects=True, vmem_limit_bytes=VMEM_LIMIT
        ),
    )(x, parts, picks, xs, cs, gu, hid)


def attend_back_kernel(
    dps, lanes, cores, busy, block, scale,
    da_ref, xn_ref, out_ref, q_ref, k_ref, kt_ref, v_ref, o_ref, lse_ref, cos_ref, sin_ref, w_ref,
    part_ref, prod_ref, left, d_ref, acc, stage, cols, do_all, dk_acc, dv_acc,
    load, stored,
):
    dp, fs, z, c = place(cores)
    seq, width = q_ref.shape
    tokens = part_ref.shape[2]
    slot = jnp.minimum(head_slot(fs, lanes, cores), busy - 1)
    fetch = pltpu.make_async_copy(
        out_ref.at[:, pl.ds(pl.multiple_of(slot * width, HD), width)], cols, load.at[0]
    )
    fetch.start()
    first, second = [pltpu.make_async_copy(ref, left, load.at[1]) for ref in (da_ref, xn_ref)]
    first.start()
    shard = prod_ref.shape[2]

    def place_rows(lo, hi):
        for p in range(dps):
            for f in range(lanes * cores):
                row = (p * lanes * cores + f) * shard
                prod_ref[p, f, :, lo:hi] = acc[row : row + shard, : hi - lo].astype(BF)

    fetch.wait()
    first.wait()

    def upstream(i, carry):
        rows = pl.ds(pl.multiple_of(i * block, block), block)
        do_all[rows, :] = dot_nn(left[rows, :], cols[...]).astype(BF)
        return carry

    mine = head_slot(fs, lanes, cores) < busy

    @pl.when(mine)
    def _():
        lax.fori_loop(0, seq // block, upstream, 0)

    @pl.when(mine)
    def _():
        acc[:, :width] = dot_tn(left[...], o_ref[...])
        place_rows(3 * width, 4 * width)

    second.start()

    def head_rows(h, carry):
        lane = pl.ds(pl.multiple_of(h * HD, HD), HD)
        k_lane = pl.ds(pl.multiple_of(width + h * HD, HD), HD)
        v_lane = pl.ds(pl.multiple_of(2 * width + h * HD, HD), HD)
        dk_acc[...] = jnp.zeros_like(dk_acc)
        dv_acc[...] = jnp.zeros_like(dv_acc)
        for j in range(seq // block):
            here = slice(j * block, (j + 1) * block)
            q = q_ref[here, lane]
            do = do_all[here, lane]
            row = jnp.sum((do.astype(F32) * o_ref[here, lane].astype(F32)).T, axis=0, keepdims=True)
            lse = lse_ref[h, :, here]
            dq = None
            for span, edge in ([(slice(0, j * block), False)] if j else []) + [(here, True)]:
                p = jnp.exp(dot_nt(k_ref[span, lane], q) * scale - lse)
                if edge:
                    p = jnp.where(causal(block), p, 0.0)
                ds = (p * (dot_nt(v_ref[span, lane], do) - row)).astype(BF)
                dv_acc[span, :] += dot_nn(p.astype(BF), do)
                dk_acc[span, :] += dot_nn(ds, q)
                term = dot_nn(kt_ref[lane, span], ds)
                dq = term if dq is None else dq + term
            d_ref[here, lane] = unrotate(dq.T * scale, cos_ref[here, :], sin_ref[here, :]).astype(BF)
        d_ref[:, k_lane] = unrotate(dk_acc[...] * scale, cos_ref[...], sin_ref[...]).astype(BF)
        d_ref[:, v_lane] = dv_acc[...].astype(BF)
        return carry

    @pl.when(mine)
    def _():
        lax.fori_loop(0, width // HD, head_rows, 0)

    blocks = [(a, b) for a in range(lanes) for b in range(cores)]
    saves = [
        pltpu.make_async_copy(stage.at[n % 2], part_ref.at[a, b], stored.at[n % 2])
        for n, (a, b) in enumerate(blocks)
    ]
    for n in range(len(blocks)):
        if n >= 2:
            saves[n - 2].wait()

        @pl.when(mine)
        def _():
            stage[n % 2] = dot_nt(d_ref[n * tokens : (n + 1) * tokens, :], w_ref[...]).astype(BF)

        @pl.when(jnp.logical_not(mine))
        def _():
            stage[n % 2] = jnp.zeros(stage.shape[1:], BF)

        saves[n].start()
    second.wait()

    @pl.when(mine)
    def _():
        acc[...] = dot_tn(left[...], d_ref[...])
        place_rows(0, 3 * width)

    for save in saves[-2:]:
        save.wait()


def attend_back(da_all, xn, out_all, saved, tables, w, shard, tokens, busy, dps, lanes, cores):
    q, k, kt, v, o, lse = saved
    cos, sin = tables
    seq, width = q.shape
    model = w.shape[0]
    block = 256
    dma = pltpu.SemaphoreType.DMA
    whole = pl.BlockSpec(memory_space=pltpu.VMEM)
    return pl.pallas_call(
        functools.partial(attend_back_kernel, dps, lanes, cores, busy, block, 1.0 / math.sqrt(HD)),
        in_specs=[ANY] * 3 + [whole] * 9,
        out_specs=[ANY, whole],
        out_shape=[
            jax.ShapeDtypeStruct((lanes, cores, tokens, model), BF),
            jax.ShapeDtypeStruct((dps, lanes * cores, shard, 4 * width), BF),
        ],
        scratch_shapes=[
            pltpu.VMEM((seq, model), BF),
            pltpu.VMEM((seq, 3 * width), BF),
            pltpu.VMEM((model, 3 * width), F32),
            pltpu.VMEM((2, tokens, model), BF),
            pltpu.VMEM((model, width), BF),
            pltpu.VMEM((seq, width), BF),
            pltpu.VMEM((seq, HD), F32),
            pltpu.VMEM((seq, HD), F32),
            dma((2,)),
            dma((2,)),
        ],
        cost_estimate=lasts(50),
        compiler_params=pltpu.CompilerParams(vmem_limit_bytes=VMEM_LIMIT),
    )(da_all, xn, out_all, q, k, kt, v, o, lse, cos, sin, w)


def finish_kernel(
    dps, lanes, cores, busy, part_ref, g_ref, x_ref, gain_ref, dx_ref, wq_ref,
    out_ref, gq_ref, go_ref, one_ref, mix_ref,
    from_core, stage, inbox, from_dp, total_g,
    z_out, z_in, c_out, c_in, g_out, g_in, m_out, m_in, local,
):
    dp, fs, z, c = place(cores)
    fss = lanes * cores
    greet(sequence_peers(dp, fs, fss) + [(lax.rem(dp + m, dps), fs) for m in range(1, dps)])

    def has_next(side):
        return z < lanes - 1 if side == 0 else z > 0

    def over(m):
        t = lax.rem(dp + m, dps)
        return send(g_ref.at[t], from_dp.at[m - 1], g_out.at[m - 1], g_in.at[m - 1], (t, fs))

    def across(m, block):
        t = lax.rem(c + m, cores)
        return send(
            part_ref.at[block, t], from_core.at[m - 1, block], c_out.at[m - 1, block], c_in.at[m - 1, block],
            (dp, z * cores + t),
        )

    def hop(side, step):
        return send(
            stage.at[side, step - 1], inbox.at[side, step - 1], z_out.at[side, step - 1],
            z_in.at[side, step - 1], (dp, fs + (cores if side == 0 else -cores)),
        )

    def home(k, owner):
        t = lax.rem(fs + k, fss)
        return send(total_g.at[t], mix_ref.at[head_slot(owner, lanes, cores)], m_out.at[k - 1], m_in.at[k - 1], (dp, t))

    def goal(side, step):
        block = z + lanes - step if side == 0 else z - lanes + step
        return block, (block >= 0) & (block < lanes)

    def begin(block):
        for m in range(1, cores):
            across(m, block).start()

    def partial_sum(block):
        total = part_ref[block, c].astype(F32)
        for m in range(1, cores):
            across(m, block).wait_recv()
            total = total + from_core[m - 1, block].astype(F32)
        return total

    def advance(step):
        for side in (0, 1):
            block, there = goal(side, step)
            fed = z > 0 if side == 0 else z < lanes - 1

            @pl.when(there)
            def _():
                total = partial_sum(block)
                stage[side, step - 1] = total.astype(BF)
                if step > 1:

                    @pl.when(fed)
                    def _():
                        hop(side, step - 1).wait_recv()
                        stage[side, step - 1] = (total + inbox[side, step - 2].astype(F32)).astype(BF)

                hop(side, step).start()

    for step in range(1, lanes):
        for side in (0, 1):
            block, there = goal(side, step)

            @pl.when(there)
            def _():
                begin(block)

    begin(z)
    for m in range(1, dps):
        over(m).start()
    for step in range(1, max(lanes - 1, 1)):
        advance(step)
    for m in range(1, dps):
        over(m).wait_recv()
    for f in range(fss):
        total = g_ref[dp, f].astype(F32)
        for m in range(1, dps):
            total = total + from_dp[m - 1, f].astype(F32)
        total_g[f] = total.astype(BF)
    keep = pltpu.make_async_copy(total_g.at[fs], mix_ref.at[head_slot(fs, lanes, cores)], local)

    @pl.when(head_slot(fs, lanes, cores) < busy)
    def _():
        for k in range(1, fss):
            home(k, fs).start()
        keep.start()

    if lanes > 1:
        advance(lanes - 1)
    out_ref[...] = partial_sum(z)
    for side in (0, 1):
        fed = z > 0 if side == 0 else z < lanes - 1

        @pl.when(fed)
        def _():
            hop(side, lanes - 1).wait_recv()
            out_ref[...] += inbox[side, lanes - 2].astype(F32)

    for k in range(1, fss):
        owner = lax.rem(fs + fss - k, fss)

        @pl.when(head_slot(owner, lanes, cores) < busy)
        def _():
            home(k, owner).wait_recv()

    @pl.when(head_slot(fs, lanes, cores) < busy)
    def _():
        keep.wait()
        for k in range(1, fss):
            home(k, fs).wait_send()

    model = out_ref.shape[1]
    width = mix_ref.shape[2] // 4
    one = None
    for slot in range(busy):
        lo = slot * width
        wide = min(width, model - lo)
        for p in range(3):
            piece = mix_ref[slot, :, p * width : p * width + wide].astype(F32)
            gq_ref[:, p * model + lo : p * model + lo + wide] = piece
            weight = wq_ref[:, p * model + lo : p * model + lo + wide].astype(F32)
            term = jnp.sum(weight * piece, axis=1, keepdims=True)
            one = term if one is None else one + term
        go_ref[:, lo : lo + wide] = mix_ref[slot, :, 3 * width : 3 * width + wide].astype(F32)
    one_ref[...] = one
    x = x_ref[...].astype(F32)
    inv = lax.rsqrt(jnp.mean(x * x, axis=1, keepdims=True) + norm_eps)
    unit = x * inv
    scaled = out_ref[...] * gain_ref[...]
    out_ref[...] = dx_ref[...] + inv * (scaled - unit * jnp.mean(scaled * unit, axis=1, keepdims=True))
    for step in range(1, lanes):
        for side in (0, 1):
            block, there = goal(side, step)

            @pl.when(there)
            def _():
                hop(side, step).wait_send()

    for m in range(1, cores):
        for block in range(lanes):
            across(m, block).wait_send()
    for m in range(1, dps):
        over(m).wait_send()


def finish(part, g, x, gain, dx, w_qkv, lanes, cores, busy):
    dps, fss = g.shape[:2]
    tokens, model = part.shape[2:]
    dma = pltpu.SemaphoreType.DMA
    hops = (2, max(lanes - 1, 1))
    ways = (max(cores - 1, 1), lanes)
    whole = pl.BlockSpec(memory_space=pltpu.VMEM)
    return pl.pallas_call(
        functools.partial(finish_kernel, dps, lanes, cores, busy),
        in_specs=[whole] * 6,
        out_specs=[whole] * 4,
        out_shape=[
            jax.ShapeDtypeStruct((tokens, model), F32),
            jax.ShapeDtypeStruct(w_qkv.shape, F32),
            jax.ShapeDtypeStruct((w_qkv.shape[0], model), F32),
            jax.ShapeDtypeStruct((w_qkv.shape[0], 1), F32),
        ],
        scratch_shapes=[
            pltpu.VMEM((busy,) + g.shape[2:], BF),
            pltpu.VMEM(ways + (tokens, model), BF),
            pltpu.VMEM(hops + (tokens, model), BF),
            pltpu.VMEM(hops + (tokens, model), BF),
            pltpu.VMEM((dps - 1,) + g.shape[1:], BF),
            pltpu.VMEM(g.shape[1:], BF),
            dma(hops), dma(hops), dma(ways), dma(ways), dma((dps - 1,)), dma((dps - 1,)),
            dma((fss - 1,)), dma((fss - 1,)), dma,
        ],
        cost_estimate=lasts(66),
        compiler_params=pltpu.CompilerParams(
            collective_id=6, has_side_effects=True, vmem_limit_bytes=VMEM_LIMIT
        ),
    )(part, g, x, gain, dx, w_qkv)


def per_device(x, w_qkv, w_out, w_shared, w_experts, gains, routes, gates, d_out):
    tokens, model = x.shape
    hidden = w_shared.shape[1] // 3
    experts, shard = w_experts.shape[:2]
    dps, fss = lax.axis_size("dp"), lax.axis_size("fsdp")
    cores = dps * fss // experts
    lanes = fss // cores
    seq = tokens * fss
    slots = tokens // 2
    per = -(-HEADS // fss)
    busy = -(-HEADS // per)
    width = per * HD
    dp, fs = lax.axis_index("dp"), lax.axis_index("fsdp")
    z, c = fs // cores, fs % cores

    def over_z(value, pairs):
        return lax.ppermute(
            value, "fsdp", [(a * cores + k, b * cores + k) for a, b in pairs for k in range(cores)]
        )

    cut = w_qkv.reshape(shard, 3, HEADS, HD)
    cut = jnp.pad(cut, ((0, 0), (0, 0), (0, fss * per - HEADS), (0, 0)))
    cut = cut.reshape(shard, 3, cores, lanes, width).transpose(3, 2, 0, 1, 4).reshape(fss, shard, 3 * width)
    wide_gains = jnp.pad(gains, ((0, 0), (0, HD - 2)))
    topk = routes.shape[1]
    table = jnp.concatenate([routes.T.astype(F32), gates.T], axis=0)
    table = jnp.pad(table, ((0, -2 * topk % 8), (0, 0)))
    x_all, slabs, tables, out_all, gains_all, picks, weigh = start(
        x, cut, table, w_out, wide_gains, topk, busy, dps, lanes, cores
    )
    x_all = x_all.reshape(seq, model)
    slabs = slabs.reshape(model, 3 * width)
    out_all = out_all.reshape(model, model)
    gain_rows = gains_all.reshape(model, HD)[:, :2].astype(F32).T
    w_heads = slabs
    gain_one, gain_two = gain_rows[0:1], gain_rows[1:2]

    half = HD // 2
    frequency = np.float32(10000.0) ** (-np.arange(half, dtype=np.float32) / np.float32(half))
    angles = np.arange(seq, dtype=np.float32)[:, None] * frequency[None, :]
    cosine, sine = np.cos(angles), np.sin(angles)
    cos = jnp.asarray(np.concatenate([cosine, cosine], axis=1), F32)
    sin = jnp.asarray(np.concatenate([-sine, sine], axis=1), F32)

    xn_one, q, k, v, kt, vt, o, lse, heads, shared_all, rows_here, rows_low = attend(
        x_all, gain_one, w_heads, cos, sin, w_experts, w_shared, tokens, busy, dps, lanes, cores
    )
    heads = heads[:, :model]
    shared_all = shared_all.reshape(model, 3 * hidden)

    middle = x.astype(F32) + dot_nt(heads, out_all)
    inv_two = lax.rsqrt(jnp.mean(middle * middle, axis=1, keepdims=True) + norm_eps)
    unit_two = middle * inv_two
    xn_two = (unit_two * gain_two).astype(BF)

    x_slots, c_slots, w_own, w_down, dx_shared, f_shared, g_core = dispatch(
        xn_two, d_out, tables, picks, rows_here, rows_low, shared_all, topk, lanes, cores
    )
    x_slots = x_slots.reshape(-1, model)
    c_slots = c_slots.reshape(-1, model)
    w_own = w_own.reshape(model, 2 * hidden)
    w_down = w_down.reshape(model, hidden)
    dx_slots, gu_slots, hid_slots, g_line = expert(x_slots, c_slots, w_own, w_down, g_core, cores)

    shape = (dps, lanes, slots, model)
    dx_routed, f_slots, g_shared = combine(
        dx_slots.reshape(shape), picks, hid_slots, w_down, g_line, lanes, cores
    )
    dxn_two = dx_shared + dx_routed
    scaled = dxn_two * gain_two
    dx_two = d_out.astype(F32) + inv_two * (
        scaled - unit_two * jnp.mean(scaled * unit_two, axis=1, keepdims=True)
    )
    d_attn = dx_two.astype(BF)

    da_all, routed, g_own = turn(
        d_attn, f_slots, weigh, (x_slots, c_slots), (gu_slots, hid_slots), shard, lanes, cores
    )
    da_all = da_all.reshape(seq, model)
    layer_out = (middle + f_shared + routed).astype(BF)
    dxn_part, g_part = attend_back(
        da_all, xn_one, out_all, (q, k, kt, v, o, lse), (cos, sin), w_heads, shard,
        tokens, busy, dps, lanes, cores,
    )
    d_x, g_qkv, g_out, one = finish(
        dxn_part, g_part, x, gain_one, dx_two, w_qkv, lanes, cores, busy
    )

    groups = [[e * cores + k for e in range(experts)] for k in range(cores)]
    g_experts = lax.all_to_all(
        g_own, ("dp", "fsdp"), split_axis=0, concat_axis=0, tiled=True, axis_index_groups=groups
    ).astype(F32)

    two = jnp.sum(w_shared[:, : 2 * hidden].astype(F32) * g_shared[:, : 2 * hidden], axis=1)
    two = two + jnp.sum(
        w_experts[:, :, : 2 * hidden].astype(F32) * g_experts[:, :, : 2 * hidden], axis=(0, 2)
    )
    g_gains = jnp.concatenate([one, two[:, None]], axis=1) / gains.astype(F32)
    return (layer_out, d_x, g_qkv, g_out, g_shared, g_experts, g_gains)


def solution(mesh):
    rows = P(("dp", "fsdp"), None)
    cube = P(None, ("dp", "fsdp"), None)
    return jax.shard_map(
        per_device,
        mesh=mesh,
        in_specs=(rows, rows, rows, rows, cube, rows, rows, rows, rows),
        out_specs=(rows, rows, rows, rows, rows, cube, rows),
        check_vma=False,
    )
```

```python
import functools
import math

import jax
import jax.numpy as jnp
import numpy as np
from jax import lax
from jax.experimental import pallas as pl
from jax.experimental.pallas import tpu as pltpu
from jax.sharding import PartitionSpec as P

HEADS = 10
HD = 128
norm_eps = 1e-06
masked_score = -1000000000.0
BF = jnp.bfloat16
F32 = jnp.float32
VMEM_LIMIT = 60 * 2**20


def dot_nn(a, b):
    return lax.dot_general(a, b, (((1,), (0,)), ((), ())), preferred_element_type=F32)


def dot_nt(a, b):
    return lax.dot_general(a, b, (((1,), (1,)), ((), ())), preferred_element_type=F32)


def dot_tn(a, b):
    return lax.dot_general(a, b, (((0,), (0,)), ((), ())), preferred_element_type=F32)


def lasts(us):
    return pl.CostEstimate(flops=0, bytes_accessed=int(us * 3.6e6), transcendentals=0)


def causal(rows):
    shape = (rows, rows)
    key = lax.broadcasted_iota(jnp.int32, shape, 0)
    query = lax.broadcasted_iota(jnp.int32, shape, 1)
    return key <= query


def unrotate(g, cos, sin):
    return g * cos - pltpu.roll(g, HD // 2, 1) * sin


def feed(x, c, w_ref, down_ref, hidden):
    gate = dot_nn(x, w_ref[:, :hidden])
    up = dot_nn(x, w_ref[:, hidden : 2 * hidden])
    down = dot_nn(c, down_ref[...])
    sig = 1.0 / (1.0 + jnp.exp(-gate))
    act = gate * sig
    dup = (down * act).astype(BF)
    dgate = (down * up * sig * (1.0 + gate * (1.0 - sig))).astype(BF)
    dx = dot_nt(dgate, w_ref[:, :hidden]) + dot_nt(dup, w_ref[:, hidden : 2 * hidden])
    return dx, dgate, dup, (act * up).astype(BF)


MESH = pl.DeviceIdType.MESH
ANY = pl.BlockSpec(memory_space=pl.ANY)


def place(cores):
    dp, fs = lax.axis_index("dp"), lax.axis_index("fsdp")
    return dp, fs, fs // cores, fs % cores


def greet(peers):
    barrier = pltpu.get_barrier_semaphore()
    for peer in peers:
        pl.semaphore_signal(barrier, inc=1, device_id=peer, device_id_type=MESH)
    pl.semaphore_wait(barrier, len(peers))


def head_slot(f, lanes, cores):
    return lax.rem(f, cores) * lanes + f // cores


def sequence_peers(dp, fs, fss):
    return [(dp, lax.rem(fs + k, fss)) for k in range(1, fss)]


def send(source, target, out, came, peer):
    return pltpu.make_async_remote_copy(
        src_ref=source, dst_ref=target, send_sem=out, recv_sem=came, device_id=peer, device_id_type=MESH
    )


class Chain:
    def __init__(self, own, full, lanes, cores, sems):
        self.own, self.full, self.lanes, self.cores = own, full, lanes, cores
        self.z_out, self.z_in, self.c_out, self.c_in, self.local = sems
        self.dp, self.fs, self.z, self.c = place(cores)

    def hop(self, side, step, block):
        by = self.cores if side == 0 else -self.cores
        source = self.own if step == 0 else self.full.at[block, self.c]
        return send(
            source, self.full.at[block, self.c], self.z_out.at[side, step], self.z_in.at[side, step],
            (self.dp, self.fs + by),
        )

    def across(self, m, block, source, core):
        return send(
            source, self.full.at[block, core], self.c_out.at[m - 1, block], self.c_in.at[m - 1, block],
            (self.dp, self.z * self.cores + lax.rem(self.c + m, self.cores)),
        )

    def keep(self):
        return pltpu.make_async_copy(self.own, self.full.at[self.z, self.c], self.local)

    def has_next(self, side):
        return self.z < self.lanes - 1 if side == 0 else self.z > 0

    def begin(self):
        for side in (0, 1):

            @pl.when(self.has_next(side))
            def _():
                self.hop(side, 0, self.z).start()

        for m in range(1, self.cores):
            self.across(m, self.z, self.own, self.c).start()
        self.keep().start()

    def came(self, side, step):
        block = self.z - step if side == 0 else self.z + step
        return block, (block >= 0) & (block < self.lanes)

    def advance(self, step):
        for side in (0, 1):
            block, there = self.came(side, step)

            @pl.when(there)
            def _():
                self.hop(side, step - 1, block).wait_recv()

            @pl.when(there & self.has_next(side))
            def _():
                self.hop(side, step, block).start()

            @pl.when(there)
            def _():
                for m in range(1, self.cores):
                    self.across(m, block, self.full.at[block, self.c], self.c).start()

    def finish(self):
        self.keep().wait()
        for m in range(1, self.cores):
            for block in range(self.lanes):
                self.across(m, block, self.own, lax.rem(self.c + self.cores - m, self.cores)).wait_recv()
        for side in (0, 1):
            for step in range(self.lanes - 1):
                block, there = self.came(side, step)

                @pl.when(there & self.has_next(side))
                def _():
                    self.hop(side, step, block).wait_send()

        for m in range(1, self.cores):
            for block in range(self.lanes):
                self.across(m, block, self.own, self.c).wait_send()


def chain_sems(lanes, cores):
    dma = pltpu.SemaphoreType.DMA
    hops = (2, max(lanes - 1, 1))
    ways = (max(cores - 1, 1), lanes)
    return [dma(hops), dma(hops), dma(ways), dma(ways), dma]


class Line:
    def __init__(self, own, buffer, lanes, cores, out, came):
        self.own, self.buffer, self.lanes, self.cores = own, buffer, lanes, cores
        self.out, self.into = out, came
        self.dp, self.fs, self.z, self.c = place(cores)

    def has_next(self, side):
        return self.z < self.lanes - 1 if side == 0 else self.z > 0

    def near(self, side):
        return (self.dp, self.fs + (self.cores if side == 0 else -self.cores))

    def hop(self, side, step, block):
        source = self.own if step == 0 else self.buffer.at[block]
        return send(
            source, self.buffer.at[block], self.out.at[side, step], self.into.at[side, step], self.near(side)
        )

    def begin(self):
        for side in (0, 1):

            @pl.when(self.has_next(side))
            def _():
                self.hop(side, 0, self.z).start()

    def came(self, side, step):
        block = self.z - step if side == 0 else self.z + step
        return block, (block >= 0) & (block < self.lanes)

    def advance(self, step, then):
        for side in (0, 1):
            block, there = self.came(side, step)

            @pl.when(there)
            def _():
                self.hop(side, step - 1, block).wait_recv()

            @pl.when(there & self.has_next(side))
            def _():
                self.hop(side, step, block).start()

            @pl.when(there)
            def _():
                then(block, self.buffer.at[block])

    def finish(self):
        for step in range(self.lanes - 1):
            for side in (0, 1):
                block, there = self.came(side, step)

                @pl.when(there & self.has_next(side))
                def _():
                    self.hop(side, step, block).wait_send()


class Spread:
    def __init__(self, stage, target, dps, lanes, cores, out, came, local):
        self.stage, self.target, self.dps, self.lanes = stage, target, dps, lanes
        self.out, self.into, self.local = out, came, local
        self.dp, self.fs, self.z, self.c = place(cores)

    def over(self, m, block):
        return send(
            self.stage.at[m, block], self.target.at[m, block], self.out.at[m - 1, block],
            self.into.at[m - 1, block], (lax.rem(self.dp + m, self.dps), self.fs),
        )

    def keep(self, block):
        return pltpu.make_async_copy(
            self.stage.at[0, block], self.target.at[0, block], self.local.at[block]
        )

    def go(self, m, block):
        if m:
            self.over(m, block).start()
        else:
            self.keep(block).start()

    def order(self):
        return list(range(1, self.dps)) + [0]

    def finish(self):
        for block in range(self.lanes):
            self.keep(block).wait()
            for m in range(1, self.dps):
                self.over(m, block).wait_recv()
        for block in range(self.lanes):
            for m in range(1, self.dps):
                self.over(m, block).wait_send()


class Rows:
    def __init__(self, own, full, dps, lanes, cores, sems):
        self.own, self.full, self.dps, self.lanes, self.cores = own, full, dps, lanes, cores
        self.z_out, self.z_in, self.d_out, self.d_in, self.c_out, self.c_in, self.local = sems
        self.dp, self.fs, self.z, self.c = place(cores)

    def along(self, k):
        t = lax.rem(self.z + k, self.lanes) * self.cores + self.c
        return send(
            self.own, self.full.at[self.dp, self.z, self.c], self.z_out.at[k - 1], self.z_in.at[k - 1],
            (self.dp, t),
        )

    def over(self, m, block):
        piece = self.full.at[block, :, self.c]
        return send(
            piece, piece, self.d_out.at[m - 1], self.d_in.at[m - 1], (lax.rem(self.dp + m, self.dps), self.fs)
        )

    def across(self, m, core):
        piece = self.full.at[:, :, core]
        peer = (self.dp, self.z * self.cores + lax.rem(self.c + m, self.cores))
        return send(piece, piece, self.c_out.at[m - 1], self.c_in.at[m - 1], peer)

    def keep(self):
        return pltpu.make_async_copy(self.own, self.full.at[self.dp, self.z, self.c], self.local)

    def begin(self):
        for k in range(1, self.lanes):
            self.along(k).start()
        self.keep().start()

    def to_dp(self):
        self.keep().wait()
        for k in range(1, self.lanes):
            self.along(k).wait_recv()
        for m in range(1, self.dps):
            self.over(m, self.dp).start()

    def to_cores(self):
        for m in range(1, self.dps):
            self.over(m, lax.rem(self.dp + self.dps - m, self.dps)).wait_recv()
        for m in range(1, self.cores):
            self.across(m, self.c).start()

    def finish(self):
        for m in range(1, self.cores):
            self.across(m, lax.rem(self.c + self.cores - m, self.cores)).wait_recv()
        for k in range(1, self.lanes):
            self.along(k).wait_send()
        for m in range(1, self.dps):
            self.over(m, self.dp).wait_send()
        for m in range(1, self.cores):
            self.across(m, self.c).wait_send()


def pair(n):
    return [pltpu.SemaphoreType.DMA((max(n - 1, 1),)) for _ in range(2)]


def rows_sems(dps, lanes, cores):
    return pair(lanes) + pair(dps) + pair(cores) + [pltpu.SemaphoreType.DMA]


def start_kernel(
    dps, lanes, cores, topk, busy, x_ref, wh_ref, tab_ref, wo_ref, gn_ref,
    full_ref, heads_ref, tabs_ref, out_ref, gains_ref, pick_ref, weigh_ref,
    h_out, h_in, hd_out, hd_in, t_out, t_in, locals_, *sems,
):
    rows = Rows(wo_ref, out_ref, dps, lanes, cores, sems[:7])
    gains = Rows(gn_ref, gains_ref, dps, lanes, cores, sems[7:14])
    chain = Chain(x_ref, full_ref, lanes, cores, sems[14:])
    dp, fs, z, c = chain.dp, chain.fs, chain.z, chain.c
    fss = lanes * cores
    slots, tokens = pick_ref.shape[2:]
    greet(sequence_peers(dp, fs, fss) + [(lax.rem(dp + m, dps), fs) for m in range(1, dps)])
    chain.begin()
    kept = [
        pltpu.make_async_copy(wh_ref.at[fs], heads_ref.at[dp, fs], locals_.at[0]),
        pltpu.make_async_copy(tab_ref, tabs_ref.at[z], locals_.at[1]),
    ]
    for copy in kept:
        copy.start()

    def heads_to(k):
        t = lax.rem(fs + k, fss)
        return send(wh_ref.at[t], heads_ref.at[dp, fs], h_out.at[k - 1], h_in.at[k - 1], (dp, t))

    def table_to(k):
        t = lax.rem(z + k, lanes) * cores + c
        return send(tab_ref, tabs_ref.at[z], t_out.at[k - 1], t_in.at[k - 1], (dp, t))

    def heads_over(m, block):
        return send(
            heads_ref.at[block], heads_ref.at[block], hd_out.at[m - 1], hd_in.at[m - 1],
            (lax.rem(dp + m, dps), fs),
        )

    mine = head_slot(fs, lanes, cores) < busy
    for k in range(1, fss):

        @pl.when(head_slot(lax.rem(fs + k, fss), lanes, cores) < busy)
        def _():
            heads_to(k).start()

    for k in range(1, lanes):
        table_to(k).start()
    gains.begin()
    rows.begin()
    for copy in kept:
        copy.wait()
    if lanes > 1:
        chain.advance(1)
    @pl.when(mine)
    def _():
        for k in range(1, fss):
            heads_to(k).wait_recv()
        for m in range(1, dps):
            heads_over(m, dp).start()

    gains.to_dp()
    rows.to_dp()
    for step in range(2, lanes):
        chain.advance(step)
    for k in range(1, lanes):
        table_to(k).wait_recv()

    triangle = (
        lax.broadcasted_iota(jnp.int32, (tokens, tokens), 0)
        <= lax.broadcasted_iota(jnp.int32, (tokens, tokens), 1)
    ).astype(BF)
    slot = lax.broadcasted_iota(jnp.int32, (slots, tokens), 0).astype(F32)
    for m in range(dps):
        name = (lax.rem(dp + m, dps) * lanes + z).astype(F32)
        for block in range(lanes):
            hit = tabs_ref[block, :topk, :] == name
            member = jnp.max(jnp.where(hit, 1.0, 0.0), axis=0, keepdims=True)
            gate = jnp.sum(jnp.where(hit, tabs_ref[block, topk : 2 * topk, :], 0.0), axis=0, keepdims=True)
            rank = dot_nn(jnp.broadcast_to(member, (8, tokens)).astype(BF), triangle)[:1] - 1.0
            match = (rank == slot) & (member > 0.5)
            pick_ref[m, block] = jnp.where(match, 1.0, 0.0).astype(BF)
            weigh_ref[m, block] = jnp.where(match, gate, 0.0).astype(BF)

    gains.to_cores()
    rows.to_cores()
    chain.finish()
    gains.finish()
    rows.finish()
    for k in range(1, fss):

        @pl.when(head_slot(lax.rem(fs + k, fss), lanes, cores) < busy)
        def _():
            heads_to(k).wait_send()

    for k in range(1, lanes):
        table_to(k).wait_send()

    @pl.when(mine)
    def _():
        for m in range(1, dps):
            heads_over(m, lax.rem(dp + dps - m, dps)).wait_recv()
            heads_over(m, dp).wait_send()


def start(x, wh, table, w_out, gains, topk, busy, dps, lanes, cores):
    fss = lanes * cores
    tokens = x.shape[0]
    dma = pltpu.SemaphoreType.DMA
    whole = pl.BlockSpec(memory_space=pltpu.VMEM)
    picks = jax.ShapeDtypeStruct((dps, lanes, tokens // 2, tokens), BF)
    shapes = [
        jax.ShapeDtypeStruct((lanes, cores) + x.shape, x.dtype),
        jax.ShapeDtypeStruct((dps,) + wh.shape, wh.dtype),
        jax.ShapeDtypeStruct((lanes,) + table.shape, table.dtype),
        jax.ShapeDtypeStruct((dps, lanes, cores) + w_out.shape, w_out.dtype),
        jax.ShapeDtypeStruct((dps, lanes, cores) + gains.shape, gains.dtype),
        picks,
        picks,
    ]
    return pl.pallas_call(
        functools.partial(start_kernel, dps, lanes, cores, topk, busy),
        in_specs=[ANY] * 5,
        out_specs=[ANY, ANY, whole, ANY, ANY, whole, whole],
        out_shape=shapes,
        scratch_shapes=pair(fss) + pair(dps) + pair(lanes) + [dma((2,))]
        + rows_sems(dps, lanes, cores) * 2 + chain_sems(lanes, cores),
        cost_estimate=lasts(70),
        compiler_params=pltpu.CompilerParams(
            collective_id=0, has_side_effects=True, vmem_limit_bytes=VMEM_LIMIT
        ),
    )(x, wh, table, w_out, gains)


class Slabs:
    def __init__(self, source, columns, target, dps, lanes, cores, sems):
        self.source, self.columns, self.target = source, columns, target
        self.lanes, self.cores, self.experts = lanes, cores, dps * lanes
        self.out, self.came, self.local = sems
        self.dp, self.fs, self.z, self.c = place(cores)
        self.me = self.dp * lanes + self.z

    def peer(self, k):
        e = lax.rem(self.me + k, self.experts)
        return (e // self.lanes, lax.rem(e, self.lanes) * self.cores + self.c)

    def to(self, k):
        e = lax.rem(self.me + k, self.experts)
        return send(
            self.source.at[e, :, self.columns], self.target.at[self.dp, self.z], self.out.at[k - 1],
            self.came.at[k - 1], self.peer(k),
        )

    def keep(self):
        return pltpu.make_async_copy(
            self.source.at[self.me, :, self.columns], self.target.at[self.dp, self.z], self.local
        )

    def begin(self):
        for k in range(1, self.experts):
            self.to(k).start()
        self.keep().start()

    def arrive(self):
        self.keep().wait()
        for k in range(1, self.experts):
            self.to(k).wait_recv()

    def finish(self):
        for k in range(1, self.experts):
            self.to(k).wait_send()


def slab_sems(experts):
    return pair(experts) + [pltpu.SemaphoreType.DMA]


def layer_peers(slabs):
    others = [
        (slabs.dp, lax.rem(slabs.z + a, slabs.lanes) * slabs.cores + lax.rem(slabs.c + m, slabs.cores))
        for a in range(slabs.lanes)
        for m in range(1, slabs.cores)
    ]
    return [slabs.peer(k) for k in range(1, slabs.experts)] + others


def attend_kernel(
    dps, lanes, cores, busy, block, scale,
    x_ref, gain_ref, w_ref, cos_ref, sin_ref, we_ref, sh_ref,
    xn_ref, q_ref, k_ref, v_ref, kt_ref, vt_ref, o_ref, lse_ref, mix_ref, all_ref, rows_ref, low_ref,
    out, came, local, *sems,
):
    dp, fs, z, c = place(cores)
    fss = lanes * cores
    tokens, width = mix_ref.shape[0], o_ref.shape[1]
    seq = x_ref.shape[0]
    up_width, low_width = rows_ref.shape[3], low_ref.shape[3]
    slabs = Slabs(we_ref, pl.ds(0, up_width), rows_ref, dps, lanes, cores, sems[:3])
    low_slabs = Slabs(we_ref, pl.ds(up_width, low_width), low_ref, dps, lanes, cores, sems[3:6])
    shared = Rows(sh_ref, all_ref, dps, lanes, cores, sems[6:])
    greet(layer_peers(slabs))
    shared.begin()
    slabs.begin()

    def project(i, carry):
        rows = pl.ds(pl.multiple_of(i * block, block), block)
        x = x_ref[rows, :].astype(F32)
        inv = lax.rsqrt(jnp.mean(x * x, axis=1, keepdims=True) + norm_eps)
        xn = (x * inv * gain_ref[...]).astype(BF)
        xn_ref[rows, :] = xn
        cos, sin = cos_ref[rows, :], sin_ref[rows, :]
        for part in range(3):
            wide = dot_nn(xn, w_ref[:, part * width : (part + 1) * width])
            for head in range(width // HD):
                cols = slice(head * HD, (head + 1) * HD)
                u = wide[:, cols]
                if part < 2:
                    u = u * cos + pltpu.roll(u, HD // 2, 1) * sin
                low = u.astype(BF)
                if part == 0:
                    q_ref[rows, cols] = low
                elif part == 1:
                    k_ref[rows, cols] = low
                    kt_ref[cols, rows] = u.T.astype(BF)
                else:
                    v_ref[rows, cols] = low
                    vt_ref[cols, rows] = u.T.astype(BF)
        return carry

    mine = head_slot(fs, lanes, cores) < busy

    @pl.when(mine)
    def _():
        lax.fori_loop(0, seq // block, project, 0)

    shared.to_dp()

    def head_rows(h, carry):
        cols = pl.ds(pl.multiple_of(h * HD, HD), HD)
        for j in range(seq // block):
            whole = j * block
            here = slice(whole, whole + block)
            q = q_ref[here, cols]
            tail = dot_nt(k_ref[here, cols], q) * scale
            tail = jnp.where(causal(block), tail, masked_score)
            top = jnp.max(tail, axis=0, keepdims=True)
            if j:
                front = dot_nt(k_ref[:whole, cols], q) * scale
                top = jnp.maximum(top, jnp.max(front, axis=0, keepdims=True))
            tail = jnp.exp(tail - top)
            total = jnp.sum(tail, axis=0, keepdims=True)
            mixed = dot_nn(vt_ref[cols, here], tail.astype(BF))
            if j:
                front = jnp.exp(front - top)
                total = total + jnp.sum(front, axis=0, keepdims=True)
                mixed = mixed + dot_nn(vt_ref[cols, :whole], front.astype(BF))
            o_ref[here, cols] = (mixed / total).T.astype(BF)
            lse_ref[h, :, here] = top + jnp.log(total)
        return carry

    @pl.when(mine)
    def _():
        lax.fori_loop(0, width // HD, head_rows, 0)

    def columns(f):
        slot = head_slot(f, lanes, cores)
        return mix_ref.at[:, pl.ds(pl.multiple_of(slot * width, HD), width)]

    def rows(f):
        return o_ref.at[pl.ds(pl.multiple_of(f * tokens, tokens), tokens), :]

    def to(k, owner):
        t = lax.rem(fs + k, fss)
        return send(rows(t), columns(owner), out.at[k - 1], came.at[k - 1], (dp, t))

    keep = pltpu.make_async_copy(rows(fs), columns(fs), local)

    @pl.when(head_slot(fs, lanes, cores) < busy)
    def _():
        for k in range(1, fss):
            to(k, fs).start()
        keep.start()

    low_slabs.begin()
    shared.to_cores()
    for k in range(1, fss):
        owner = lax.rem(fs + fss - k, fss)

        @pl.when(head_slot(owner, lanes, cores) < busy)
        def _():
            to(k, owner).wait_recv()

    @pl.when(head_slot(fs, lanes, cores) < busy)
    def _():
        keep.wait()
        for k in range(1, fss):
            to(k, fs).wait_send()

    shared.finish()
    slabs.arrive()
    slabs.finish()
    low_slabs.arrive()
    low_slabs.finish()


def attend(x_all, gain, w, cos, sin, w_experts, w_shared, tokens, busy, dps, lanes, cores):
    seq, model = x_all.shape
    width = w.shape[1] // 3
    experts, shard, thrice = w_experts.shape
    block = seq // 8
    fss = lanes * cores
    dma = pltpu.SemaphoreType.DMA
    whole = pl.BlockSpec(memory_space=pltpu.VMEM)
    flat = jax.ShapeDtypeStruct((seq, width), BF)
    turned = jax.ShapeDtypeStruct((width, seq), BF)
    return pl.pallas_call(
        functools.partial(attend_kernel, dps, lanes, cores, busy, block, 1.0 / math.sqrt(HD)),
        in_specs=[whole] * 5 + [ANY, ANY],
        out_specs=[whole] * 8 + [ANY] * 4,
        out_shape=[
            jax.ShapeDtypeStruct((seq, model), BF),
            flat, flat, flat, turned, turned, flat,
            jax.ShapeDtypeStruct((width // HD, 1, seq), F32),
            jax.ShapeDtypeStruct((tokens, busy * width), BF),
            jax.ShapeDtypeStruct((dps, lanes, cores) + w_shared.shape, BF),
            jax.ShapeDtypeStruct((dps, lanes, shard, thrice // 3 * 2), BF),
            jax.ShapeDtypeStruct((dps, lanes, shard, thrice // 3), BF),
        ],
        scratch_shapes=[dma((fss - 1,)), dma((fss - 1,)), dma]
        + slab_sems(experts) * 2 + rows_sems(dps, lanes, cores),
        cost_estimate=lasts(100),
        compiler_params=pltpu.CompilerParams(
            collective_id=2, has_side_effects=True, vmem_limit_bytes=VMEM_LIMIT
        ),
    )(x_all, gain, w, cos, sin, w_experts, w_shared)


def greet_cross(line, dps, cores=1):
    barrier = pltpu.get_barrier_semaphore()
    for m in range(1, dps):
        peer = (lax.rem(line.dp + m, dps), line.fs)
        pl.semaphore_signal(barrier, inc=1, device_id=peer, device_id_type=MESH)
    for side in (0, 1):

        @pl.when(line.has_next(side))
        def _():
            pl.semaphore_signal(barrier, inc=1, device_id=line.near(side), device_id_type=MESH)

    for m in range(1, cores):
        peer = (line.dp, line.z * cores + lax.rem(line.c + m, cores))
        pl.semaphore_signal(barrier, inc=1, device_id=peer, device_id_type=MESH)
    ends = line.has_next(0).astype(jnp.int32) + line.has_next(1).astype(jnp.int32)
    pl.semaphore_wait(barrier, dps - 1 + cores - 1 + ends)


class CoreSum:
    def __init__(self, source, own, scratch, dps, lanes, cores):
        self.source, self.own = source, own
        self.from_core, self.out, self.came = scratch
        self.dps, self.lanes, self.cores = dps, lanes, cores
        self.dp, self.fs, self.z, self.c = place(cores)

    def across(self, m):
        t = lax.rem(self.c + m, self.cores)
        return send(
            self.source.at[t], self.from_core.at[m - 1], self.out.at[m - 1], self.came.at[m - 1],
            (self.dp, self.z * self.cores + t),
        )

    def begin(self):
        for m in range(1, self.cores):
            self.across(m).start()

    def finish(self):
        for m in range(1, self.cores):
            self.across(m).wait_recv()

        def add(i, carry):
            p, q = i // self.lanes, lax.rem(i, self.lanes)
            total = self.source[self.c, p, q].astype(F32)
            for m in range(1, self.cores):
                total = total + self.from_core[m - 1, p, q].astype(F32)
            self.own[p, q] = total.astype(BF)
            return carry

        lax.fori_loop(0, self.dps * self.lanes, add, 0)
        for m in range(1, self.cores):
            self.across(m).wait_send()


def dispatch_kernel(
    dps, lanes, cores, topk, x_ref, up_ref, tabs_ref, pick_ref, rows_ref, low_ref, shared_ref,
    out_ref, c_ref, w_ref, wd_ref, dx_ref, f_ref, own_ref, g_ref, acts, acc, buffer, stage, up_buffer, up_stage, l_out, l_in, s_out, s_in, s_local,
    ul_out, ul_in, us_out, us_in, us_local, w_out, w_in, w_local, wd_out, wd_in, wd_local, *core,
):
    line = Line(x_ref, buffer, lanes, cores, l_out, l_in)
    spread = Spread(stage, out_ref, dps, lanes, cores, s_out, s_in, s_local)
    up_line = Line(up_ref, up_buffer, lanes, cores, ul_out, ul_in)
    up_spread = Spread(up_stage, c_ref, dps, lanes, cores, us_out, us_in, us_local)
    hidden = shared_ref.shape[1] // 3
    greet_cross(line, dps, cores)

    def across(m, core):
        peer = (line.dp, line.z * cores + lax.rem(line.c + m, cores))
        return send(rows_ref, w_ref.at[:, :, core], w_out.at[m - 1], w_in.at[m - 1], peer)

    def across_down(m, core):
        peer = (line.dp, line.z * cores + lax.rem(line.c + m, cores))
        return send(low_ref, wd_ref.at[:, :, core], wd_out.at[m - 1], wd_in.at[m - 1], peer)

    keep = pltpu.make_async_copy(rows_ref, w_ref.at[:, :, line.c], w_local)
    keep_down = pltpu.make_async_copy(low_ref, wd_ref.at[:, :, line.c], wd_local)

    def pick(block, source):
        for m in spread.order():
            stage[m, block] = dot_nn(pick_ref[m, block], source[...]).astype(BF)
            spread.go(m, block)

    def up_pick(block, source):
        for m in up_spread.order():
            name = (lax.rem(line.dp + m, dps) * lanes + line.z).astype(F32)
            hit = tabs_ref[block, :topk, :] == name
            gate = jnp.sum(jnp.where(hit, tabs_ref[block, topk : 2 * topk, :], 0.0), axis=0, keepdims=True)
            one = pick_ref[m, block]
            scale = jnp.sum(one.astype(F32) * gate, axis=1, keepdims=True)
            up_stage[m, block] = (dot_nn(one, source[...]) * scale).astype(BF)
            up_spread.go(m, block)

    line.begin()
    pick(line.z, x_ref)
    up_line.begin()
    up_pick(line.z, up_ref)
    keep.start()
    keep_down.start()
    for m in range(1, cores):
        across(m, line.c).start()
        across_down(m, line.c).start()
    experts, shard = dps * lanes, g_ref.shape[3]
    summed = CoreSum(g_ref, own_ref, core, dps, lanes, cores)

    def shared_forward():
        down_ref = shared_ref.at[:, 2 * hidden :]
        dx, gate, up, hid = feed(x_ref[...], up_ref[...], shared_ref, down_ref, hidden)
        dx_ref[...] = dx
        acts[0] = gate
        acts[1] = up
        acts[2] = hid
        f_ref[...] = dot_nt(hid, down_ref[...])

    def shared_gradient(third):
        acc[...] = dot_tn((x_ref if third < 2 else up_ref)[...], acts[third])
        for e in range(experts):
            for k in range(cores):
                row = (e * cores + k) * shard
                piece = acc[row : row + shard, :].astype(BF)
                g_ref[k, e // lanes, e % lanes, :, third * hidden : (third + 1) * hidden] = piece
        if third == 2:
            summed.begin()

    work = [shared_forward] + [functools.partial(shared_gradient, third) for third in range(3)]
    for step in range(1, lanes):
        line.advance(step, pick)
        up_line.advance(step, up_pick)
        work.pop(0)()
    for left in work:
        left()
    spread.finish()
    line.finish()
    up_spread.finish()
    up_line.finish()
    summed.finish()
    keep.wait()
    keep_down.wait()
    for m in range(1, cores):
        across(m, lax.rem(line.c + cores - m, cores)).wait_recv()
        across(m, line.c).wait_send()
        across_down(m, lax.rem(line.c + cores - m, cores)).wait_recv()
        across_down(m, line.c).wait_send()


def dispatch(x, upstream, tables, picks, rows, low, shared, topk, lanes, cores):
    dps, _, slots, tokens = picks.shape
    model = x.shape[1]
    shard, hidden = low.shape[2:]
    dma = pltpu.SemaphoreType.DMA
    hops = (2, max(lanes - 1, 1))
    ways = (dps - 1, lanes)
    whole = pl.BlockSpec(memory_space=pltpu.VMEM)
    buffers = [pltpu.VMEM((lanes, tokens, model), BF), pltpu.VMEM((dps, lanes, slots, model), BF)]
    moves = [dma(hops), dma(hops), dma(ways), dma(ways), dma((lanes,))]
    return pl.pallas_call(
        functools.partial(dispatch_kernel, dps, lanes, cores, topk),
        in_specs=[whole] * 4 + [ANY, ANY, whole],
        out_specs=[ANY] * 4 + [whole] * 3,
        out_shape=[
            jax.ShapeDtypeStruct((dps, lanes, slots, model), BF),
            jax.ShapeDtypeStruct((dps, lanes, slots, model), BF),
            jax.ShapeDtypeStruct((dps, lanes, cores) + rows.shape[2:], BF),
            jax.ShapeDtypeStruct((dps, lanes, cores, shard, hidden), BF),
            jax.ShapeDtypeStruct((tokens, model), F32),
            jax.ShapeDtypeStruct((tokens, model), F32),
            jax.ShapeDtypeStruct((dps, lanes, shard, 3 * hidden), BF),
        ],
        scratch_shapes=[
            pltpu.VMEM((cores, dps, lanes, shard, 3 * hidden), BF),
            pltpu.VMEM((3, tokens, shared.shape[1] // 3), BF),
            pltpu.VMEM((model, shared.shape[1] // 3), F32),
        ]
        + buffers * 2 + moves * 2 + (pair(cores) + [dma]) * 2
        + [pltpu.VMEM((max(cores - 1, 1), dps, lanes, shard, 3 * hidden), BF)] + pair(cores),
        cost_estimate=lasts(125),
        compiler_params=pltpu.CompilerParams(
            collective_id=3, has_side_effects=True, vmem_limit_bytes=VMEM_LIMIT
        ),
    )(x, upstream, tables, picks, rows, low, shared)


def expert_kernel(
    steps, dps, lanes, cores, hidden, x_ref, c_ref, w_ref, down_ref, own_ref,
    dx_ref, gu_ref, hid_ref, f_ref, line_ref, mine, from_dp, out, came, local,
):
    dp, fs, z, c = place(cores)
    step = pl.program_id(0)

    def over(m):
        t = lax.rem(dp + m, dps)
        return send(own_ref.at[t], from_dp.at[m - 1], out.at[m - 1], came.at[m - 1], (t, fs))

    keep = pltpu.make_async_copy(own_ref.at[dp], mine, local)

    @pl.when(step == 0)
    def _():
        greet([(lax.rem(dp + m, dps), fs) for m in range(1, dps)])
        for m in range(1, dps):
            over(m).start()
        keep.start()

    dx, dgate, dup, hid = feed(x_ref[...], c_ref[...], w_ref, down_ref, hidden)
    dx_ref[...] = dx.astype(dx_ref.dtype)
    gu_ref[:, :hidden] = dgate
    gu_ref[:, hidden:] = dup
    hid_ref[...] = hid
    f_ref[...] = dot_nt(hid, down_ref[...]).astype(BF)

    @pl.when(step == steps - 1)
    def _():
        keep.wait()
        for m in range(1, dps):
            over(m).wait_recv()
        for q in range(lanes):
            total = mine[q].astype(F32)
            for m in range(1, dps):
                total = total + from_dp[m - 1, q].astype(F32)
            line_ref[q] = total.astype(BF)
        for m in range(1, dps):
            over(m).wait_send()


def expert(x, c, w, down, own, cores):
    rows, model = x.shape
    hidden = down.shape[1]
    dps, lanes = own.shape[:2]
    block = min(512, rows)
    dma = pltpu.SemaphoreType.DMA
    row = lambda cols: pl.BlockSpec((block, cols), lambda i: (i, 0))
    return pl.pallas_call(
        functools.partial(expert_kernel, rows // block, dps, lanes, cores, hidden),
        grid=(rows // block,),
        in_specs=[
            row(model),
            row(model),
            pl.BlockSpec(w.shape, lambda i: (0, 0)),
            pl.BlockSpec(down.shape, lambda i: (0, 0)),
            ANY,
        ],
        out_specs=[
            row(model), row(2 * hidden), row(hidden), row(model), pl.BlockSpec(own.shape[1:], lambda i: (0, 0, 0)),
        ],
        out_shape=[
            jax.ShapeDtypeStruct((rows, model), BF),
            jax.ShapeDtypeStruct((rows, 2 * hidden), BF),
            jax.ShapeDtypeStruct((rows, hidden), BF),
            jax.ShapeDtypeStruct((rows, model), BF),
            jax.ShapeDtypeStruct(own.shape[1:], BF),
        ],
        scratch_shapes=[
            pltpu.VMEM(own.shape[1:], BF),
            pltpu.VMEM((dps - 1,) + own.shape[1:], BF),
        ]
        + pair(dps) + [dma],
        cost_estimate=lasts(40),
        compiler_params=pltpu.CompilerParams(
            collective_id=7, has_side_effects=True, vmem_limit_bytes=VMEM_LIMIT
        ),
    )(x, c, w, down, own)


class Combine:
    def __init__(self, parts, picks, result, scratch, dps, lanes, cores):
        self.parts, self.picks, self.result = parts, picks, result
        self.back, self.stage, self.inbox = scratch[:3]
        self.z_out, self.z_in, self.d_out, self.d_in, self.local = scratch[3:]
        self.dps, self.lanes, self.cores = dps, lanes, cores
        self.dp, self.fs, self.z, self.c = place(cores)

    def over(self, m, block):
        return send(
            self.parts.at[m, block], self.back.at[block, m], self.d_out.at[m - 1, block],
            self.d_in.at[m - 1, block], (lax.rem(self.dp + self.dps - m, self.dps), self.fs),
        )

    def keep(self, block):
        return pltpu.make_async_copy(
            self.parts.at[0, block], self.back.at[block, 0], self.local.at[block]
        )

    def hop(self, side, step):
        return send(
            self.stage.at[side, step - 1], self.inbox.at[side, step - 1], self.z_out.at[side, step - 1],
            self.z_in.at[side, step - 1],
            (self.dp, self.fs + (self.cores if side == 0 else -self.cores)),
        )

    def goal(self, side, step):
        block = self.z + self.lanes - step if side == 0 else self.z - self.lanes + step
        return block, (block >= 0) & (block < self.lanes)

    def fed(self, side):
        return self.z > 0 if side == 0 else self.z < self.lanes - 1

    def send_block(self, block):
        for m in range(1, self.dps):
            self.over(m, block).start()
        self.keep(block).start()

    def begin(self):
        for step in range(1, self.lanes):
            for side in (0, 1):
                block, there = self.goal(side, step)

                @pl.when(there)
                def _():
                    self.send_block(block)

        self.send_block(self.z)

    def partial_sum(self, block):
        self.keep(block).wait()
        total = dot_tn(self.picks[0, block], self.back[block, 0])
        for m in range(1, self.dps):
            self.over(m, block).wait_recv()
            total = total + dot_tn(self.picks[m, block], self.back[block, m])
        return total

    def advance(self, step):
        for side in (0, 1):
            block, there = self.goal(side, step)

            @pl.when(there)
            def _():
                total = self.partial_sum(block)
                self.stage[side, step - 1] = total.astype(BF)
                if step > 1:

                    @pl.when(self.fed(side))
                    def _():
                        self.hop(side, step - 1).wait_recv()
                        more = self.inbox[side, step - 2].astype(F32)
                        self.stage[side, step - 1] = (total + more).astype(BF)

                self.hop(side, step).start()

    def finish(self):
        self.result[...] = self.partial_sum(self.z)
        for side in (0, 1):

            @pl.when(self.fed(side))
            def _():
                self.hop(side, self.lanes - 1).wait_recv()
                self.result[...] += self.inbox[side, self.lanes - 2].astype(F32)

        for step in range(1, self.lanes):
            for side in (0, 1):
                block, there = self.goal(side, step)

                @pl.when(there)
                def _():
                    self.hop(side, step).wait_send()

        for block in range(self.lanes):
            for m in range(1, self.dps):
                self.over(m, block).wait_send()


def combine_scratch(dps, lanes, slots, tokens, model):
    dma = pltpu.SemaphoreType.DMA
    hops = (2, max(lanes - 1, 1))
    ways = (dps - 1, lanes)
    return [
        pltpu.VMEM((lanes, dps, slots, model), BF),
        pltpu.VMEM(hops + (tokens, model), BF),
        pltpu.VMEM(hops + (tokens, model), BF),
        dma(hops), dma(hops), dma(ways), dma(ways), dma((lanes,)),
    ]


class Gradient:
    def __init__(self, refs, total, scratch, experts, shard, cores):
        self.x, self.c_rows, self.gu, self.hid = refs
        self.total = total
        self.left, self.right, self.acc, self.stage, self.inbox, self.load, self.out, self.came = scratch
        self.experts, self.shard, self.cores = experts, shard, cores
        self.hidden = self.hid.shape[1]
        self.dp, self.fs, self.z, self.c = place(cores)

    def rows_in(self, third):
        source = self.x if third < 2 else self.c_rows
        return pltpu.make_async_copy(source, self.left, self.load.at[0])

    def columns_in(self, third):
        source = self.hid if third == 2 else self.gu.at[:, third * self.hidden : (third + 1) * self.hidden]
        return pltpu.make_async_copy(source, self.right, self.load.at[1])

    def across(self, third, m):
        t = lax.rem(self.c + m, self.cores)
        return send(
            self.stage.at[third, t], self.inbox.at[third, m - 1], self.out.at[third, m - 1],
            self.came.at[third, m - 1], (self.dp, self.z * self.cores + t),
        )

    def begin(self):
        self.rows_in(0).start()
        self.columns_in(0).start()

    def multiply(self, third):
        if third != 1:
            self.rows_in(third).wait()
        self.columns_in(third).wait()
        self.acc[...] = dot_tn(self.left[...], self.right[...])
        if third < 2:
            self.columns_in(third + 1).start()
        if third == 1:
            self.rows_in(2).start()
        for e in range(self.experts):
            for k in range(self.cores):
                row = (e * self.cores + k) * self.shard
                self.stage[third, k, e] = self.acc[row : row + self.shard, :].astype(BF)
        for m in range(1, self.cores):
            self.across(third, m).start()

    def collect(self, third):
        for m in range(1, self.cores):
            self.across(third, m).wait_recv()
        for e in range(self.experts):
            total = self.stage[third, self.c, e].astype(F32)
            for m in range(1, self.cores):
                total = total + self.inbox[third, m - 1, e].astype(F32)
            self.total[e, :, third * self.hidden : (third + 1) * self.hidden] = total.astype(BF)

    def finish(self):
        for third in range(3):
            for m in range(1, self.cores):
                self.across(third, m).wait_send()


def combine_kernel(
    dps, lanes, cores, part_ref, pick_ref, xs_ref, cs_ref, gu_ref, hid_ref, line_ref,
    out_ref, g_ref, sum_ref, from_z, s_out, s_in, *scratch,
):
    work = Combine(part_ref, pick_ref, out_ref, scratch[:8], dps, lanes, cores)
    gradient = Gradient(
        (xs_ref, cs_ref, gu_ref, hid_ref), g_ref, scratch[8:], g_ref.shape[0], g_ref.shape[1], cores
    )
    dp, fs, z, c = place(cores)

    def along(k):
        t = lax.rem(z + k, lanes)
        return send(
            line_ref.at[t], from_z.at[k - 1], s_out.at[k - 1], s_in.at[k - 1], (dp, t * cores + c)
        )

    gradient.begin()
    greet(
        [(lax.rem(dp + m, dps), fs) for m in range(1, dps)]
        + [(dp, lax.rem(z + k, lanes) * cores + c) for k in range(1, lanes)]
        + [(dp, z * cores + lax.rem(c + m, cores)) for m in range(1, cores)]
    )
    work.begin()
    for k in range(1, lanes):
        along(k).start()
    gradient.multiply(0)
    for step in range(1, lanes):
        work.advance(step)
        if step == 1:
            gradient.multiply(1)
    if lanes == 1:
        gradient.multiply(1)
    gradient.multiply(2)
    total = line_ref[z].astype(F32)
    for k in range(1, lanes):
        along(k).wait_recv()
        total = total + from_z[k - 1].astype(F32)
    sum_ref[...] = total
    work.finish()
    for third in range(3):
        gradient.collect(third)
    gradient.finish()
    for k in range(1, lanes):
        along(k).wait_send()


def combine(parts, picks, slots_in, grads, line, lanes, cores):
    dps, _, slots, model = parts.shape
    tokens = picks.shape[3]
    xs, cs = slots_in
    gu, hid = grads
    experts, shard = dps * lanes, line.shape[1]
    hidden = hid.shape[1]
    dma = pltpu.SemaphoreType.DMA
    others = max(cores - 1, 1)
    whole = pl.BlockSpec(memory_space=pltpu.VMEM)
    return pl.pallas_call(
        functools.partial(combine_kernel, dps, lanes, cores),
        in_specs=[ANY, whole] + [ANY] * 4 + [whole],
        out_specs=[whole] * 3,
        out_shape=[
            jax.ShapeDtypeStruct((tokens, model), F32),
            jax.ShapeDtypeStruct((experts, shard, 3 * hidden), BF),
            jax.ShapeDtypeStruct(line.shape[1:], F32),
        ],
        scratch_shapes=[pltpu.VMEM((max(lanes - 1, 1),) + line.shape[1:], BF)]
        + pair(lanes)
        + combine_scratch(dps, lanes, slots, tokens, model)
        + [
            pltpu.VMEM(xs.shape, BF),
            pltpu.VMEM(hid.shape, BF),
            pltpu.VMEM((model, hidden), F32),
            pltpu.VMEM((3, cores, experts, shard, hidden), BF),
            pltpu.VMEM((3, others, experts, shard, hidden), BF),
            dma((2,)), dma((3, others)), dma((3, others)),
        ],
        cost_estimate=lasts(70),
        compiler_params=pltpu.CompilerParams(
            collective_id=4, has_side_effects=True, vmem_limit_bytes=VMEM_LIMIT
        ),
    )(parts, picks, xs, cs, gu, hid, line)


def turn_kernel(
    dps, lanes, cores, x_ref, part_ref, pick_ref, middle_ref, shared_ref, full_ref, out_ref, routed, *scratch
):
    work = Combine(part_ref, pick_ref, routed, scratch[:8], dps, lanes, cores)
    chain = Chain(x_ref, full_ref, lanes, cores, scratch[8:])
    dp, fs = chain.dp, chain.fs
    greet(sequence_peers(dp, fs, lanes * cores) + [(lax.rem(dp + m, dps), fs) for m in range(1, dps)])
    chain.begin()
    work.begin()
    for step in range(1, lanes):
        chain.advance(step)
        work.advance(step)
    chain.finish()
    work.finish()
    out_ref[...] = (middle_ref[...] + shared_ref[...] + routed[...]).astype(BF)


def turn(x, parts, picks, middle, shared, lanes, cores):
    dps, _, slots, model = parts.shape
    tokens = picks.shape[3]
    whole = pl.BlockSpec(memory_space=pltpu.VMEM)
    return pl.pallas_call(
        functools.partial(turn_kernel, dps, lanes, cores),
        in_specs=[ANY, ANY, whole, whole, whole],
        out_specs=[ANY, whole],
        out_shape=[
            jax.ShapeDtypeStruct((lanes, cores) + x.shape, x.dtype),
            jax.ShapeDtypeStruct((tokens, model), BF),
        ],
        scratch_shapes=[pltpu.VMEM((tokens, model), F32)]
        + combine_scratch(dps, lanes, slots, tokens, model) + chain_sems(lanes, cores),
        cost_estimate=lasts(90),
        compiler_params=pltpu.CompilerParams(
            collective_id=1, has_side_effects=True, vmem_limit_bytes=VMEM_LIMIT
        ),
    )(x, parts, picks, middle, shared)


def attend_back_kernel(
    dps, lanes, cores, busy, block, scale,
    da_ref, xn_ref, out_ref, q_ref, k_ref, kt_ref, v_ref, o_ref, lse_ref, cos_ref, sin_ref, w_ref,
    part_ref, prod_ref, left, d_ref, acc, stage, cols, do_all, dk_acc, dv_acc,
    load, stored,
):
    dp, fs, z, c = place(cores)
    seq, width = q_ref.shape
    tokens = part_ref.shape[2]
    slot = jnp.minimum(head_slot(fs, lanes, cores), busy - 1)
    fetch = pltpu.make_async_copy(
        out_ref.at[:, pl.ds(pl.multiple_of(slot * width, HD), width)], cols, load.at[0]
    )
    fetch.start()
    first, second = [pltpu.make_async_copy(ref, left, load.at[1]) for ref in (da_ref, xn_ref)]
    first.start()
    shard = prod_ref.shape[2]

    def place_rows(lo, hi):
        for p in range(dps):
            for f in range(lanes * cores):
                row = (p * lanes * cores + f) * shard
                prod_ref[p, f, :, lo:hi] = acc[row : row + shard, : hi - lo].astype(BF)

    fetch.wait()
    first.wait()

    def upstream(i, carry):
        rows = pl.ds(pl.multiple_of(i * block, block), block)
        do_all[rows, :] = dot_nn(left[rows, :], cols[...]).astype(BF)
        return carry

    mine = head_slot(fs, lanes, cores) < busy

    @pl.when(mine)
    def _():
        lax.fori_loop(0, seq // block, upstream, 0)

    @pl.when(mine)
    def _():
        acc[:, :width] = dot_tn(left[...], o_ref[...])
        place_rows(3 * width, 4 * width)

    second.start()

    def head_rows(h, carry):
        lane = pl.ds(pl.multiple_of(h * HD, HD), HD)
        k_lane = pl.ds(pl.multiple_of(width + h * HD, HD), HD)
        v_lane = pl.ds(pl.multiple_of(2 * width + h * HD, HD), HD)
        dk_acc[...] = jnp.zeros_like(dk_acc)
        dv_acc[...] = jnp.zeros_like(dv_acc)
        for j in range(seq // block):
            here = slice(j * block, (j + 1) * block)
            q = q_ref[here, lane]
            do = do_all[here, lane]
            row = jnp.sum((do.astype(F32) * o_ref[here, lane].astype(F32)).T, axis=0, keepdims=True)
            lse = lse_ref[h, :, here]
            dq = None
            for span, edge in ([(slice(0, j * block), False)] if j else []) + [(here, True)]:
                p = jnp.exp(dot_nt(k_ref[span, lane], q) * scale - lse)
                if edge:
                    p = jnp.where(causal(block), p, 0.0)
                ds = (p * (dot_nt(v_ref[span, lane], do) - row)).astype(BF)
                dv_acc[span, :] += dot_nn(p.astype(BF), do)
                dk_acc[span, :] += dot_nn(ds, q)
                term = dot_nn(kt_ref[lane, span], ds)
                dq = term if dq is None else dq + term
            d_ref[here, lane] = unrotate(dq.T * scale, cos_ref[here, :], sin_ref[here, :]).astype(BF)
        d_ref[:, k_lane] = unrotate(dk_acc[...] * scale, cos_ref[...], sin_ref[...]).astype(BF)
        d_ref[:, v_lane] = dv_acc[...].astype(BF)
        return carry

    @pl.when(mine)
    def _():
        lax.fori_loop(0, width // HD, head_rows, 0)

    blocks = [(a, b) for a in range(lanes) for b in range(cores)]
    saves = [
        pltpu.make_async_copy(stage.at[n % 2], part_ref.at[a, b], stored.at[n % 2])
        for n, (a, b) in enumerate(blocks)
    ]
    for n in range(len(blocks)):
        if n >= 2:
            saves[n - 2].wait()

        @pl.when(mine)
        def _():
            stage[n % 2] = dot_nt(d_ref[n * tokens : (n + 1) * tokens, :], w_ref[...]).astype(BF)

        @pl.when(jnp.logical_not(mine))
        def _():
            stage[n % 2] = jnp.zeros(stage.shape[1:], BF)

        saves[n].start()
    second.wait()

    @pl.when(mine)
    def _():
        acc[...] = dot_tn(left[...], d_ref[...])
        place_rows(0, 3 * width)

    for save in saves[-2:]:
        save.wait()


def attend_back(da_all, xn, out_all, saved, tables, w, shard, tokens, busy, dps, lanes, cores):
    q, k, kt, v, o, lse = saved
    cos, sin = tables
    seq, width = q.shape
    model = w.shape[0]
    block = 256
    dma = pltpu.SemaphoreType.DMA
    whole = pl.BlockSpec(memory_space=pltpu.VMEM)
    return pl.pallas_call(
        functools.partial(attend_back_kernel, dps, lanes, cores, busy, block, 1.0 / math.sqrt(HD)),
        in_specs=[ANY] * 3 + [whole] * 9,
        out_specs=[ANY, whole],
        out_shape=[
            jax.ShapeDtypeStruct((lanes, cores, tokens, model), BF),
            jax.ShapeDtypeStruct((dps, lanes * cores, shard, 4 * width), BF),
        ],
        scratch_shapes=[
            pltpu.VMEM((seq, model), BF),
            pltpu.VMEM((seq, 3 * width), BF),
            pltpu.VMEM((model, 3 * width), F32),
            pltpu.VMEM((2, tokens, model), BF),
            pltpu.VMEM((model, width), BF),
            pltpu.VMEM((seq, width), BF),
            pltpu.VMEM((seq, HD), F32),
            pltpu.VMEM((seq, HD), F32),
            dma((2,)),
            dma((2,)),
        ],
        cost_estimate=lasts(50),
        compiler_params=pltpu.CompilerParams(vmem_limit_bytes=VMEM_LIMIT),
    )(da_all, xn, out_all, q, k, kt, v, o, lse, cos, sin, w)


def finish_kernel(
    dps, lanes, cores, busy, part_ref, g_ref, x_ref, gain_ref, dx_ref, wq_ref,
    out_ref, gq_ref, go_ref, one_ref, mix_ref,
    from_core, stage, inbox, from_dp, total_g,
    z_out, z_in, c_out, c_in, g_out, g_in, m_out, m_in, local,
):
    dp, fs, z, c = place(cores)
    fss = lanes * cores
    greet(sequence_peers(dp, fs, fss) + [(lax.rem(dp + m, dps), fs) for m in range(1, dps)])

    def has_next(side):
        return z < lanes - 1 if side == 0 else z > 0

    def over(m):
        t = lax.rem(dp + m, dps)
        return send(g_ref.at[t], from_dp.at[m - 1], g_out.at[m - 1], g_in.at[m - 1], (t, fs))

    def across(m, block):
        t = lax.rem(c + m, cores)
        return send(
            part_ref.at[block, t], from_core.at[m - 1, block], c_out.at[m - 1, block], c_in.at[m - 1, block],
            (dp, z * cores + t),
        )

    def hop(side, step):
        return send(
            stage.at[side, step - 1], inbox.at[side, step - 1], z_out.at[side, step - 1],
            z_in.at[side, step - 1], (dp, fs + (cores if side == 0 else -cores)),
        )

    def home(k, owner):
        t = lax.rem(fs + k, fss)
        return send(total_g.at[t], mix_ref.at[head_slot(owner, lanes, cores)], m_out.at[k - 1], m_in.at[k - 1], (dp, t))

    def goal(side, step):
        block = z + lanes - step if side == 0 else z - lanes + step
        return block, (block >= 0) & (block < lanes)

    def begin(block):
        for m in range(1, cores):
            across(m, block).start()

    def partial_sum(block):
        total = part_ref[block, c].astype(F32)
        for m in range(1, cores):
            across(m, block).wait_recv()
            total = total + from_core[m - 1, block].astype(F32)
        return total

    def advance(step):
        for side in (0, 1):
            block, there = goal(side, step)
            fed = z > 0 if side == 0 else z < lanes - 1

            @pl.when(there)
            def _():
                total = partial_sum(block)
                stage[side, step - 1] = total.astype(BF)
                if step > 1:

                    @pl.when(fed)
                    def _():
                        hop(side, step - 1).wait_recv()
                        stage[side, step - 1] = (total + inbox[side, step - 2].astype(F32)).astype(BF)

                hop(side, step).start()

    for step in range(1, lanes):
        for side in (0, 1):
            block, there = goal(side, step)

            @pl.when(there)
            def _():
                begin(block)

    begin(z)
    for m in range(1, dps):
        over(m).start()
    for step in range(1, max(lanes - 1, 1)):
        advance(step)
    for m in range(1, dps):
        over(m).wait_recv()
    for f in range(fss):
        total = g_ref[dp, f].astype(F32)
        for m in range(1, dps):
            total = total + from_dp[m - 1, f].astype(F32)
        total_g[f] = total.astype(BF)
    keep = pltpu.make_async_copy(total_g.at[fs], mix_ref.at[head_slot(fs, lanes, cores)], local)

    @pl.when(head_slot(fs, lanes, cores) < busy)
    def _():
        for k in range(1, fss):
            home(k, fs).start()
        keep.start()

    if lanes > 1:
        advance(lanes - 1)
    out_ref[...] = partial_sum(z)
    for side in (0, 1):
        fed = z > 0 if side == 0 else z < lanes - 1

        @pl.when(fed)
        def _():
            hop(side, lanes - 1).wait_recv()
            out_ref[...] += inbox[side, lanes - 2].astype(F32)

    for k in range(1, fss):
        owner = lax.rem(fs + fss - k, fss)

        @pl.when(head_slot(owner, lanes, cores) < busy)
        def _():
            home(k, owner).wait_recv()

    @pl.when(head_slot(fs, lanes, cores) < busy)
    def _():
        keep.wait()
        for k in range(1, fss):
            home(k, fs).wait_send()

    model = out_ref.shape[1]
    width = mix_ref.shape[2] // 4
    one = None
    for slot in range(busy):
        lo = slot * width
        wide = min(width, model - lo)
        for p in range(3):
            piece = mix_ref[slot, :, p * width : p * width + wide].astype(F32)
            gq_ref[:, p * model + lo : p * model + lo + wide] = piece
            weight = wq_ref[:, p * model + lo : p * model + lo + wide].astype(F32)
            term = jnp.sum(weight * piece, axis=1, keepdims=True)
            one = term if one is None else one + term
        go_ref[:, lo : lo + wide] = mix_ref[slot, :, 3 * width : 3 * width + wide].astype(F32)
    one_ref[...] = one
    x = x_ref[...].astype(F32)
    inv = lax.rsqrt(jnp.mean(x * x, axis=1, keepdims=True) + norm_eps)
    unit = x * inv
    scaled = out_ref[...] * gain_ref[...]
    out_ref[...] = dx_ref[...] + inv * (scaled - unit * jnp.mean(scaled * unit, axis=1, keepdims=True))
    for step in range(1, lanes):
        for side in (0, 1):
            block, there = goal(side, step)

            @pl.when(there)
            def _():
                hop(side, step).wait_send()

    for m in range(1, cores):
        for block in range(lanes):
            across(m, block).wait_send()
    for m in range(1, dps):
        over(m).wait_send()


def finish(part, g, x, gain, dx, w_qkv, lanes, cores, busy):
    dps, fss = g.shape[:2]
    tokens, model = part.shape[2:]
    dma = pltpu.SemaphoreType.DMA
    hops = (2, max(lanes - 1, 1))
    ways = (max(cores - 1, 1), lanes)
    whole = pl.BlockSpec(memory_space=pltpu.VMEM)
    return pl.pallas_call(
        functools.partial(finish_kernel, dps, lanes, cores, busy),
        in_specs=[whole] * 6,
        out_specs=[whole] * 4,
        out_shape=[
            jax.ShapeDtypeStruct((tokens, model), F32),
            jax.ShapeDtypeStruct(w_qkv.shape, F32),
            jax.ShapeDtypeStruct((w_qkv.shape[0], model), F32),
            jax.ShapeDtypeStruct((w_qkv.shape[0], 1), F32),
        ],
        scratch_shapes=[
            pltpu.VMEM((busy,) + g.shape[2:], BF),
            pltpu.VMEM(ways + (tokens, model), BF),
            pltpu.VMEM(hops + (tokens, model), BF),
            pltpu.VMEM(hops + (tokens, model), BF),
            pltpu.VMEM((dps - 1,) + g.shape[1:], BF),
            pltpu.VMEM(g.shape[1:], BF),
            dma(hops), dma(hops), dma(ways), dma(ways), dma((dps - 1,)), dma((dps - 1,)),
            dma((fss - 1,)), dma((fss - 1,)), dma,
        ],
        cost_estimate=lasts(66),
        compiler_params=pltpu.CompilerParams(
            collective_id=6, has_side_effects=True, vmem_limit_bytes=VMEM_LIMIT
        ),
    )(part, g, x, gain, dx, w_qkv)


def per_device(x, w_qkv, w_out, w_shared, w_experts, gains, routes, gates, d_out):
    tokens, model = x.shape
    hidden = w_shared.shape[1] // 3
    experts, shard = w_experts.shape[:2]
    dps, fss = lax.axis_size("dp"), lax.axis_size("fsdp")
    cores = dps * fss // experts
    lanes = fss // cores
    seq = tokens * fss
    slots = tokens // 2
    per = -(-HEADS // fss)
    busy = -(-HEADS // per)
    width = per * HD
    dp, fs = lax.axis_index("dp"), lax.axis_index("fsdp")
    z, c = fs // cores, fs % cores

    def over_z(value, pairs):
        return lax.ppermute(
            value, "fsdp", [(a * cores + k, b * cores + k) for a, b in pairs for k in range(cores)]
        )

    cut = w_qkv.reshape(shard, 3, HEADS, HD)
    cut = jnp.pad(cut, ((0, 0), (0, 0), (0, fss * per - HEADS), (0, 0)))
    cut = cut.reshape(shard, 3, cores, lanes, width).transpose(3, 2, 0, 1, 4).reshape(fss, shard, 3 * width)
    wide_gains = jnp.pad(gains, ((0, 0), (0, HD - 2)))
    topk = routes.shape[1]
    table = jnp.concatenate([routes.T.astype(F32), gates.T], axis=0)
    table = jnp.pad(table, ((0, -2 * topk % 8), (0, 0)))
    x_all, slabs, tables, out_all, gains_all, picks, weigh = start(
        x, cut, table, w_out, wide_gains, topk, busy, dps, lanes, cores
    )
    x_all = x_all.reshape(seq, model)
    slabs = slabs.reshape(model, 3 * width)
    out_all = out_all.reshape(model, model)
    gain_rows = gains_all.reshape(model, HD)[:, :2].astype(F32).T
    w_heads = slabs
    gain_one, gain_two = gain_rows[0:1], gain_rows[1:2]

    half = HD // 2
    frequency = np.float32(10000.0) ** (-np.arange(half, dtype=np.float32) / np.float32(half))
    angles = np.arange(seq, dtype=np.float32)[:, None] * frequency[None, :]
    cosine, sine = np.cos(angles), np.sin(angles)
    cos = jnp.asarray(np.concatenate([cosine, cosine], axis=1), F32)
    sin = jnp.asarray(np.concatenate([-sine, sine], axis=1), F32)

    xn_one, q, k, v, kt, vt, o, lse, heads, shared_all, rows_here, rows_low = attend(
        x_all, gain_one, w_heads, cos, sin, w_experts, w_shared, tokens, busy, dps, lanes, cores
    )
    heads = heads[:, :model]
    shared_all = shared_all.reshape(model, 3 * hidden)

    middle = x.astype(F32) + dot_nt(heads, out_all)
    inv_two = lax.rsqrt(jnp.mean(middle * middle, axis=1, keepdims=True) + norm_eps)
    unit_two = middle * inv_two
    xn_two = (unit_two * gain_two).astype(BF)

    x_slots, c_slots, w_own, w_down, dx_shared, f_shared, g_core = dispatch(
        xn_two, d_out, tables, picks, rows_here, rows_low, shared_all, topk, lanes, cores
    )
    x_slots = x_slots.reshape(-1, model)
    c_slots = c_slots.reshape(-1, model)
    w_own = w_own.reshape(model, 2 * hidden)
    w_down = w_down.reshape(model, hidden)
    dx_slots, gu_slots, hid_slots, f_slots, g_line = expert(x_slots, c_slots, w_own, w_down, g_core, cores)

    shape = (dps, lanes, slots, model)
    dx_routed, g_own, g_shared = combine(
        dx_slots.reshape(shape), picks, (x_slots, c_slots), (gu_slots, hid_slots), g_line, lanes, cores
    )
    dxn_two = dx_shared + dx_routed
    scaled = dxn_two * gain_two
    dx_two = d_out.astype(F32) + inv_two * (
        scaled - unit_two * jnp.mean(scaled * unit_two, axis=1, keepdims=True)
    )
    d_attn = dx_two.astype(BF)

    da_all, layer_out = turn(d_attn, f_slots.reshape(shape), weigh, middle, f_shared, lanes, cores)
    da_all, g_own = lax.optimization_barrier((da_all, g_own))
    da_all = da_all.reshape(seq, model)
    dxn_part, g_part = attend_back(
        da_all, xn_one, out_all, (q, k, kt, v, o, lse), (cos, sin), w_heads, shard,
        tokens, busy, dps, lanes, cores,
    )
    d_x, g_qkv, g_out, one = finish(
        dxn_part, g_part, x, gain_one, dx_two, w_qkv, lanes, cores, busy
    )

    groups = [[e * cores + k for e in range(experts)] for k in range(cores)]
    g_experts = lax.all_to_all(
        g_own, ("dp", "fsdp"), split_axis=0, concat_axis=0, tiled=True, axis_index_groups=groups
    ).astype(F32)

    two = jnp.sum(w_shared[:, : 2 * hidden].astype(F32) * g_shared[:, : 2 * hidden], axis=1)
    two = two + jnp.sum(
        w_experts[:, :, : 2 * hidden].astype(F32) * g_experts[:, :, : 2 * hidden], axis=(0, 2)
    )
    g_gains = jnp.concatenate([one, two[:, None]], axis=1) / gains.astype(F32)
    return (layer_out, d_x, g_qkv, g_out, g_shared, g_experts, g_gains)


def solution(mesh):
    rows = P(("dp", "fsdp"), None)
    cube = P(None, ("dp", "fsdp"), None)
    return jax.shard_map(
        per_device,
        mesh=mesh,
        in_specs=(rows, rows, rows, rows, cube, rows, rows, rows, rows),
        out_specs=(rows, rows, rows, rows, rows, cube, rows),
        check_vma=False,
    )
```
